32 devices in a mesh: nodes: 8 (over y, x, core), queries: 4 (over z).
Axes of the slice: x: 2, y: 2, z: 4, core: 2. Of those that a mesh axis runs over, the one named last changes fastest.
Arguments:
- state_in: float32 [2048, 512], P('nodes', 'queries')
- edge_src: int32 [32768], P('nodes'), may hold values from 0 to 767
- edge_dst: int32 [32768], P('nodes'), may hold values from 0 to 255
- edge_rel: int32 [32768], P('nodes'), may hold values from 0 to 534
- edge_count: int32 [8], P('nodes'), may hold values from 1024 to 4096, as said below
- send_list: int32 [8, 8, 64], P('nodes'), may hold values from 0 to 255
- query_head: int32 [16], P('queries'), may hold values from 0 to 2047
- query_rel: int32 [16], P('queries'), may hold values from 0 to 534
- pos_tail: int32 [16], P('queries'), may hold values from 0 to 2047
- neg_ids: int32 [16, 1024], P('queries', 'nodes'), may hold values from 0 to 255
- rel_table: float32 [535, 32], replicated, may hold values from -1.8 to 1.8
- layer_weight: float32 [32, 32], replicated, may hold values from -1 to 1
- mlp_entity: float32 [32, 64], replicated, may hold values from -1 to 1
- mlp_query: float32 [32, 64], replicated, may hold values from -1 to 1
- score_weight: float32 [64], replicated, may hold values from -0.75 to 0.75
Outputs:
- new_state: float32 [2048, 512], P('nodes', 'queries')
- loss: float32 [16], P('queries')
- grad_rel: float32 [535, 32], replicated
- grad_layer: float32 [32, 32], replicated
- grad_entity: float32 [32, 64], replicated
- grad_query: float32 [32, 64], replicated
- grad_score: float32 [64], replicated
The draws below stay inside these ranges and needn't reach their ends.
Inputs may be any that keep to these rules, and one draw needn't show every extreme that they name: `edge_count`: some partition holds exactly 4096 live edges.
All inputs are finite; a program needn't handle non-finite values.
Results may differ from the reference program's by a relative error of at most 0.0003.
Values sent between devices are 32-bit elements; how exact they have to be, the bound alone decides.
No kernel may reach another device: no remote copies, remote signals or barrier semaphores. Data moves between devices by JAX's collectives and lax.ppermute only.
A program may use at most 64 MiB of HBM per device.

```python
import math
import jax
import jax.numpy as jnp
import numpy as np
from jax import lax

D = 32
NREL = 535
HID = 64
ENT_DEV = 256
NEG_DEV = 128
BND = 64
ENTITIES = 2048
QUERIES = 16
NEG = 1024
EDGE_DEV = 4096
HALO = 512
N_NODES = 8


def draw_state_in(key, part):
    first_key, second_key = jax.random.split(key, 2)
    ramp = 0.5 + jnp.arange(ENTITIES, dtype=jnp.float32) / ENTITIES
    rough = jnp.exp(jax.random.uniform(second_key, (ENTITIES, 1), jnp.float32, 0.0, math.log(3.0)))
    values = jax.random.normal(first_key, (ENTITIES, QUERIES * D), jnp.float32)
    return (ramp[:, None] * rough * values).astype(jnp.float32)


def draw_edge_count(key, part):
    counts = jax.random.randint(key, (N_NODES,), EDGE_DEV // 4, EDGE_DEV + 1, jnp.int32)
    fullest = jax.random.randint(jax.random.fold_in(key, 7), (), 0, N_NODES, jnp.int32)
    return counts.at[fullest].set(EDGE_DEV)


def set_ends(drawn, rng, least, high):
    spot = [jax.random.randint(jax.random.fold_in(rng, axis), (), 0, length) for axis, length in enumerate(drawn.shape)]
    longest = drawn.shape.index(max(drawn.shape))
    beside = spot[:longest] + [(spot[longest] + 1) % drawn.shape[longest]] + spot[longest + 1:]
    return drawn.at[tuple(spot)].set(least).at[tuple(beside)].set(high)


def rank_bounds(amount, slope):
    weights = [(1 << 20) // math.isqrt(standing ** slope) + 1 for standing in range(1, amount + 1)]
    scale = 1 + sum(weights) // (1 << 30)
    return np.cumsum(np.array([max(1, weight // scale) for weight in weights]))


def ranked_ids(key, extent, count, slope):
    table = rank_bounds(count, slope)
    ticket = jax.random.randint(jax.random.fold_in(key, 1), extent, 0, int(table[count - 1]))
    standing = jnp.searchsorted(jnp.asarray(table, jnp.int32), ticket, side="right")
    return jax.random.permutation(jax.random.fold_in(key, 2), count)[standing].astype(jnp.int32)


def gaussian(key, extent, scale, limit, kind=jnp.bfloat16):
    values = jax.random.normal(key, extent, jnp.float32) * scale
    return jnp.minimum(jnp.maximum(values, -limit), limit).astype(kind)


def setup_inputs(seed: int = 0) -> dict:
    seeds = jax.random.split(jax.random.key(seed), 16)
    return {
        "state_in": draw_state_in(jax.random.fold_in(seeds[15], 71), 0),
        "edge_src": set_ends(jax.random.randint(seeds[1], (N_NODES * EDGE_DEV,), 0, ENT_DEV + HALO), jax.random.fold_in(seeds[1], 1), 0, (ENT_DEV + HALO) - 1).astype(jnp.int32),
        "edge_dst": set_ends(jax.random.randint(seeds[2], (N_NODES * EDGE_DEV,), 0, ENT_DEV), jax.random.fold_in(seeds[2], 1), 0, ENT_DEV - 1).astype(jnp.int32),
        "edge_rel": set_ends(ranked_ids(seeds[3], (N_NODES * EDGE_DEV,), NREL, 2), jax.random.fold_in(seeds[3], 3), 0, NREL - 1).astype(jnp.int32),
        "edge_count": draw_edge_count(jax.random.fold_in(seeds[15], 71), 0),
        "send_list": set_ends(jax.random.randint(seeds[5], (N_NODES, N_NODES, BND), 0, ENT_DEV), jax.random.fold_in(seeds[5], 1), 0, ENT_DEV - 1).astype(jnp.int32),
        "query_head": set_ends(jax.random.randint(seeds[6], (QUERIES,), 0, ENTITIES), jax.random.fold_in(seeds[6], 1), 0, ENTITIES - 1).astype(jnp.int32),
        "query_rel": set_ends(jax.random.randint(seeds[7], (QUERIES,), 0, NREL), jax.random.fold_in(seeds[7], 1), 0, NREL - 1).astype(jnp.int32),
        "pos_tail": set_ends(jax.random.randint(seeds[8], (QUERIES,), 0, ENTITIES), jax.random.fold_in(seeds[8], 1), 0, ENTITIES - 1).astype(jnp.int32),
        "neg_ids": set_ends(jax.random.randint(seeds[9], (QUERIES, NEG), 0, ENT_DEV), jax.random.fold_in(seeds[9], 1), 0, ENT_DEV - 1).astype(jnp.int32),
        "rel_table": gaussian(seeds[10], (NREL, D), 0.3, 1.8, jnp.float32),
        "layer_weight": gaussian(seeds[11], (D, D), D ** -0.5, 1.0, jnp.float32),
        "mlp_entity": gaussian(seeds[12], (D, HID), D ** -0.5, 1.0, jnp.float32),
        "mlp_query": gaussian(seeds[13], (D, HID), D ** -0.5, 1.0, jnp.float32),
        "score_weight": gaussian(seeds[14], (HID,), HID ** -0.5, 0.75, jnp.float32),
    }


adversarial = 0.5


def edge_block(part_index, edge_src, edge_dst, edge_rel, edge_count, send_list):
    start = part_index * EDGE_DEV
    src_slot = lax.dynamic_slice_in_dim(edge_src, start, EDGE_DEV)
    dst_slot = lax.dynamic_slice_in_dim(edge_dst, start, EDGE_DEV)
    rel_slot = lax.dynamic_slice_in_dim(edge_rel, start, EDGE_DEV)
    remote = jnp.maximum(src_slot - ENT_DEV, 0).astype(jnp.int32)
    provider = (remote // BND).astype(jnp.int32)
    position = (remote % BND).astype(jnp.int32)
    far_entity = send_list[provider, part_index, position]
    source = jnp.where(src_slot < ENT_DEV, part_index * ENT_DEV + src_slot, provider * ENT_DEV + far_entity).astype(jnp.int32)
    live_mask = (jnp.arange(EDGE_DEV) < edge_count[part_index]).astype(jnp.float32)
    return source, dst_slot, rel_slot, live_mask


def reference(state_in, edge_src, edge_dst, edge_rel, edge_count, send_list, query_head, query_rel, pos_tail, neg_ids, rel_table, layer_weight, mlp_entity, mlp_query, score_weight):
    high = lax.Precision.HIGHEST
    state_cube = state_in.reshape(ENTITIES, QUERIES, D)
    parts = jnp.arange(N_NODES, dtype=jnp.int32)

    def forward_part(part_index):
        source, dst_slot, rel_slot, live_mask = edge_block(part_index, edge_src, edge_dst, edge_rel, edge_count, send_list)
        rel_rows = rel_table[rel_slot] * live_mask[:, None]
        message = state_cube[source] * rel_rows[:, None, :]
        return jax.ops.segment_sum(message, dst_slot, num_segments=ENT_DEV)

    summed = lax.map(forward_part, parts).reshape(ENTITIES, QUERIES, D)
    query_vec = rel_table[query_rel]
    head_mask = (jnp.arange(ENTITIES)[:, None] == query_head[None, :]).astype(jnp.float32)
    summed = summed + head_mask[:, :, None] * query_vec[None, :, :]
    pre_act = jnp.einsum('eqd,df->eqf', summed, layer_weight, precision=high)
    new_cube = state_cube + jax.nn.relu(pre_act)

    query_ids = jnp.arange(QUERIES)[:, None]
    negative_entity = ((jnp.arange(NEG) // NEG_DEV) * ENT_DEV)[None, :].astype(jnp.int32) + neg_ids
    pick_rows = jnp.concatenate([negative_entity, pos_tail[:, None]], axis=1)
    picked = new_cube[pick_rows, query_ids]
    hidden_pre = jnp.einsum('qrd,dh->qrh', picked, mlp_entity, precision=high) + jnp.dot(query_vec, mlp_query, precision=high)[:, None, :]
    hidden_act = jax.nn.relu(hidden_pre)
    scores = jnp.einsum('qrh,h->qr', hidden_act, score_weight, precision=high)
    neg_scores = scores[:, :-1]
    pos_score = scores[:, -1]
    weights_exp = jnp.exp(adversarial * neg_scores)
    total = jnp.sum(weights_exp, axis=1)
    loss = jax.nn.softplus(-pos_score) + jnp.sum(weights_exp * jax.nn.softplus(neg_scores), axis=1) / total
    neg_coeff = weights_exp / total[:, None] * jax.nn.sigmoid(neg_scores) / QUERIES
    pos_coeff = (jax.nn.sigmoid(pos_score) - 1.0) / QUERIES
    coeffs = jnp.concatenate([neg_coeff, pos_coeff[:, None]], axis=1)

    grad_hidden = coeffs[:, :, None] * score_weight[None, None, :] * (hidden_pre > 0).astype(jnp.float32)
    grad_score = jnp.einsum('qr,qrh->h', coeffs, hidden_act, precision=high)
    grad_entity = jnp.einsum('qrd,qrh->dh', picked, grad_hidden, precision=high)
    hidden_total = jnp.sum(grad_hidden, axis=1)
    grad_query = jnp.dot(query_vec.T, hidden_total, precision=high)
    grad_picked = jnp.einsum('qrh,dh->qrd', grad_hidden, mlp_entity, precision=high)
    grad_qvec = jnp.dot(hidden_total, mlp_query.T, precision=high)
    grad_cube = jnp.zeros((ENTITIES, QUERIES, D), jnp.float32).at[pick_rows, query_ids].add(grad_picked)
    grad_pre = grad_cube * (pre_act > 0).astype(jnp.float32)
    grad_layer = jnp.einsum('eqd,eqf->df', summed, grad_pre, precision=high)
    grad_sum = jnp.einsum('eqf,df->eqd', grad_pre, layer_weight, precision=high)
    grad_qvec = grad_qvec + grad_sum[query_head, jnp.arange(QUERIES)]

    def backward_part(part_index):
        source, dst_slot, rel_slot, live_mask = edge_block(part_index, edge_src, edge_dst, edge_rel, edge_count, send_list)
        upstream = grad_sum[part_index * ENT_DEV + dst_slot]
        edge_terms = jnp.einsum('eqd,eqd->ed', upstream, state_cube[source], precision=high) * live_mask[:, None]
        return jax.ops.segment_sum(edge_terms, rel_slot, num_segments=NREL)

    grad_rel = jnp.sum(lax.map(backward_part, parts), axis=0)
    grad_rel = grad_rel + jax.ops.segment_sum(grad_qvec, query_rel, num_segments=NREL)
    new_state = new_cube.reshape(ENTITIES, QUERIES * D)
    return (new_state, loss, grad_rel, grad_layer, grad_entity, grad_query, grad_score)
```

```python
import functools

import jax
import jax.numpy as jnp
from jax import lax
from jax.experimental import pallas as pl
from jax.experimental.pallas import tpu as pltpu
from jax.sharding import PartitionSpec as P

adversarial = 0.5
HIGH = lax.Precision.HIGHEST
F32 = jnp.float32
BF16 = jnp.bfloat16
LANES = 128
FORWARD = 3
BACKWARD = 2


def pad_to(count, unit):
    return -(-count // unit) * unit


def split_rows(values, pieces):
    found = []
    for _ in range(pieces):
        piece = values.astype(BF16)
        values = values - piece.astype(F32)
        found.append(piece)
    return jnp.concatenate(found, axis=0)


def join_rows(values, pieces):
    rows = values.shape[0] // pieces
    total = values[:rows]
    for piece in range(1, pieces):
        total = total + values[piece * rows : (piece + 1) * rows]
    return total


def one_hot(index_row, rows):
    spots = lax.broadcasted_iota(jnp.int32, (rows, index_row.shape[1]), 0)
    return (spots == index_row).astype(F32).astype(BF16)


def dot_nn(left, right, precision=None):
    return lax.dot_general(
        left, right, (((1,), (0,)), ((), ())), precision=precision, preferred_element_type=F32
    )


def dot_nt(left, right, precision=None):
    return lax.dot_general(
        left, right, (((1,), (1,)), ((), ())), precision=precision, preferred_element_type=F32
    )


def local_row(entity, node, ent_local):
    return jnp.where(entity // ent_local == node, entity % ent_local, -1)


def forward_kernel(
    sizes,
    count_ref,
    head_ref,
    qrel_ref,
    tail_ref,
    state_ref,
    recv_ref,
    src_ref,
    dst_ref,
    rel_ref,
    neg_ref,
    table_ref,
    layer_ref,
    ment_ref,
    mquery_ref,
    score_ref,
    new_ref,
    srct_ref,
    summed_ref,
    pre_ref,
    picked_ref,
    hidden_ref,
    qvec_ref,
    coef_ref,
    totals_ref,
    qrows_ref,
):
    ent, q_local, width, edges, chunk, neg, nodes, queries_total = sizes
    node = lax.axis_index("nodes")
    rel_rows = pad_to(table_ref.shape[0], 16)
    state_t = state_ref[...].T
    recv_t = recv_ref[...].T
    table_bits = jnp.concatenate([split_rows(state_t, FORWARD), split_rows(recv_t, FORWARD)], axis=1)
    slots = table_bits.shape[1]
    rel_t = table_ref[...].T
    rel_bits = jnp.concatenate(
        [split_rows(rel_t, FORWARD), jnp.zeros((FORWARD * width, rel_rows - table_ref.shape[0]), BF16)], axis=1
    )
    live = count_ref[0]
    total = jnp.zeros((FORWARD * q_local * width, ent), F32)
    for start in range(0, edges, chunk):
        span = pl.ds(start, chunk)
        source = join_rows(dot_nn(table_bits, one_hot(src_ref[:, span], slots)), FORWARD)
        srct_ref[:, span] = source
        relation = join_rows(dot_nn(rel_bits, one_hot(rel_ref[:, span], rel_rows)), FORWARD)
        message = source * jnp.concatenate([relation] * q_local, axis=0)
        spot = lax.broadcasted_iota(jnp.int32, (1, chunk), 1) + start
        ends = jnp.where(spot < live, dst_ref[:, span], -1)
        total = total + dot_nt(split_rows(message, FORWARD), one_hot(ends, ent))
    summed = join_rows(total, FORWARD)

    qrows_ref[...] = jnp.zeros_like(qrows_ref)
    for q in range(q_local):
        qrows_ref[q : q + 1, 0:width] = table_ref[pl.ds(qrel_ref[q], 1), :]
    qvec = qrows_ref[...].T[0:width, :]
    qvec_ref[...] = qvec
    entity_row = lax.broadcasted_iota(jnp.int32, (1, ent), 1)
    lane_row = lax.broadcasted_iota(jnp.int32, (1, LANES), 1)
    layer_t = layer_ref[...].T
    new_parts = []
    for q in range(q_local):
        rows = slice(q * width, (q + 1) * width)
        here = (entity_row == local_row(head_ref[q], node, ent)).astype(F32)
        part = summed[rows] + qvec[:, q : q + 1] * here
        summed_ref[rows, :] = part
        pre = dot_nn(layer_t, part, HIGH)
        pre_ref[rows, :] = pre
        new_parts.append(state_t[rows] + jnp.maximum(pre, 0.0))
    new_t = jnp.concatenate(new_parts, axis=0)
    new_ref[...] = new_t.T

    picks = []
    for q in range(q_local):
        hot = one_hot(neg_ref[q : q + 1, :], ent)
        picks.append(join_rows(dot_nn(split_rows(new_parts[q], FORWARD), hot), FORWARD))
    tails = jnp.full((1, LANES), -1, jnp.int32)
    for q in range(q_local):
        tails = jnp.where(lane_row == q, local_row(tail_ref[q], node, ent), tails)
    every = join_rows(dot_nn(split_rows(new_t, FORWARD), one_hot(tails, ent)), FORWARD)
    positive = jnp.zeros((width, LANES), F32)
    for q in range(q_local):
        positive = positive + jnp.where(lane_row == q, every[q * width : (q + 1) * width], 0.0)
    picks.append(positive)
    picked = jnp.concatenate(picks, axis=1)
    picked_ref[...] = picked
    query_part = dot_nn(mquery_ref[...].T, qvec, HIGH)
    plain = dot_nn(ment_ref[...].T, picked, HIGH)
    for q in range(q_local):
        span = slice(q * neg, (q + 1) * neg)
        hidden_ref[:, span] = plain[:, span] + query_part[:, q : q + 1]
    hidden_ref[:, q_local * neg :] = plain[:, q_local * neg :] + query_part
    hidden = hidden_ref[...]
    scores = jnp.sum(jnp.maximum(hidden, 0.0) * score_ref[...], axis=0, keepdims=True)
    part_total = jnp.zeros((1, LANES), F32)
    part_weighted = jnp.zeros((1, LANES), F32)
    for q in range(q_local):
        mine = scores[:, q * neg : (q + 1) * neg]
        weights = jnp.exp(adversarial * mine)
        decay = jnp.exp(-jnp.abs(mine))
        softplus = jnp.maximum(mine, 0.0) + jnp.log1p(decay)
        own = jnp.sum(weights, axis=1, keepdims=True)
        part_total = jnp.where(lane_row == q, own, part_total)
        part_weighted = jnp.where(
            lane_row == q, jnp.sum(weights * softplus, axis=1, keepdims=True), part_weighted
        )
        sigmoid = jnp.where(mine >= 0.0, 1.0, decay) / (1.0 + decay)
        share = weights / jnp.where(own > 0.0, own, 1.0)
        coef_ref[:, q * neg : (q + 1) * neg] = share * sigmoid * (1.0 / queries_total)
    final = scores[:, q_local * neg :]
    decay = jnp.exp(-jnp.abs(final))
    present = tails >= 0
    part_positive = jnp.where(present, jnp.maximum(-final, 0.0) + jnp.log1p(decay), 0.0)
    missing = jnp.where(final >= 0.0, decay, 1.0) / (1.0 + decay)
    coef_ref[:, q_local * neg :] = jnp.where(present, -missing, 0.0) * (1.0 / queries_total)
    tile = jnp.concatenate(
        [part_total, part_weighted, part_positive, jnp.zeros((5, LANES), F32)], axis=0
    )
    for n in range(nodes):
        totals_ref[n] = tile


def backward_kernel(
    sizes,
    count_ref,
    head_ref,
    qrel_ref,
    tail_ref,
    srct_ref,
    dst_ref,
    rel_ref,
    neg_ref,
    layer_ref,
    ment_ref,
    mquery_ref,
    score_ref,
    summed_ref,
    pre_ref,
    picked_ref,
    hidden_ref,
    qvec_ref,
    coef_ref,
    out_ref,
):
    ent, q_local, width, edges, chunk, neg, relations = sizes
    node = lax.axis_index("nodes")
    rel_lanes = pad_to(relations, LANES)
    rel_rows = pad_to(relations, 16)
    hid = ment_ref.shape[1]
    coef = coef_ref[...]
    hidden = hidden_ref[...]
    picked = picked_ref[...]
    qvec = qvec_ref[...]
    grad_hidden = jnp.where(hidden > 0.0, coef * score_ref[...], 0.0)
    active = jnp.maximum(hidden, 0.0)
    both = jnp.concatenate([ment_ref[...], mquery_ref[...]], axis=0)
    grad_both = dot_nn(both, grad_hidden, HIGH)
    entity_row = lax.broadcasted_iota(jnp.int32, (1, ent), 1)
    rel_row = lax.broadcasted_iota(jnp.int32, (1, rel_lanes), 1)
    layer = layer_ref[...]

    def small(span, vectors, gradient_layer, block):
        left = jnp.concatenate([picked[:, span], vectors], axis=0)
        right = grad_hidden[:, span]
        pair = dot_nt(left, right, HIGH)
        score = dot_nt(
            jnp.broadcast_to(coef[:, span], (width, coef[:, span].shape[1])), active[:, span], HIGH
        )
        rest = jnp.concatenate([gradient_layer, pair[:width], pair[width:], score], axis=1)
        rest = jnp.concatenate(
            [rest, jnp.zeros((width, pad_to(rest.shape[1], LANES) - rest.shape[1]), F32)], axis=1
        )
        out_ref[block * width : (block + 1) * width, rel_lanes:] = rest

    sums = []
    relation_seed = []
    tail_sums = []
    tail_seed = jnp.zeros((width, rel_lanes), F32)
    tail_layer = jnp.zeros((width, width), F32)
    last = slice(q_local * neg, q_local * neg + LANES)
    for q in range(q_local):
        rows = slice(q * width, (q + 1) * width)
        span = slice(q * neg, (q + 1) * neg)
        gate = pre_ref[rows, :] > 0.0
        summed = summed_ref[rows, :]
        at_head = (entity_row == local_row(head_ref[q], node, ent)).astype(F32)
        at_rel = (rel_row == qrel_ref[q]).astype(F32)
        cube = join_rows(
            dot_nt(split_rows(grad_both[:width, span], BACKWARD), one_hot(neg_ref[q : q + 1, :], ent)), BACKWARD)
        grad_pre = jnp.where(gate, cube, 0.0)
        grad_sum = dot_nn(layer, grad_pre, HIGH)
        sums.append(grad_sum)
        grad_qvec = jnp.sum(grad_both[width:, span], axis=1, keepdims=True) + jnp.sum(
            grad_sum * at_head, axis=1, keepdims=True
        )
        relation_seed.append(grad_qvec * at_rel)
        small(
            span,
            jnp.broadcast_to(qvec[:, q : q + 1], (width, neg)),
            dot_nt(summed, grad_pre, HIGH),
            q,
        )
        spot = q_local * neg + q
        at_tail = (entity_row == local_row(tail_ref[q], node, ent)).astype(F32)
        tail_pre = jnp.where(gate, grad_both[:width, spot : spot + 1] * at_tail, 0.0)
        tail_layer = tail_layer + dot_nt(summed, tail_pre, HIGH)
        tail_sum = dot_nn(layer, tail_pre, HIGH)
        tail_sums.append(jnp.sum(tail_sum, axis=1, keepdims=True))
        tail_qvec = grad_both[width:, spot : spot + 1] + jnp.sum(
            tail_sum * at_head, axis=1, keepdims=True
        )
        tail_seed = tail_seed + tail_qvec * at_rel
    small(last, qvec, tail_layer, q_local)
    sum_bits = split_rows(jnp.concatenate(sums, axis=0), BACKWARD)
    live = count_ref[0]
    blocks = (q_local + 1) * width
    total = jnp.zeros((BACKWARD * blocks, rel_rows), F32)
    for start in range(0, edges, chunk):
        span = pl.ds(start, chunk)
        spot = lax.broadcasted_iota(jnp.int32, (1, chunk), 1) + start
        ends = jnp.where(spot < live, dst_ref[:, span], -1)
        source = srct_ref[:, span]
        upstream = join_rows(dot_nn(sum_bits, one_hot(ends, ent)), BACKWARD)
        tail_terms = jnp.zeros((width, chunk), F32)
        for q in range(q_local):
            row = local_row(tail_ref[q], node, ent)
            hit = ((ends == row) & (ends >= 0)).astype(F32)
            tail_terms = tail_terms + (tail_sums[q] * hit) * source[q * width : (q + 1) * width]
        terms = jnp.concatenate([upstream * source, tail_terms], axis=0)
        total = total + dot_nt(split_rows(terms, BACKWARD), one_hot(rel_ref[:, span], rel_rows))
    gathered = join_rows(total, BACKWARD)
    gathered = jnp.concatenate(
        [gathered, jnp.zeros((blocks, rel_lanes - rel_rows), F32)], axis=1
    )
    seeds = jnp.concatenate(relation_seed + [tail_seed], axis=0)
    out_ref[:, :rel_lanes] = gathered + seeds


def combine_kernel(sizes, totals_ref, own_ref, grads_ref, sent_ref, loss_ref):
    q_local, width, tiles = sizes
    everyone = jnp.sum(totals_ref[...], axis=0)
    total = everyone[0:1, :]
    own = own_ref[0, 0:1, :]
    scale = own / total
    loss = everyone[2:3, :] + everyone[1:2, :] / total
    for q in range(q_local):
        loss_ref[q] = loss[0, q]
    mixed = grads_ref[q_local * width :, :]
    for q in range(q_local):
        mixed = mixed + grads_ref[q * width : (q + 1) * width, :] * scale[:, q : q + 1]
    for tile in range(tiles):
        sent_ref[:, tile, :] = mixed[:, tile * LANES : (tile + 1) * LANES]
    for tile in range(tiles, sent_ref.shape[1]):
        sent_ref[:, tile, :] = jnp.zeros((width, LANES), F32)


def spread_kernel(parts_ref, out_ref):
    total = jnp.sum(parts_ref[...], axis=0)
    for n in range(out_ref.shape[0]):
        out_ref[n] = total


def unpack_kernel(sizes, rows_ref, rel_ref, layer_ref, ment_ref, mquery_ref, score_ref):
    relations, width, hid, tiles = sizes
    flat = jnp.concatenate([rows_ref[:, tile, :] for tile in range(tiles)], axis=1)
    rel_lanes = pad_to(relations, LANES)
    rel_ref[...] = flat[:, :rel_lanes].T[:relations, :]
    start = rel_lanes
    layer_ref[...] = flat[:, start : start + width]
    start += width
    ment_ref[...] = flat[:, start : start + hid]
    start += hid
    mquery_ref[...] = flat[:, start : start + hid]
    start += hid
    score_ref[...] = flat[0:1, start : start + hid]


def vmem(count):
    return [pl.BlockSpec(memory_space=pltpu.VMEM)] * count


def smem(count):
    return [pl.BlockSpec(memory_space=pltpu.SMEM)] * count


PARAMS = pltpu.CompilerParams(vmem_limit_bytes=40 * 1024 * 1024)


def shape(*dims):
    return jax.ShapeDtypeStruct(dims, F32)


def body(
    state_in,
    edge_src,
    edge_dst,
    edge_rel,
    edge_count,
    send_list,
    query_head,
    query_rel,
    pos_tail,
    neg_ids,
    rel_table,
    layer_weight,
    mlp_entity,
    mlp_query,
    score_weight,
):
    nodes = lax.axis_size("nodes")
    queries = lax.axis_size("queries")
    ent, width_all = state_in.shape
    relations, width = rel_table.shape
    hid = mlp_entity.shape[1]
    q_local = width_all // width
    edges = edge_src.shape[0]
    bound = send_list.shape[2]
    neg = neg_ids.shape[1]
    columns = q_local * neg + LANES
    chunk = min(512, edges)
    outgoing = state_in.at[send_list.reshape(-1)].get(mode="promise_in_bounds")
    arrived = lax.all_to_all(
        outgoing.reshape(nodes, bound, width_all), "nodes", split_axis=0, concat_axis=0, tiled=True
    )
    received = arrived.reshape(nodes * bound, width_all)
    src_row = edge_src.reshape(1, edges)
    dst_row = edge_dst.reshape(1, edges)
    rel_row = edge_rel.reshape(1, edges)
    score_column = score_weight.reshape(hid, 1)
    new_state, source_t, summed, pre, picked, hidden, qvec, coef, totals = pl.pallas_call(
        functools.partial(
            forward_kernel,
            (ent, q_local, width, edges, chunk, neg, nodes, q_local * queries),
        ),
        out_shape=(
            shape(ent, width_all),
            shape(width_all, edges),
            shape(width_all, ent),
            shape(width_all, ent),
            shape(width, columns),
            shape(hid, columns),
            shape(width, LANES),
            shape(1, columns),
            shape(nodes, 8, LANES),
        ),
        in_specs=smem(4) + vmem(11),
        out_specs=tuple(vmem(9)),
        scratch_shapes=[pltpu.VMEM((LANES, LANES), F32)],
        compiler_params=PARAMS,
        name="forward",
    )(
        edge_count,
        query_head,
        query_rel,
        pos_tail,
        state_in,
        received,
        src_row,
        dst_row,
        rel_row,
        neg_ids,
        rel_table,
        layer_weight,
        mlp_entity,
        mlp_query,
        score_column,
    )
    all_totals = lax.all_to_all(totals, "nodes", split_axis=0, concat_axis=0, tiled=True)
    rel_lanes = pad_to(relations, LANES)
    lanes = rel_lanes + pad_to(width + 3 * hid, LANES)
    tiles = lanes // LANES
    grads = pl.pallas_call(
        functools.partial(
            backward_kernel, (ent, q_local, width, edges, chunk, neg, relations)
        ),
        out_shape=shape((q_local + 1) * width, lanes),
        in_specs=smem(4) + vmem(14),
        out_specs=vmem(1)[0],
        compiler_params=PARAMS,
        name="backward",
    )(
        edge_count,
        query_head,
        query_rel,
        pos_tail,
        source_t,
        dst_row,
        rel_row,
        neg_ids,
        layer_weight,
        mlp_entity,
        mlp_query,
        score_column,
        summed,
        pre,
        picked,
        hidden,
        qvec,
        coef,
    )
    tile_rows = pad_to(tiles, 8)
    sent, loss = pl.pallas_call(
        functools.partial(combine_kernel, (q_local, width, tiles)),
        out_shape=(shape(width, tile_rows, LANES), shape(q_local)),
        in_specs=vmem(3),
        out_specs=(vmem(1)[0], smem(1)[0]),
        compiler_params=PARAMS,
        name="combine",
    )(all_totals, totals, grads)

    def spread(parts, count):
        return pl.pallas_call(
            spread_kernel,
            out_shape=shape(count, tile_rows, LANES),
            in_specs=vmem(1),
            out_specs=vmem(1)[0],
            compiler_params=PARAMS,
            name="spread",
        )(parts)

    if nodes * queries == width:
        axes = ("nodes", "queries")
        parts = lax.all_to_all(sent, axes, split_axis=0, concat_axis=0, tiled=True)
        rows = lax.all_to_all(
            spread(parts, width), axes, split_axis=0, concat_axis=0, tiled=True
        )
    elif nodes == width:
        parts = lax.all_to_all(sent, "nodes", split_axis=0, concat_axis=0, tiled=True)
        mine = lax.psum(spread(parts, 1), "queries")
        rows = lax.all_to_all(
            jnp.broadcast_to(mine, sent.shape), "nodes", split_axis=0, concat_axis=0, tiled=True
        )
    else:
        rows = lax.psum(sent, ("nodes", "queries"))
    grad_rel, grad_layer, grad_entity, grad_query, grad_score = pl.pallas_call(
        functools.partial(unpack_kernel, (relations, width, hid, tiles)),
        out_shape=(
            shape(relations, width),
            shape(width, width),
            shape(width, hid),
            shape(width, hid),
            shape(1, hid),
        ),
        in_specs=vmem(1),
        out_specs=tuple(vmem(5)),
        compiler_params=PARAMS,
        name="unpack",
    )(rows)
    return new_state, loss, grad_rel, grad_layer, grad_entity, grad_query, grad_score.reshape(hid)


def solution(mesh):
    in_specs = (
        P("nodes", "queries"),
        P("nodes"),
        P("nodes"),
        P("nodes"),
        P("nodes"),
        P("nodes", None, None),
        P("queries"),
        P("queries"),
        P("queries"),
        P("queries", "nodes"),
        P(),
        P(),
        P(),
        P(),
        P(),
    )
    out_specs = (P("nodes", "queries"), P("queries"), P(), P(), P(), P(), P())
    return jax.shard_map(body, mesh=mesh, in_specs=in_specs, out_specs=out_specs, check_vma=False)
```

```python
import functools

import jax
import jax.numpy as jnp
from jax import lax
from jax.experimental import pallas as pl
from jax.experimental.pallas import tpu as pltpu
from jax.sharding import PartitionSpec as P

adversarial = 0.5
HIGH = lax.Precision.HIGHEST
F32 = jnp.float32
BF16 = jnp.bfloat16
LANES = 128
SUBLANES = 8
FORWARD = 3
BACKWARD = 2


def pad_to(count, unit):
    return -(-count // unit) * unit


def split(values, pieces, axis=0):
    found = []
    for _ in range(pieces):
        piece = values.astype(BF16)
        values = values - piece.astype(F32)
        found.append(piece)
    return jnp.concatenate(found, axis=axis)


def join(values, pieces, axis=0):
    size = values.shape[axis] // pieces
    parts = [
        lax.slice_in_dim(values, piece * size, (piece + 1) * size, axis=axis)
        for piece in range(pieces)
    ]
    return functools.reduce(jnp.add, parts)


def one_hot(index_row, rows):
    spots = lax.broadcasted_iota(jnp.int32, (rows, index_row.shape[1]), 0)
    return (spots == index_row).astype(F32).astype(BF16)


def dot_nn(left, right, precision=None):
    return lax.dot_general(
        left, right, (((1,), (0,)), ((), ())), precision=precision, preferred_element_type=F32
    )


def dot_nt(left, right, precision=None):
    return lax.dot_general(
        left, right, (((1,), (1,)), ((), ())), precision=precision, preferred_element_type=F32
    )


def local_row(entity, ent_local):
    node = lax.axis_index("nodes")
    return jnp.where(entity // ent_local == node, entity % ent_local, -1)


def in_lanes(small_row):
    lane = lax.broadcasted_iota(jnp.int32, (1, LANES), 1)
    found = jnp.full((1, LANES), -1, jnp.int32)
    for spot in range(small_row.shape[1]):
        found = jnp.where(lane == spot, small_row[:, spot : spot + 1], found)
    return found


def as_column(row):
    size = row.shape[1]
    across = lax.broadcasted_iota(jnp.int32, (size, size), 1)
    down = lax.broadcasted_iota(jnp.int32, (size, size), 0)
    return jnp.sum(jnp.where(across == down, row, 0.0), axis=1, keepdims=True)


def on_diagonal(block, times):
    size = block.shape[0]
    wide = jnp.concatenate([jnp.concatenate([block] * times, axis=1)] * times, axis=0)
    across = lax.broadcasted_iota(jnp.int32, wide.shape, 1) // size
    down = lax.broadcasted_iota(jnp.int32, wide.shape, 0) // size
    return jnp.where(across == down, wide, 0.0)


def send_kernel(send_ref, state_ref, out_ref):
    count, bound = send_ref.shape
    ent = state_ref.shape[0]
    pieces = split(state_ref[...], FORWARD, axis=1)
    wanted = send_ref[...].T
    entity = lax.broadcasted_iota(jnp.int32, (bound, ent), 1)
    for n in range(count):
        hot = (entity == wanted[:, n : n + 1]).astype(F32).astype(BF16)
        out_ref[n] = join(dot_nn(hot, pieces), FORWARD, axis=1)


def early_kernel(sizes, state_ref, src_ref, rel_ref, table_ref, local_ref, relation_ref):
    chunk, = sizes
    ent = state_ref.shape[0]
    width, relations = table_ref.shape
    edges = src_ref.shape[1]
    rel_rows = pad_to(relations, 16)
    state_bits = split(state_ref[...].T, FORWARD)
    rel_bits = split(table_ref[...], FORWARD)
    rel_bits = jnp.concatenate(
        [rel_bits, jnp.zeros((FORWARD * width, rel_rows - relations), BF16)], axis=1
    )
    for start in range(0, edges, chunk):
        span = slice(start, start + chunk)
        local_ref[:, span] = join(dot_nn(state_bits, one_hot(src_ref[:, span], ent)), FORWARD)
        relation_ref[:, span] = join(
            dot_nn(rel_bits, one_hot(rel_ref[:, span], rel_rows)), FORWARD
        )


def forward_kernel(
    sizes,
    count_ref,
    head_ref,
    qrel_ref,
    tail_ref,
    state_ref,
    recv_ref,
    src_ref,
    dst_ref,
    neg_ref,
    local_ref,
    relation_ref,
    table_ref,
    layer_ref,
    ment_ref,
    mquery_ref,
    score_ref,
    new_ref,
    srct_ref,
    entity_ref,
    columns_ref,
    totals_ref,
):
    chunk, queries_total = sizes
    ent = state_ref.shape[0]
    edges = src_ref.shape[1]
    width, relations = table_ref.shape
    hid = ment_ref.shape[1]
    q_local, neg = neg_ref.shape
    blocks = q_local * width
    recv_bits = split(recv_ref[...].T, FORWARD)
    live = count_ref[...]
    total = jnp.zeros((FORWARD * blocks, ent), F32)
    for start in range(0, edges, chunk):
        span = slice(start, start + chunk)
        far = one_hot(src_ref[:, span] - ent, recv_bits.shape[1])
        source = local_ref[:, span] + join(dot_nn(recv_bits, far), FORWARD)
        srct_ref[:, span] = source
        message = source * jnp.concatenate([relation_ref[:, span]] * q_local, axis=0)
        spot = lax.broadcasted_iota(jnp.int32, (1, chunk), 1) + start
        ends = jnp.where(spot < live, dst_ref[:, span], -1)
        total = total + dot_nt(split(message, FORWARD), one_hot(ends, ent))
    summed = join(total, FORWARD)

    entity_row = lax.broadcasted_iota(jnp.int32, (1, ent), 1)
    lane_row = lax.broadcasted_iota(jnp.int32, (1, LANES), 1)
    heads = local_row(head_ref[...], ent)
    tails = in_lanes(local_row(tail_ref[...], ent))
    table_bits = jnp.concatenate(
        [
            split(table_ref[...], FORWARD),
            jnp.zeros((FORWARD * width, pad_to(relations, LANES) - relations), BF16),
        ],
        axis=1,
    )
    qvec = join(dot_nn(table_bits, one_hot(in_lanes(qrel_ref[...]), table_bits.shape[1])), FORWARD)
    seeds = [
        qvec[:, q : q + 1] * (entity_row == heads[:, q : q + 1]).astype(F32)
        for q in range(q_local)
    ]
    summed = summed + jnp.concatenate(seeds, axis=0)
    pre = dot_nn(on_diagonal(layer_ref[...].T, q_local), summed, HIGH)
    entity_ref[:blocks, :] = summed
    entity_ref[blocks:, :] = pre
    new_t = state_ref[...].T + jnp.maximum(pre, 0.0)
    new_ref[...] = new_t.T

    for q in range(q_local):
        own = new_t[q * width : (q + 1) * width]
        hot = one_hot(neg_ref[q : q + 1, :], ent)
        columns_ref[:width, q * neg : (q + 1) * neg] = join(
            dot_nn(split(own, FORWARD), hot), FORWARD
        )
    every = join(dot_nn(split(new_t, FORWARD), one_hot(tails, ent)), FORWARD)
    positive = jnp.zeros((width, LANES), F32)
    for q in range(q_local):
        positive = positive + jnp.where(lane_row == q, every[q * width : (q + 1) * width], 0.0)
    last = slice(q_local * neg, q_local * neg + LANES)
    columns_ref[:width, last] = positive
    count = q_local * neg + LANES
    query_part = dot_nn(mquery_ref[...].T, qvec, HIGH)
    plain = dot_nn(ment_ref[...].T, columns_ref[:width, :count], HIGH)
    for q in range(q_local):
        span = slice(q * neg, (q + 1) * neg)
        columns_ref[width : width + hid, span] = plain[:, span] + query_part[:, q : q + 1]
    columns_ref[width : width + hid, last] = plain[:, last] + query_part
    columns_ref[:width, count:] = qvec
    columns_ref[width : width + hid, count:] = jnp.zeros((hid, LANES), F32)
    hidden = columns_ref[width : width + hid, :count]
    scores = jnp.sum(
        jnp.maximum(hidden, 0.0) * as_column(score_ref[...]), axis=0, keepdims=True
    )
    part_total = jnp.zeros((1, LANES), F32)
    part_weighted = jnp.zeros((1, LANES), F32)
    base = width + hid
    columns_ref[base:, :] = jnp.zeros((SUBLANES, count + LANES), F32)
    for q in range(q_local):
        span = slice(q * neg, (q + 1) * neg)
        mine = scores[:, span]
        weights = jnp.exp(adversarial * mine)
        decay = jnp.exp(-jnp.abs(mine))
        softplus = jnp.maximum(mine, 0.0) + jnp.log1p(decay)
        own = jnp.sum(weights, axis=1, keepdims=True)
        part_total = jnp.where(lane_row == q, own, part_total)
        part_weighted = jnp.where(
            lane_row == q, jnp.sum(weights * softplus, axis=1, keepdims=True), part_weighted
        )
        sigmoid = jnp.where(mine >= 0.0, 1.0, decay) / (1.0 + decay)
        share = weights / jnp.where(own > 0.0, own, 1.0)
        columns_ref[base : base + 1, span] = share * sigmoid * (1.0 / queries_total)
        columns_ref[base + 1 : base + 2, span] = neg_ref[q : q + 1, :].astype(F32)
    final = scores[:, last]
    decay = jnp.exp(-jnp.abs(final))
    present = tails >= 0
    part_positive = jnp.where(present, jnp.maximum(-final, 0.0) + jnp.log1p(decay), 0.0)
    missing = jnp.where(final >= 0.0, decay, 1.0) / (1.0 + decay)
    columns_ref[base : base + 1, last] = jnp.where(present, -missing, 0.0) * (1.0 / queries_total)
    columns_ref[base + 1 : base + 2, last] = tails.astype(F32)
    columns_ref[base : base + 1, count:] = in_lanes(heads).astype(F32)
    columns_ref[base + 1 : base + 2, count:] = in_lanes(qrel_ref[...]).astype(F32)
    tile = jnp.concatenate(
        [part_total, part_weighted, part_positive, jnp.zeros((5, LANES), F32)], axis=0
    )
    for n in range(totals_ref.shape[0]):
        totals_ref[n] = tile


def backward_kernel(
    sizes,
    count_ref,
    srct_ref,
    dst_ref,
    rel_ref,
    layer_ref,
    ment_ref,
    mquery_ref,
    score_ref,
    entity_ref,
    columns_ref,
    out_ref,
):
    chunk, relations, q_local, neg = sizes
    width, hid = ment_ref.shape
    ent = entity_ref.shape[1]
    edges = dst_ref.shape[1]
    blocks = q_local * width
    count = q_local * neg + LANES
    last = slice(q_local * neg, count)
    base = width + hid
    rel_lanes = pad_to(relations, LANES)
    rel_rows = pad_to(relations, 16)
    picked = columns_ref[:width, :count]
    hidden = columns_ref[width:base, :count]
    qvec = columns_ref[:width, count:]
    coef = columns_ref[base : base + 1, :count]
    picks = columns_ref[base + 1 : base + 2, :count].astype(jnp.int32)
    heads = columns_ref[base : base + 1, count:].astype(jnp.int32)
    qrels = columns_ref[base + 1 : base + 2, count:].astype(jnp.int32)
    tails = picks[:, last]
    grad_hidden = jnp.where(hidden > 0.0, coef * as_column(score_ref[...]), 0.0)
    active = jnp.maximum(hidden, 0.0)
    both = jnp.concatenate([ment_ref[...], mquery_ref[...]], axis=0)
    grad_both = dot_nn(both, grad_hidden, HIGH)
    entity_row = lax.broadcasted_iota(jnp.int32, (1, ent), 1)
    rel_row = lax.broadcasted_iota(jnp.int32, (1, rel_lanes), 1)
    layer = on_diagonal(layer_ref[...], q_local)
    summed = entity_ref[:blocks, :]
    gate = entity_ref[blocks:, :] > 0.0

    cubes, tail_cubes = [], []
    for q in range(q_local):
        span = slice(q * neg, (q + 1) * neg)
        hot = one_hot(picks[:, span], ent)
        cubes.append(join(dot_nt(split(grad_both[:width, span], BACKWARD), hot), BACKWARD))
        spot = q_local * neg + q
        at_tail = (entity_row == tails[:, q : q + 1]).astype(F32)
        tail_cubes.append(grad_both[:width, spot : spot + 1] * at_tail)
    grad_pre = jnp.where(gate, jnp.concatenate(cubes, axis=0), 0.0)
    tail_pre = jnp.where(gate, jnp.concatenate(tail_cubes, axis=0), 0.0)
    grad_sum = dot_nn(layer, grad_pre, HIGH)
    tail_sum = dot_nn(layer, tail_pre, HIGH)
    grad_layer = dot_nt(summed, grad_pre, HIGH)
    tail_layer = dot_nt(summed, tail_pre, HIGH)

    seeds = []
    tail_seed = jnp.zeros((width, rel_lanes), F32)
    layer_parts = []
    tail_part = jnp.zeros((width, width), F32)
    for q in range(q_local):
        rows = slice(q * width, (q + 1) * width)
        span = slice(q * neg, (q + 1) * neg)
        spot = q_local * neg + q
        at_head = (entity_row == heads[:, q : q + 1]).astype(F32)
        at_rel = (rel_row == qrels[:, q : q + 1]).astype(F32)
        grad_qvec = jnp.sum(grad_both[width:, span], axis=1, keepdims=True) + jnp.sum(
            grad_sum[rows] * at_head, axis=1, keepdims=True
        )
        seeds.append(grad_qvec * at_rel)
        tail_qvec = grad_both[width:, spot : spot + 1] + jnp.sum(
            tail_sum[rows] * at_head, axis=1, keepdims=True
        )
        tail_seed = tail_seed + tail_qvec * at_rel
        layer_parts.append(grad_layer[rows, rows])
        tail_part = tail_part + tail_layer[rows, rows]
    seeds.append(tail_seed)
    layer_parts.append(tail_part)
    spare = out_ref.shape[1] - rel_lanes - width - 3 * hid
    for block in range(q_local + 1):
        if block < q_local:
            span = slice(block * neg, (block + 1) * neg)
            vectors = jnp.broadcast_to(qvec[:, block : block + 1], (width, neg))
        else:
            span, vectors = last, qvec
        size = span.stop - span.start
        entity_part = dot_nt(picked[:, span], grad_hidden[:, span], HIGH)
        query_part = dot_nt(vectors, grad_hidden[:, span], HIGH)
        score_part = dot_nt(
            jnp.broadcast_to(coef[:, span], (width, size)), active[:, span], HIGH
        )
        rest = [layer_parts[block], entity_part, query_part, score_part]
        rest.append(jnp.zeros((width, spare), F32))
        out_ref[block * width : (block + 1) * width, rel_lanes:] = jnp.concatenate(rest, axis=1)

    sum_bits = split(grad_sum, BACKWARD)
    tail_column = jnp.sum(tail_sum, axis=1, keepdims=True)
    live = count_ref[...]
    total = jnp.zeros((BACKWARD * (blocks + width), rel_rows), F32)
    for start in range(0, edges, chunk):
        span = slice(start, start + chunk)
        spot = lax.broadcasted_iota(jnp.int32, (1, chunk), 1) + start
        ends = jnp.where(spot < live, dst_ref[:, span], -2)
        source = srct_ref[:, span]
        upstream = join(dot_nn(sum_bits, one_hot(ends, ent)), BACKWARD)
        tail_terms = jnp.zeros((width, chunk), F32)
        for q in range(q_local):
            rows = slice(q * width, (q + 1) * width)
            hit = (ends == tails[:, q : q + 1]).astype(F32)
            tail_terms = tail_terms + (tail_column[rows] * hit) * source[rows]
        terms = jnp.concatenate([upstream * source, tail_terms], axis=0)
        total = total + dot_nt(split(terms, BACKWARD), one_hot(rel_ref[:, span], rel_rows))
    gathered = join(total, BACKWARD)
    if rel_lanes > rel_rows:
        gathered = jnp.concatenate(
            [gathered, jnp.zeros((blocks + width, rel_lanes - rel_rows), F32)], axis=1
        )
    out_ref[:, :rel_lanes] = gathered + jnp.concatenate(seeds, axis=0)


def combine_kernel(sizes, totals_ref, own_ref, grads_ref, sent_ref, loss_ref):
    q_local, width = sizes
    everyone = jnp.sum(totals_ref[...], axis=0)
    total = everyone[0:1, :]
    scale = own_ref[0, 0:1, :] / total
    loss_ref[...] = (everyone[2:3, :] + everyone[1:2, :] / total)[:, :q_local]
    mixed = grads_ref[q_local * width :, :]
    for q in range(q_local):
        mixed = mixed + grads_ref[q * width : (q + 1) * width, :] * scale[:, q : q + 1]
    across = mixed.shape[1] // LANES
    tiles = width // SUBLANES * across
    for tile in range(tiles):
        top, left = tile // across * SUBLANES, tile % across * LANES
        sent_ref[tile] = mixed[top : top + SUBLANES, left : left + LANES]
    for tile in range(tiles, sent_ref.shape[0]):
        sent_ref[tile] = jnp.zeros((SUBLANES, LANES), F32)


def spread_kernel(parts_ref, out_ref):
    total = jnp.sum(parts_ref[...], axis=0)
    for n in range(out_ref.shape[0]):
        out_ref[n] = total


def unpack_kernel(sizes, tiles_ref, rel_ref, layer_ref, ment_ref, mquery_ref, score_ref):
    relations, across = sizes
    width, hid = ment_ref.shape
    down = width // SUBLANES
    flat = jnp.concatenate(
        [
            jnp.concatenate([tiles_ref[row * across + tile] for tile in range(across)], axis=1)
            for row in range(down)
        ],
        axis=0,
    )
    rel_lanes = pad_to(relations, LANES)
    rel_ref[...] = flat[:, :relations]
    start = rel_lanes
    layer_ref[...] = flat[:, start : start + width]
    start += width
    ment_ref[...] = flat[:, start : start + hid]
    start += hid
    mquery_ref[...] = flat[:, start : start + hid]
    start += hid
    score_ref[...] = flat[0:1, start : start + hid]


def vmem(count):
    return [pl.BlockSpec(memory_space=pltpu.VMEM)] * count


def call(kernel, name, outs, flops, *operands):
    found = pl.pallas_call(
        kernel,
        out_shape=tuple(jax.ShapeDtypeStruct(dims, F32) for dims in outs),
        in_specs=vmem(len(operands)),
        out_specs=tuple(vmem(len(outs))),
        compiler_params=pltpu.CompilerParams(vmem_limit_bytes=40 * 1024 * 1024),
        cost_estimate=pl.CostEstimate(flops=flops, bytes_accessed=1 << 20, transcendentals=0),
        name=name,
    )(*operands)
    return found[0] if len(outs) == 1 else found


def swap(values, axes):
    return lax.all_to_all(values, axes, split_axis=0, concat_axis=0, tiled=True)


def body(
    state_in,
    edge_src,
    edge_dst,
    edge_rel,
    edge_count,
    send_list,
    query_head,
    query_rel,
    pos_tail,
    neg_ids,
    rel_table,
    layer_weight,
    mlp_entity,
    mlp_query,
    score_weight,
):
    nodes = lax.axis_size("nodes")
    queries = lax.axis_size("queries")
    ent, width_all = state_in.shape
    relations, width = rel_table.shape
    hid = mlp_entity.shape[1]
    q_local = width_all // width
    edges = edge_src.shape[0]
    bound = send_list.shape[2]
    neg = neg_ids.shape[1]
    columns = q_local * neg + 2 * LANES
    chunk = min(512, edges)
    src_row = edge_src.reshape(1, edges)
    dst_row = edge_dst.reshape(1, edges)
    rel_row = edge_rel.reshape(1, edges)
    count = edge_count.reshape(1, 1)
    score_row = score_weight.reshape(1, hid)
    table_t = rel_table.T
    outgoing = call(
        send_kernel, "send", [(nodes, bound, width_all)], 10**9, send_list[0], state_in
    )
    received = swap(outgoing, "nodes").reshape(nodes * bound, width_all)
    local, relation = call(
        functools.partial(early_kernel, (chunk,)),
        "early",
        [(width_all, edges), (width, edges)],
        4 * 10**9,
        state_in,
        src_row,
        rel_row,
        table_t,
    )
    new_state, source_t, entity, cols, totals = call(
        functools.partial(forward_kernel, (chunk, q_local * queries)),
        "forward",
        [
            (ent, width_all),
            (width_all, edges),
            (2 * width_all, ent),
            (width + hid + SUBLANES, columns),
            (nodes, SUBLANES, LANES),
        ],
        4 * 10**9,
        count,
        query_head.reshape(1, q_local),
        query_rel.reshape(1, q_local),
        pos_tail.reshape(1, q_local),
        state_in,
        received,
        src_row,
        dst_row,
        neg_ids,
        local,
        relation,
        table_t,
        layer_weight,
        mlp_entity,
        mlp_query,
        score_row,
    )
    all_totals = swap(totals, "nodes")
    rel_lanes = pad_to(relations, LANES)
    lanes = rel_lanes + pad_to(width + 3 * hid, LANES)
    across = lanes // LANES
    grads = call(
        functools.partial(backward_kernel, (chunk, relations, q_local, neg)),
        "backward",
        [((q_local + 1) * width, lanes)],
        4 * 10**9,
        count,
        source_t,
        dst_row,
        rel_row,
        layer_weight,
        mlp_entity,
        mlp_query,
        score_row,
        entity,
        cols,
    )
    tiles = width // SUBLANES * across
    wide = nodes * queries
    group = wide if wide <= pad_to(tiles, nodes) else nodes
    held = pad_to(tiles, group)
    sent, loss = call(
        functools.partial(combine_kernel, (q_local, width)),
        "combine",
        [(held, SUBLANES, LANES), (1, q_local)],
        10**6,
        all_totals,
        totals,
        grads,
    )
    axes = ("nodes", "queries") if group == wide else "nodes"
    own = held // group
    parts = swap(sent, axes).reshape(group, own * SUBLANES, LANES)
    if group == wide:
        mine = call(spread_kernel, "spread", [(group, own * SUBLANES, LANES)], 10**6, parts)
    else:
        mine = lax.psum(jnp.sum(parts, axis=0), "queries")
        mine = jnp.broadcast_to(mine, (group,) + mine.shape)
    final = swap(mine, axes).reshape(held, SUBLANES, LANES)
    grad_rel, grad_layer, grad_entity, grad_query, grad_score = call(
        functools.partial(unpack_kernel, (relations, across)),
        "unpack",
        [(width, relations), (width, width), (width, hid), (width, hid), (1, hid)],
        10**6,
        final,
    )
    return (
        new_state,
        loss.reshape(q_local),
        grad_rel.T,
        grad_layer,
        grad_entity,
        grad_query,
        grad_score.reshape(hid),
    )


def solution(mesh):
    in_specs = (
        P("nodes", "queries"),
        P("nodes"),
        P("nodes"),
        P("nodes"),
        P("nodes"),
        P("nodes", None, None),
        P("queries"),
        P("queries"),
        P("queries"),
        P("queries", "nodes"),
        P(),
        P(),
        P(),
        P(),
        P(),
    )
    out_specs = (P("nodes", "queries"), P("queries"), P(), P(), P(), P(), P())
    return jax.shard_map(body, mesh=mesh, in_specs=in_specs, out_specs=out_specs, check_vma=False)
```

```python
import functools

import jax
import jax.numpy as jnp
from jax import lax
from jax.experimental import pallas as pl
from jax.experimental.pallas import tpu as pltpu
from jax.sharding import PartitionSpec as P

adversarial = 0.5
HIGH = lax.Precision.HIGHEST
F32 = jnp.float32
BF16 = jnp.bfloat16
LANES = 128
SUBLANES = 8
FORWARD = 3
BACKWARD = 2
SEND_LIMIT = 64 << 20


def pad_to(count, unit):
    return -(-count // unit) * unit


def split(values, pieces, axis=0):
    found = []
    for _ in range(pieces):
        piece = values.astype(BF16)
        values = values - piece.astype(F32)
        found.append(piece)
    return jnp.concatenate(found, axis=axis)


def join(values, pieces, axis=0):
    size = values.shape[axis] // pieces
    parts = [
        lax.slice_in_dim(values, piece * size, (piece + 1) * size, axis=axis)
        for piece in range(pieces)
    ]
    return functools.reduce(jnp.add, parts)


def one_hot(index_row, rows):
    parts = []
    for base in range(0, rows, 256):
        size = min(256, rows - base)
        local = index_row - base
        key = jnp.where((local >= 0) & (local < size), local, -1).astype(F32).astype(BF16)
        spots = lax.broadcasted_iota(jnp.int32, (size, index_row.shape[1]), 0)
        same = spots.astype(F32).astype(BF16) == key
        parts.append(jnp.where(same, jnp.ones((), BF16), jnp.zeros((), BF16)))
    return parts[0] if len(parts) == 1 else jnp.concatenate(parts, axis=0)


def dot_nn(left, right, precision=None):
    return lax.dot_general(
        left, right, (((1,), (0,)), ((), ())), precision=precision, preferred_element_type=F32
    )


def dot_nt(left, right, precision=None):
    return lax.dot_general(
        left, right, (((1,), (1,)), ((), ())), precision=precision, preferred_element_type=F32
    )


def local_row(entity, ent_local):
    node = lax.axis_index("nodes")
    return jnp.where(entity // ent_local == node, entity % ent_local, -1)


def in_lanes(small_row):
    lane = lax.broadcasted_iota(jnp.int32, (1, LANES), 1)
    found = jnp.full((1, LANES), -1, jnp.int32)
    for spot in range(small_row.shape[1]):
        found = jnp.where(lane == spot, small_row[:, spot : spot + 1], found)
    return found


def as_column(row):
    size = row.shape[1]
    across = lax.broadcasted_iota(jnp.int32, (size, size), 1)
    down = lax.broadcasted_iota(jnp.int32, (size, size), 0)
    return jnp.sum(jnp.where(across == down, row, 0.0), axis=1, keepdims=True)


def on_diagonal(block, times):
    size = block.shape[0]
    wide = jnp.concatenate([jnp.concatenate([block] * times, axis=1)] * times, axis=0)
    across = lax.broadcasted_iota(jnp.int32, wide.shape, 1) // size
    down = lax.broadcasted_iota(jnp.int32, wide.shape, 0) // size
    return jnp.where(across == down, wide, 0.0)


def send_kernel(send_hbm, state_hbm, out_ref, send_ref, state_ref, sems):
    copies = [
        pltpu.make_async_copy(send_hbm, send_ref, sems.at[0]),
        pltpu.make_async_copy(state_hbm, state_ref, sems.at[1]),
    ]
    for copy in copies:
        copy.start()
    for copy in copies:
        copy.wait()
    count, bound = send_ref.shape
    ent = state_ref.shape[0]
    pieces = split(state_ref[...], FORWARD, axis=1)
    wanted = send_ref[...].T
    entity = lax.broadcasted_iota(jnp.int32, (bound, ent), 1)
    for n in range(count):
        hot = (entity == wanted[:, n : n + 1]).astype(F32).astype(BF16)
        out_ref[n] = join(dot_nn(hot, pieces), FORWARD, axis=1)


def early_kernel(sizes, state_ref, src_ref, rel_ref, table_ref, local_ref, relation_ref):
    chunk, = sizes
    ent = state_ref.shape[0]
    width, relations = table_ref.shape
    edges = src_ref.shape[1]
    rel_rows = pad_to(relations, 16)
    state_bits = split(state_ref[...].T, FORWARD)
    rel_bits = split(table_ref[...], FORWARD)
    rel_bits = jnp.concatenate(
        [rel_bits, jnp.zeros((FORWARD * width, rel_rows - relations), BF16)], axis=1
    )
    for start in range(0, edges, chunk):
        span = slice(start, start + chunk)
        local_ref[:, span] = join(dot_nn(state_bits, one_hot(src_ref[:, span], ent)), FORWARD)
        relation_ref[:, span] = join(
            dot_nn(rel_bits, one_hot(rel_ref[:, span], rel_rows)), FORWARD
        )


def forward_kernel(
    sizes,
    count_ref,
    head_ref,
    qrel_ref,
    tail_ref,
    state_ref,
    recv_ref,
    src_ref,
    dst_ref,
    neg_ref,
    local_ref,
    relation_ref,
    table_ref,
    layer_ref,
    ment_ref,
    mquery_ref,
    score_ref,
    new_ref,
    srct_ref,
    summed_ref,
    gate_ref,
    columns_ref,
    totals_ref,
):
    chunk, queries_total = sizes
    ent = state_ref.shape[0]
    edges = src_ref.shape[1]
    width, relations = table_ref.shape
    hid = ment_ref.shape[1]
    q_local, neg = neg_ref.shape
    blocks = q_local * width
    recv_bits = split(recv_ref[...].T, FORWARD)
    live = count_ref[...]
    total = jnp.zeros((FORWARD * blocks, ent), F32)
    for start in range(0, edges, chunk):
        span = slice(start, start + chunk)
        far = one_hot(src_ref[:, span] - ent, recv_bits.shape[1])
        source = local_ref[:, span] + join(dot_nn(recv_bits, far), FORWARD)
        srct_ref[:, span] = source
        message = source * jnp.concatenate([relation_ref[:, span]] * q_local, axis=0)
        spot = lax.broadcasted_iota(jnp.int32, (1, chunk), 1) + start
        ends = jnp.where(spot < live, dst_ref[:, span], -1)
        total = total + dot_nt(split(message, FORWARD), one_hot(ends, ent))
    summed = join(total, FORWARD)

    entity_row = lax.broadcasted_iota(jnp.int32, (1, ent), 1)
    lane_row = lax.broadcasted_iota(jnp.int32, (1, LANES), 1)
    heads = local_row(head_ref[...], ent)
    tails = in_lanes(local_row(tail_ref[...], ent))
    table_bits = jnp.concatenate(
        [
            split(table_ref[...], FORWARD),
            jnp.zeros((FORWARD * width, pad_to(relations, LANES) - relations), BF16),
        ],
        axis=1,
    )
    qvec = join(dot_nn(table_bits, one_hot(in_lanes(qrel_ref[...]), table_bits.shape[1])), FORWARD)
    seeds = [
        qvec[:, q : q + 1] * (entity_row == heads[:, q : q + 1]).astype(F32)
        for q in range(q_local)
    ]
    summed = summed + jnp.concatenate(seeds, axis=0)
    pre = dot_nn(on_diagonal(layer_ref[...].T, q_local), summed, HIGH)
    summed_ref[...] = summed
    gate_ref[...] = (pre > 0.0).astype(F32).astype(BF16)
    new_t = state_ref[...].T + jnp.maximum(pre, 0.0)
    new_ref[...] = new_t.T

    for q in range(q_local):
        own = new_t[q * width : (q + 1) * width]
        hot = one_hot(neg_ref[q : q + 1, :], ent)
        columns_ref[:width, q * neg : (q + 1) * neg] = join(
            dot_nn(split(own, FORWARD), hot), FORWARD
        )
    every = join(dot_nn(split(new_t, FORWARD), one_hot(tails, ent)), FORWARD)
    positive = jnp.zeros((width, LANES), F32)
    for q in range(q_local):
        positive = positive + jnp.where(lane_row == q, every[q * width : (q + 1) * width], 0.0)
    last = slice(q_local * neg, q_local * neg + LANES)
    columns_ref[:width, last] = positive
    count = q_local * neg + LANES
    query_part = dot_nn(mquery_ref[...].T, qvec, HIGH)
    plain = dot_nn(ment_ref[...].T, columns_ref[:width, :count], HIGH)
    for q in range(q_local):
        span = slice(q * neg, (q + 1) * neg)
        columns_ref[width : width + hid, span] = plain[:, span] + query_part[:, q : q + 1]
    columns_ref[width : width + hid, last] = plain[:, last] + query_part
    columns_ref[:width, count:] = qvec
    columns_ref[width : width + hid, count:] = jnp.zeros((hid, LANES), F32)
    hidden = columns_ref[width : width + hid, :count]
    scores = jnp.sum(
        jnp.maximum(hidden, 0.0) * as_column(score_ref[...]), axis=0, keepdims=True
    )
    part_total = jnp.zeros((1, LANES), F32)
    part_weighted = jnp.zeros((1, LANES), F32)
    base = width + hid
    columns_ref[base:, :] = jnp.zeros((SUBLANES, count + LANES), F32)
    for q in range(q_local):
        span = slice(q * neg, (q + 1) * neg)
        mine = scores[:, span]
        weights = jnp.exp(adversarial * mine)
        decay = jnp.exp(-jnp.abs(mine))
        softplus = jnp.maximum(mine, 0.0) + jnp.log1p(decay)
        own = jnp.sum(weights, axis=1, keepdims=True)
        part_total = jnp.where(lane_row == q, own, part_total)
        part_weighted = jnp.where(
            lane_row == q, jnp.sum(weights * softplus, axis=1, keepdims=True), part_weighted
        )
        sigmoid = jnp.where(mine >= 0.0, 1.0, decay) / (1.0 + decay)
        share = weights / jnp.where(own > 0.0, own, 1.0)
        columns_ref[base : base + 1, span] = share * sigmoid * (1.0 / queries_total)
        columns_ref[base + 1 : base + 2, span] = neg_ref[q : q + 1, :].astype(F32)
    final = scores[:, last]
    decay = jnp.exp(-jnp.abs(final))
    present = tails >= 0
    part_positive = jnp.where(present, jnp.maximum(-final, 0.0) + jnp.log1p(decay), 0.0)
    missing = jnp.where(final >= 0.0, decay, 1.0) / (1.0 + decay)
    columns_ref[base : base + 1, last] = jnp.where(present, -missing, 0.0) * (1.0 / queries_total)
    columns_ref[base + 1 : base + 2, last] = tails.astype(F32)
    columns_ref[base : base + 1, count:] = in_lanes(heads).astype(F32)
    columns_ref[base + 1 : base + 2, count:] = in_lanes(qrel_ref[...]).astype(F32)
    tile = jnp.concatenate(
        [part_total, part_weighted, part_positive, jnp.zeros((5, LANES), F32)], axis=0
    )
    for n in range(totals_ref.shape[0]):
        totals_ref[n] = tile


def backward_kernel(
    sizes,
    count_ref,
    srct_ref,
    dst_ref,
    rel_ref,
    layer_ref,
    ment_ref,
    mquery_ref,
    score_ref,
    summed_ref,
    gate_ref,
    columns_ref,
    out_ref,
):
    chunk, relations, q_local, neg = sizes
    width, hid = ment_ref.shape
    ent = summed_ref.shape[1]
    edges = dst_ref.shape[1]
    blocks = q_local * width
    count = q_local * neg + LANES
    last = slice(q_local * neg, count)
    base = width + hid
    rel_lanes = pad_to(relations, LANES)
    rel_rows = pad_to(relations, 16)
    picked = columns_ref[:width, :count]
    hidden = columns_ref[width:base, :count]
    qvec = columns_ref[:width, count:]
    coef = columns_ref[base : base + 1, :count]
    picks = columns_ref[base + 1 : base + 2, :count].astype(jnp.int32)
    heads = columns_ref[base : base + 1, count:].astype(jnp.int32)
    qrels = columns_ref[base + 1 : base + 2, count:].astype(jnp.int32)
    tails = picks[:, last]
    grad_hidden = jnp.where(hidden > 0.0, coef * as_column(score_ref[...]), 0.0)
    active = jnp.maximum(hidden, 0.0)
    both = jnp.concatenate([ment_ref[...], mquery_ref[...]], axis=0)
    grad_both = dot_nn(both, grad_hidden, HIGH)
    entity_row = lax.broadcasted_iota(jnp.int32, (1, ent), 1)
    rel_row = lax.broadcasted_iota(jnp.int32, (1, rel_lanes), 1)
    layer = on_diagonal(layer_ref[...], q_local)
    summed = summed_ref[...]
    gate = gate_ref[...].astype(F32)

    cubes, tail_cubes = [], []
    for q in range(q_local):
        span = slice(q * neg, (q + 1) * neg)
        hot = one_hot(picks[:, span], ent)
        cubes.append(join(dot_nt(split(grad_both[:width, span], BACKWARD), hot), BACKWARD))
        spot = q_local * neg + q
        at_tail = (entity_row == tails[:, q : q + 1]).astype(F32)
        tail_cubes.append(grad_both[:width, spot : spot + 1] * at_tail)
    grad_pre = gate * jnp.concatenate(cubes, axis=0)
    tail_pre = gate * jnp.concatenate(tail_cubes, axis=0)
    grad_sum = dot_nn(layer, grad_pre, HIGH)
    tail_sum = dot_nn(layer, tail_pre, HIGH)
    grad_layer = dot_nt(summed, grad_pre, HIGH)
    tail_layer = dot_nt(summed, tail_pre, HIGH)

    seeds = []
    tail_seed = jnp.zeros((width, rel_lanes), F32)
    layer_parts = []
    tail_part = jnp.zeros((width, width), F32)
    for q in range(q_local):
        rows = slice(q * width, (q + 1) * width)
        span = slice(q * neg, (q + 1) * neg)
        spot = q_local * neg + q
        at_head = (entity_row == heads[:, q : q + 1]).astype(F32)
        at_rel = (rel_row == qrels[:, q : q + 1]).astype(F32)
        grad_qvec = jnp.sum(grad_both[width:, span], axis=1, keepdims=True) + jnp.sum(
            grad_sum[rows] * at_head, axis=1, keepdims=True
        )
        seeds.append(grad_qvec * at_rel)
        tail_qvec = grad_both[width:, spot : spot + 1] + jnp.sum(
            tail_sum[rows] * at_head, axis=1, keepdims=True
        )
        tail_seed = tail_seed + tail_qvec * at_rel
        layer_parts.append(grad_layer[rows, rows])
        tail_part = tail_part + tail_layer[rows, rows]
    seeds.append(tail_seed)
    layer_parts.append(tail_part)
    spare = out_ref.shape[1] - rel_lanes - width - 3 * hid
    for block in range(q_local + 1):
        if block < q_local:
            span = slice(block * neg, (block + 1) * neg)
            vectors = jnp.broadcast_to(qvec[:, block : block + 1], (width, neg))
        else:
            span, vectors = last, qvec
        size = span.stop - span.start
        entity_part = dot_nt(picked[:, span], grad_hidden[:, span], HIGH)
        query_part = dot_nt(vectors, grad_hidden[:, span], HIGH)
        score_part = dot_nt(
            jnp.broadcast_to(coef[:, span], (width, size)), active[:, span], HIGH
        )
        rest = [layer_parts[block], entity_part, query_part, score_part]
        rest.append(jnp.zeros((width, spare), F32))
        out_ref[block * width : (block + 1) * width, rel_lanes:] = jnp.concatenate(rest, axis=1)

    sum_bits = split(grad_sum, BACKWARD)
    tail_column = jnp.sum(tail_sum, axis=1, keepdims=True)
    live = count_ref[...]
    total = jnp.zeros((BACKWARD * (blocks + width), rel_rows), F32)
    for start in range(0, edges, chunk):
        span = slice(start, start + chunk)
        spot = lax.broadcasted_iota(jnp.int32, (1, chunk), 1) + start
        ends = jnp.where(spot < live, dst_ref[:, span], -2)
        source = srct_ref[:, span]
        upstream = join(dot_nn(sum_bits, one_hot(ends, ent)), BACKWARD)
        tail_terms = jnp.zeros((width, chunk), F32)
        for q in range(q_local):
            rows = slice(q * width, (q + 1) * width)
            hit = (ends == tails[:, q : q + 1]).astype(F32)
            tail_terms = tail_terms + (tail_column[rows] * hit) * source[rows]
        terms = jnp.concatenate([upstream * source, tail_terms], axis=0)
        total = total + dot_nt(split(terms, BACKWARD), one_hot(rel_ref[:, span], rel_rows))
    gathered = join(total, BACKWARD)
    if rel_lanes > rel_rows:
        gathered = jnp.concatenate(
            [gathered, jnp.zeros((blocks + width, rel_lanes - rel_rows), F32)], axis=1
        )
    out_ref[:, :rel_lanes] = gathered + jnp.concatenate(seeds, axis=0)


def combine_kernel(sizes, totals_ref, own_ref, grads_ref, sent_ref):
    q_local, width = sizes
    total = jnp.sum(totals_ref[...], axis=0)[0:1, :]
    scale = own_ref[0, 0:1, :] / total
    mixed = grads_ref[q_local * width :, :]
    for q in range(q_local):
        mixed = mixed + grads_ref[q * width : (q + 1) * width, :] * scale[:, q : q + 1]
    across = mixed.shape[1] // LANES
    tiles = width // SUBLANES * across
    for tile in range(tiles):
        top, left = tile // across * SUBLANES, tile % across * LANES
        sent_ref[tile] = mixed[top : top + SUBLANES, left : left + LANES]
    for tile in range(tiles, sent_ref.shape[0]):
        sent_ref[tile] = jnp.zeros((SUBLANES, LANES), F32)


def spread_kernel(parts_ref, out_ref):
    total = jnp.sum(parts_ref[...], axis=0)
    for n in range(out_ref.shape[0]):
        out_ref[n] = total


def unpack_kernel(
    sizes, tiles_ref, totals_ref, rel_ref, layer_ref, ment_ref, mquery_ref, score_ref, loss_ref
):
    relations, across = sizes
    width, hid = ment_ref.shape
    down = width // SUBLANES
    flat = jnp.concatenate(
        [
            jnp.concatenate([tiles_ref[row * across + tile] for tile in range(across)], axis=1)
            for row in range(down)
        ],
        axis=0,
    )
    rel_lanes = pad_to(relations, LANES)
    rel_ref[...] = flat[:, :relations]
    start = rel_lanes
    layer_ref[...] = flat[:, start : start + width]
    start += width
    ment_ref[...] = flat[:, start : start + hid]
    start += hid
    mquery_ref[...] = flat[:, start : start + hid]
    start += hid
    score_ref[...] = flat[0:1, start : start + hid]
    everyone = jnp.sum(totals_ref[...], axis=0)
    loss = everyone[2:3, :] + everyone[1:2, :] / everyone[0:1, :]
    loss_ref[...] = loss[:, : loss_ref.shape[1]]


def vmem(count):
    return [pl.BlockSpec(memory_space=pltpu.VMEM)] * count


def call(kernel, name, outs, flops, *operands, scratch=(), limit=40 << 20, far=(), alias=None):
    spaces = [pltpu.HBM if spot in far else pltpu.VMEM for spot in range(len(operands))]
    found = pl.pallas_call(
        kernel,
        out_shape=tuple(
            dims if isinstance(dims, jax.ShapeDtypeStruct) else jax.ShapeDtypeStruct(dims, F32)
            for dims in outs
        ),
        in_specs=[pl.BlockSpec(memory_space=space) for space in spaces],
        out_specs=tuple(pl.BlockSpec(memory_space=pltpu.VMEM) for _ in outs),
        scratch_shapes=scratch,
        input_output_aliases=alias or {},
        compiler_params=pltpu.CompilerParams(vmem_limit_bytes=limit),
        cost_estimate=pl.CostEstimate(flops=flops, bytes_accessed=1 << 20, transcendentals=0),
        name=name,
    )(*operands)
    return found[0] if len(outs) == 1 else found


def swap(values, axes):
    return lax.all_to_all(values, axes, split_axis=0, concat_axis=0, tiled=True)


def body(
    state_in,
    edge_src,
    edge_dst,
    edge_rel,
    edge_count,
    send_list,
    query_head,
    query_rel,
    pos_tail,
    neg_ids,
    rel_table,
    layer_weight,
    mlp_entity,
    mlp_query,
    score_weight,
):
    nodes = lax.axis_size("nodes")
    queries = lax.axis_size("queries")
    ent, width_all = state_in.shape
    relations, width = rel_table.shape
    hid = mlp_entity.shape[1]
    q_local = width_all // width
    edges = edge_src.shape[0]
    bound = send_list.shape[2]
    neg = neg_ids.shape[1]
    columns = q_local * neg + 2 * LANES
    chunk = min(512, edges)
    src_row = edge_src.reshape(1, edges)
    dst_row = edge_dst.reshape(1, edges)
    rel_row = edge_rel.reshape(1, edges)
    count = edge_count.reshape(1, 1)
    score_row = score_weight.reshape(1, hid)
    table_t = rel_table.T
    outgoing = call(
        send_kernel,
        "send",
        [(nodes, bound, width_all)],
        10**9,
        send_list[0],
        state_in,
        scratch=[
            pltpu.VMEM((nodes, bound), jnp.int32),
            pltpu.VMEM((ent, width_all), F32),
            pltpu.SemaphoreType.DMA((2,)),
        ],
        far=(0, 1),
        limit=SEND_LIMIT,
    )
    received = swap(outgoing, "nodes").reshape(nodes * bound, width_all)
    local, relation = call(
        functools.partial(early_kernel, (chunk,)),
        "early",
        [(width_all, edges), (width, edges)],
        4 * 10**9,
        state_in,
        src_row,
        rel_row,
        table_t,
    )
    new_state, source_t, summed, gate, cols, totals = call(
        functools.partial(forward_kernel, (chunk, q_local * queries)),
        "forward",
        [
            (ent, width_all),
            (width_all, edges),
            (width_all, ent),
            jax.ShapeDtypeStruct((width_all, ent), BF16),
            (width + hid + SUBLANES, columns),
            (nodes, SUBLANES, LANES),
        ],
        4 * 10**9,
        count,
        query_head.reshape(1, q_local),
        query_rel.reshape(1, q_local),
        pos_tail.reshape(1, q_local),
        state_in,
        received,
        src_row,
        dst_row,
        neg_ids,
        local,
        relation,
        table_t,
        layer_weight,
        mlp_entity,
        mlp_query,
        score_row,
        alias={9: 1},
    )
    all_totals = swap(totals, "nodes")
    rel_lanes = pad_to(relations, LANES)
    lanes = rel_lanes + pad_to(width + 3 * hid, LANES)
    across = lanes // LANES
    grads = call(
        functools.partial(backward_kernel, (chunk, relations, q_local, neg)),
        "backward",
        [((q_local + 1) * width, lanes)],
        4 * 10**9,
        count,
        source_t,
        dst_row,
        rel_row,
        layer_weight,
        mlp_entity,
        mlp_query,
        score_row,
        summed,
        gate,
        cols,
    )
    tiles = width // SUBLANES * across
    wide = nodes * queries
    group = wide if wide <= pad_to(tiles, nodes) else nodes
    held = pad_to(tiles, group)
    sent = call(
        functools.partial(combine_kernel, (q_local, width)),
        "combine",
        [(held, SUBLANES, LANES)],
        10**6,
        all_totals,
        totals,
        grads,
    )
    axes = ("nodes", "queries") if group == wide else "nodes"
    own = held // group
    parts = swap(sent, axes).reshape(group, own * SUBLANES, LANES)
    if group == wide:
        mine = call(spread_kernel, "spread", [(group, own * SUBLANES, LANES)], 10**6, parts)
    else:
        mine = lax.psum(jnp.sum(parts, axis=0), "queries")
        mine = jnp.broadcast_to(mine, (group,) + mine.shape)
    final = swap(mine, axes).reshape(held, SUBLANES, LANES)
    grad_rel, grad_layer, grad_entity, grad_query, grad_score, loss = call(
        functools.partial(unpack_kernel, (relations, across)),
        "unpack",
        [(width, relations), (width, width), (width, hid), (width, hid), (1, hid), (1, q_local)],
        10**6,
        final,
        all_totals,
    )
    return (
        new_state,
        loss.reshape(q_local),
        grad_rel.T,
        grad_layer,
        grad_entity,
        grad_query,
        grad_score.reshape(hid),
    )


def solution(mesh):
    in_specs = (
        P("nodes", "queries"),
        P("nodes"),
        P("nodes"),
        P("nodes"),
        P("nodes"),
        P("nodes", None, None),
        P("queries"),
        P("queries"),
        P("queries"),
        P("queries", "nodes"),
        P(),
        P(),
        P(),
        P(),
        P(),
    )
    out_specs = (P("nodes", "queries"), P("queries"), P(), P(), P(), P(), P())
    return jax.shard_map(body, mesh=mesh, in_specs=in_specs, out_specs=out_specs, check_vma=False)
```

```python
import functools

import jax
import jax.numpy as jnp
from jax import lax
from jax.experimental import pallas as pl
from jax.experimental.pallas import tpu as pltpu
from jax.sharding import PartitionSpec as P

adversarial = 0.5
HIGH = lax.Precision.HIGHEST
F32 = jnp.float32
BF16 = jnp.bfloat16
LANES = 128
SUBLANES = 8
FORWARD = 3
BACKWARD = 2
SEND_LIMIT = 64 << 20


def pad_to(count, unit):
    return -(-count // unit) * unit


def split(values, pieces, axis=0):
    found = []
    for _ in range(pieces):
        piece = values.astype(BF16)
        values = values - piece.astype(F32)
        found.append(piece)
    return jnp.concatenate(found, axis=axis)


def join(values, pieces, axis=0):
    size = values.shape[axis] // pieces
    parts = [
        lax.slice_in_dim(values, piece * size, (piece + 1) * size, axis=axis)
        for piece in range(pieces)
    ]
    return functools.reduce(jnp.add, parts)


def one_hot(index_row, rows):
    parts = []
    for base in range(0, rows, 256):
        size = min(256, rows - base)
        local = index_row - base
        key = jnp.where((local >= 0) & (local < size), local, -1).astype(F32).astype(BF16)
        spots = lax.broadcasted_iota(jnp.int32, (size, index_row.shape[1]), 0)
        same = spots.astype(F32).astype(BF16) == key
        parts.append(jnp.where(same, jnp.ones((), BF16), jnp.zeros((), BF16)))
    return parts[0] if len(parts) == 1 else jnp.concatenate(parts, axis=0)


def dot_nn(left, right, precision=None):
    return lax.dot_general(
        left, right, (((1,), (0,)), ((), ())), precision=precision, preferred_element_type=F32
    )


def dot_nt(left, right, precision=None):
    return lax.dot_general(
        left, right, (((1,), (1,)), ((), ())), precision=precision, preferred_element_type=F32
    )


def pieces_of(values, count):
    found = []
    for _ in range(count):
        piece = values.astype(BF16)
        values = values - piece.astype(F32)
        found.append(piece)
    return found


LEFT = {6: (0, 0, 1, 0, 2, 1), 3: (0, 0, 1)}
RIGHT = {6: (0, 1, 0, 2, 0, 1), 3: (0, 1, 0)}


def stack_left(values, terms, axis=1):
    pieces = pieces_of(values, max(LEFT[terms]) + 1)
    return jnp.concatenate([pieces[spot] for spot in LEFT[terms]], axis=axis)


def stack_right(values, terms, axis=0):
    pieces = pieces_of(values, max(RIGHT[terms]) + 1)
    return jnp.concatenate([pieces[spot] for spot in RIGHT[terms]], axis=axis)


def local_row(entity, ent_local):
    node = lax.axis_index("nodes")
    return jnp.where(entity // ent_local == node, entity % ent_local, -1)


def in_lanes(small_row):
    lane = lax.broadcasted_iota(jnp.int32, (1, LANES), 1)
    found = jnp.full((1, LANES), -1, jnp.int32)
    for spot in range(small_row.shape[1]):
        found = jnp.where(lane == spot, small_row[:, spot : spot + 1], found)
    return found


def as_column(row):
    size = row.shape[1]
    across = lax.broadcasted_iota(jnp.int32, (size, size), 1)
    down = lax.broadcasted_iota(jnp.int32, (size, size), 0)
    return jnp.sum(jnp.where(across == down, row, 0.0), axis=1, keepdims=True)


def as_row(column):
    size = column.shape[0]
    across = lax.broadcasted_iota(jnp.int32, (size, size), 1)
    down = lax.broadcasted_iota(jnp.int32, (size, size), 0)
    return jnp.sum(jnp.where(across == down, column, 0.0), axis=0, keepdims=True)


def fill_rows(rows, count):
    missing = count - len(rows)
    return jnp.concatenate(rows + [jnp.zeros((missing,) + rows[0].shape[1:], rows[0].dtype)], axis=0)


def kept_layout(q_local, ent, neg, parts=2):
    columns = q_local * neg + LANES
    ends = [0, q_local * ent] + [q_local * ent + (part + 1) * columns for part in range(1 + parts)]
    return [slice(low, high) for low, high in zip(ends, ends[1:])]


def send_kernel(send_ref, state_ref, out_ref):
    count, bound = send_ref.shape
    ent = state_ref.shape[0]
    pieces = split(state_ref[...], FORWARD, axis=1)
    wanted = send_ref[...].T
    entity = lax.broadcasted_iota(jnp.int32, (bound, ent), 1)
    for n in range(count):
        hot = (entity == wanted[:, n : n + 1]).astype(F32).astype(BF16)
        out_ref[n] = join(dot_nn(hot, pieces), FORWARD, axis=1)


def early_kernel(
    sizes,
    state_ref,
    src_ref,
    rel_ref,
    table_ref,
    head_ref,
    qrel_ref,
    tail_ref,
    layer_ref,
    ment_ref,
    mquery_ref,
    score_ref,
    local_ref,
    relation_ref,
    prep_ref,
    marks_ref,
):
    (chunk,) = sizes
    ent = state_ref.shape[0]
    width, relations = table_ref.shape
    hid = ment_ref.shape[1]
    edges = src_ref.shape[1]
    rel_rows = pad_to(relations, 16)
    state_bits = split(state_ref[...].T, FORWARD)
    rel_bits = split(table_ref[...], FORWARD)
    rel_bits = jnp.concatenate(
        [rel_bits, jnp.zeros((FORWARD * width, rel_rows - relations), BF16)], axis=1
    )
    for start in range(0, edges, chunk):
        span = slice(start, start + chunk)
        local_ref[:, span] = join(dot_nn(state_bits, one_hot(src_ref[:, span], ent)), FORWARD)
        relation_ref[:, span] = join(
            dot_nn(rel_bits, one_hot(rel_ref[:, span], rel_rows)), FORWARD
        )
    heads = in_lanes(local_row(head_ref[...], ent))
    tails = in_lanes(local_row(tail_ref[...], ent))
    qrels = in_lanes(qrel_ref[...])
    marks_ref[...] = fill_rows([heads, tails, qrels], SUBLANES)
    qvec = join(dot_nn(rel_bits, one_hot(qrels, rel_rows)), FORWARD)
    prep_ref[:width, :] = qvec
    prep_ref[width : width + hid, :] = dot_nn(mquery_ref[...].T, qvec, HIGH)
    prep_ref[width + hid :, :] = jnp.broadcast_to(as_column(score_ref[...]), (hid, LANES))


def forward_kernel(
    sizes,
    count_ref,
    state_ref,
    recv_ref,
    src_ref,
    dst_ref,
    neg_ref,
    local_ref,
    relation_ref,
    prep_ref,
    marks_ref,
    layer_ref,
    ment_ref,
    new_ref,
    srct_ref,
    kept_ref,
    gate_ref,
    coef_ref,
    totals_ref,
):
    chunk, queries_total = sizes
    ent, blocks = state_ref.shape
    edges = src_ref.shape[1]
    width, hid = ment_ref.shape
    q_local, neg = neg_ref.shape
    per_query = neg // LANES
    layout = kept_layout(q_local, ent, neg)
    recv_bits = split(recv_ref[...].T, FORWARD)
    live = count_ref[...]
    total = jnp.zeros((FORWARD * blocks, ent), F32)
    for start in range(0, edges, chunk):
        span = slice(start, start + chunk)
        far = one_hot(src_ref[:, span] - ent, recv_bits.shape[1])
        source = local_ref[:, span] + join(dot_nn(recv_bits, far), FORWARD)
        srct_ref[:, span] = source
        message = source * jnp.concatenate([relation_ref[:, span]] * q_local, axis=0)
        spot = lax.broadcasted_iota(jnp.int32, (1, chunk), 1) + start
        ends = jnp.where(spot < live, dst_ref[:, span], -1)
        total = total + dot_nt(split(message, FORWARD), one_hot(ends, ent))
    summed = join(total, FORWARD)

    entity_row = lax.broadcasted_iota(jnp.int32, (1, ent), 1)
    lane_row = lax.broadcasted_iota(jnp.int32, (1, LANES), 1)
    heads = marks_ref[0:1, :]
    tails = marks_ref[1:2, :]
    parts = []
    for q in range(q_local):
        at_head = (entity_row == heads[:, q : q + 1]).astype(F32)
        parts.append(summed[q * width : (q + 1) * width] + prep_ref[:width, q : q + 1] * at_head)
    wide = jnp.concatenate(parts, axis=1)
    kept_ref[:, layout[0]] = wide
    pre = dot_nn(stack_left(layer_ref[...].T, 6), stack_right(wide, 6))
    state_t = state_ref[...].T
    new_parts, picks, positive = [], [], None
    for q in range(q_local):
        rows = slice(q * width, (q + 1) * width)
        mine = pre[:, q * ent : (q + 1) * ent]
        gate_ref[rows, :] = (mine > 0.0).astype(F32).astype(BF16)
        new = state_t[rows] + jnp.maximum(mine, 0.0)
        new_parts.append(new)
        own_tail = jnp.where(lane_row == q, tails, -1)
        hot = one_hot(jnp.concatenate([neg_ref[q : q + 1, :], own_tail], axis=1), ent)
        picked = join(dot_nn(split(new, FORWARD), hot), FORWARD)
        picks.append(picked[:, :neg])
        last = picked[:, neg:]
        positive = last if positive is None else positive + last
    new_ref[...] = jnp.concatenate(new_parts, axis=0).T
    picked = jnp.concatenate(picks + [positive], axis=1)
    kept_ref[:, layout[1]] = picked
    plain = dot_nn(stack_left(ment_ref[...].T, 6), stack_right(picked, 6))
    rows = []
    for block in range(plain.shape[1] // LANES):
        span = slice(block * LANES, (block + 1) * LANES)
        q = block // per_query
        part = prep_ref[width : width + hid, :]
        if q < q_local:
            part = part[:, q : q + 1]
        hidden = plain[:, span] + part
        for part in range(hid // width):
            left = layout[2 + part].start + block * LANES
            kept_ref[:, left : left + LANES] = hidden[part * width : (part + 1) * width]
        weighted = jnp.maximum(hidden, 0.0) * prep_ref[width + hid :, :]
        rows.append(jnp.sum(weighted, axis=0, keepdims=True))
    height = coef_ref.shape[0]
    scores = fill_rows(rows, height)
    weights = jnp.exp(adversarial * scores)
    decay = jnp.exp(-jnp.abs(scores))
    near = jnp.log1p(decay)
    softplus = jnp.maximum(scores, 0.0) + near
    flipped = jnp.maximum(-scores, 0.0) + near
    share = 1.0 / (1.0 + decay)
    sigmoid = jnp.where(scores >= 0.0, share, decay * share)
    missing = jnp.where(scores >= 0.0, decay * share, share)
    row_total = jnp.sum(weights, axis=1, keepdims=True)
    row_weighted = jnp.sum(weights * softplus, axis=1, keepdims=True)
    present = (tails >= 0) & (lane_row < q_local)
    tail_row = len(rows) - 1
    positives = jnp.where(present, flipped[tail_row : tail_row + 1], 0.0)
    owns, weighteds, row_owns = [], [], []
    for q in range(q_local):
        mine = slice(q * per_query, (q + 1) * per_query)
        own = jnp.sum(row_total[mine], axis=0, keepdims=True)
        owns.append(own)
        row_owns.extend([own] * per_query)
        weighteds.append(jnp.sum(row_weighted[mine], axis=0, keepdims=True))
    row_own = fill_rows(row_owns, height)
    coef = weights * sigmoid / jnp.where(row_own > 0.0, row_own, 1.0)
    spot = lax.broadcasted_iota(jnp.int32, (height, LANES), 0)
    coef = jnp.where(spot < tail_row, coef, 0.0)
    coef = jnp.where((spot == tail_row) & present, -missing, coef)
    coef_ref[...] = coef * (1.0 / queries_total)
    tall = totals_ref.shape[1]
    pair = jnp.where(
        lax.broadcasted_iota(jnp.int32, (tall, LANES), 1) == 0,
        fill_rows(owns, tall),
        fill_rows(weighteds, tall),
    )
    down = lax.broadcasted_iota(jnp.int32, (tall, LANES), 0)
    tile = jnp.where(down == tall - 1, positives, pair)
    for n in range(totals_ref.shape[0]):
        totals_ref[n] = tile


def backward_kernel(
    sizes,
    count_ref,
    srct_ref,
    dst_ref,
    rel_ref,
    neg_ref,
    prep_ref,
    marks_ref,
    layer_ref,
    ment_ref,
    mquery_ref,
    kept_ref,
    gate_ref,
    coef_ref,
    out_ref,
):
    chunk, relations = sizes
    width, hid = ment_ref.shape
    blocks, ent = gate_ref.shape
    q_local, neg = neg_ref.shape
    edges = dst_ref.shape[1]
    layout = kept_layout(q_local, ent, neg)
    picked = kept_ref[:, layout[1]]
    hidden = jnp.concatenate([kept_ref[:, spot] for spot in layout[2:]], axis=0)
    per_query = neg // LANES
    rel_lanes = pad_to(relations, LANES)
    rel_rows = pad_to(relations, 16)
    heads = marks_ref[0:1, :]
    tails = marks_ref[1:2, :]
    qrels = marks_ref[2:3, :]
    entity_row = lax.broadcasted_iota(jnp.int32, (1, ent), 1)
    rel_row = lax.broadcasted_iota(jnp.int32, (1, rel_lanes), 1)
    grad_parts, coef_parts = [], []
    for block in range(hidden.shape[1] // LANES):
        span = slice(block * LANES, (block + 1) * LANES)
        coef = coef_ref[block : block + 1, :]
        coef_parts.append(coef)
        grad_parts.append(
            jnp.where(hidden[:, span] > 0.0, coef * prep_ref[width + hid :, :], 0.0)
        )
    grad_hidden = jnp.concatenate(grad_parts, axis=1)
    both = jnp.concatenate([ment_ref[...], mquery_ref[...]], axis=0)
    grad_both = dot_nn(stack_left(both, 3), stack_right(grad_hidden, 3))
    last = q_local * neg
    pres, tail_pres = [], []
    for q in range(q_local):
        rows = slice(q * width, (q + 1) * width)
        span = slice(q * neg, (q + 1) * neg)
        gate = gate_ref[rows, :].astype(F32)
        hot = one_hot(neg_ref[q : q + 1, :], ent)
        cube = join(dot_nt(split(grad_both[:width, span], BACKWARD), hot), BACKWARD)
        pres.append(gate * cube)
        at_tail = (entity_row == tails[:, q : q + 1]).astype(F32)
        tail_pres.append(gate * (grad_both[:width, last + q : last + q + 1] * at_tail))
    stacked = stack_right(jnp.concatenate(pres + tail_pres, axis=1), 3)
    sums = dot_nn(stack_left(layer_ref[...], 3), stacked)
    grad_sums = [sums[:, q * ent : (q + 1) * ent] for q in range(2 * q_local)]
    sum_bits = split(jnp.concatenate(grad_sums[:q_local], axis=0), BACKWARD)
    tail_columns = [
        jnp.sum(grad_sums[q_local + q], axis=1, keepdims=True) for q in range(q_local)
    ]

    live = count_ref[...]
    total = jnp.zeros((BACKWARD * (blocks + width), rel_rows), F32)
    for start in range(0, edges, chunk):
        span = slice(start, start + chunk)
        spot = lax.broadcasted_iota(jnp.int32, (1, chunk), 1) + start
        ends = jnp.where(spot < live, dst_ref[:, span], -2)
        source = srct_ref[:, span]
        upstream = join(dot_nn(sum_bits, one_hot(ends, ent)), BACKWARD)
        tail_terms = jnp.zeros((width, chunk), F32)
        for q in range(q_local):
            rows = slice(q * width, (q + 1) * width)
            hit = (ends == tails[:, q : q + 1]).astype(F32)
            tail_terms = tail_terms + (tail_columns[q] * hit) * source[rows]
        terms = jnp.concatenate([upstream * source, tail_terms], axis=0)
        total = total + dot_nt(split(terms, BACKWARD), one_hot(rel_ref[:, span], rel_rows))
    gathered = join(total, BACKWARD)
    if rel_lanes > rel_rows:
        gathered = jnp.concatenate(
            [gathered, jnp.zeros((blocks + width, rel_lanes - rel_rows), F32)], axis=1
        )

    seeds = []
    tail_seed = jnp.zeros((width, rel_lanes), F32)
    tail_layer = jnp.zeros((width, width), F32)
    spare = jnp.zeros((width, out_ref.shape[1] - rel_lanes - width - 3 * hid), F32)
    for block in range(q_local + 1):
        if block < q_local:
            q = block
            rows = slice(q * width, (q + 1) * width)
            span = slice(q * neg, (q + 1) * neg)
            at_head = (entity_row == heads[:, q : q + 1]).astype(F32)
            at_rel = (rel_row == qrels[:, q : q + 1]).astype(F32)
            grad_qvec = jnp.sum(grad_both[width:, span], axis=1, keepdims=True) + jnp.sum(
                grad_sums[q] * at_head, axis=1, keepdims=True
            )
            seeds.append(grad_qvec * at_rel)
            tail_qvec = grad_both[width:, last + q : last + q + 1] + jnp.sum(
                grad_sums[q_local + q] * at_head, axis=1, keepdims=True
            )
            tail_seed = tail_seed + tail_qvec * at_rel
            left = stack_left(kept_ref[:, q * ent : (q + 1) * ent], 3)
            right = jnp.concatenate(
                [stack_right(pres[q], 3, axis=1), stack_right(tail_pres[q], 3, axis=1)], axis=0
            )
            layers = dot_nt(left, right)
            layer_part = layers[:, :width]
            tail_layer = tail_layer + layers[:, width:]
            vectors = jnp.broadcast_to(prep_ref[:width, q : q + 1], (width, neg))
            coef_rows = coef_parts[q * per_query : (q + 1) * per_query]
        else:
            span = slice(last, last + LANES)
            layer_part = tail_layer
            vectors = prep_ref[:width, :]
            coef_rows = coef_parts[-1:]
        size = span.stop - span.start
        coef = jnp.broadcast_to(jnp.concatenate(coef_rows, axis=1), (width, size))
        right = jnp.concatenate([grad_hidden[:, span], jnp.maximum(hidden[:, span], 0.0)], axis=0)
        right = stack_right(right, 3, axis=1)
        entity_part = dot_nt(stack_left(picked[:, span], 3), right)[:, :hid]
        query_part = dot_nt(stack_left(vectors, 3), right)[:, :hid]
        score_part = dot_nt(stack_left(coef, 3), right)[:, hid:]
        rest = [layer_part, entity_part, query_part, score_part, spare]
        out_ref[block * width : (block + 1) * width, rel_lanes:] = jnp.concatenate(rest, axis=1)
    seeds.append(tail_seed)
    out_ref[:, :rel_lanes] = gathered + jnp.concatenate(seeds, axis=0)


def combine_kernel(sizes, totals_ref, grads_ref, sent_ref):
    q_local, width = sizes
    total = jnp.sum(totals_ref[...], axis=0)
    scale = totals_ref[lax.axis_index("nodes")] / total
    mixed = grads_ref[q_local * width :, :]
    for q in range(q_local):
        mixed = mixed + grads_ref[q * width : (q + 1) * width, :] * scale[q : q + 1, 0:1]
    across = mixed.shape[1] // LANES
    tiles = width // SUBLANES * across
    for tile in range(tiles):
        top, left = tile // across * SUBLANES, tile % across * LANES
        sent_ref[tile] = mixed[top : top + SUBLANES, left : left + LANES]
    for tile in range(tiles, sent_ref.shape[0]):
        sent_ref[tile] = jnp.zeros((SUBLANES, LANES), F32)


def spread_kernel(parts_ref, out_ref):
    total = jnp.sum(parts_ref[...], axis=0)
    for n in range(out_ref.shape[0]):
        out_ref[n] = total


def unpack_kernel(
    sizes, tiles_ref, totals_ref, rel_ref, layer_ref, ment_ref, mquery_ref, score_ref, loss_ref
):
    relations, across = sizes
    width, hid = ment_ref.shape
    down = width // SUBLANES
    flat = jnp.concatenate(
        [
            jnp.concatenate([tiles_ref[row * across + tile] for tile in range(across)], axis=1)
            for row in range(down)
        ],
        axis=0,
    )
    rel_lanes = pad_to(relations, LANES)
    rel_ref[...] = flat[:, :relations]
    start = rel_lanes
    layer_ref[...] = flat[:, start : start + width]
    start += width
    ment_ref[...] = flat[:, start : start + hid]
    start += hid
    mquery_ref[...] = flat[:, start : start + hid]
    start += hid
    score_ref[...] = flat[0:1, start : start + hid]
    everyone = jnp.sum(totals_ref[...], axis=0)
    count = loss_ref.shape[1]
    ratio = as_row(everyone[:count, 1:2] / everyone[:count, 0:1])
    loss_ref[...] = everyone[-1:, :count] + ratio


def call(kernel, name, outs, flops, *operands, scratch=(), limit=40 << 20, far=(), alias=None):
    spaces = [pltpu.HBM if spot in far else pltpu.VMEM for spot in range(len(operands))]
    found = pl.pallas_call(
        kernel,
        out_shape=tuple(
            dims if isinstance(dims, jax.ShapeDtypeStruct) else jax.ShapeDtypeStruct(dims, F32)
            for dims in outs
        ),
        in_specs=[pl.BlockSpec(memory_space=space) for space in spaces],
        out_specs=tuple(pl.BlockSpec(memory_space=pltpu.VMEM) for _ in outs),
        scratch_shapes=scratch,
        input_output_aliases=alias or {},
        compiler_params=pltpu.CompilerParams(vmem_limit_bytes=limit),
        cost_estimate=pl.CostEstimate(flops=flops, bytes_accessed=1 << 20, transcendentals=0),
        name=name,
    )(*operands)
    return found[0] if len(outs) == 1 else found


def swap(values, axes):
    return lax.all_to_all(values, axes, split_axis=0, concat_axis=0, tiled=True)


def body(
    state_in,
    edge_src,
    edge_dst,
    edge_rel,
    edge_count,
    send_list,
    query_head,
    query_rel,
    pos_tail,
    neg_ids,
    rel_table,
    layer_weight,
    mlp_entity,
    mlp_query,
    score_weight,
):
    nodes = lax.axis_size("nodes")
    queries = lax.axis_size("queries")
    ent, width_all = state_in.shape
    relations, width = rel_table.shape
    hid = mlp_entity.shape[1]
    q_local = width_all // width
    edges = edge_src.shape[0]
    bound = send_list.shape[2]
    neg = neg_ids.shape[1]
    columns = q_local * neg + LANES
    chunk = min(1024, edges)
    src_row = edge_src.reshape(1, edges)
    dst_row = edge_dst.reshape(1, edges)
    rel_row = edge_rel.reshape(1, edges)
    count = edge_count.reshape(1, 1)
    score_row = score_weight.reshape(1, hid)
    table_t = rel_table.T
    outgoing = call(
        send_kernel, "send", [(nodes, bound, width_all)], 10**9, send_list[0], state_in
    )
    received = swap(outgoing, "nodes").reshape(nodes * bound, width_all)
    local, relation, prep, marks = call(
        functools.partial(early_kernel, (chunk,)),
        "early",
        [
            (width_all, edges),
            (width, edges),
            (width + 2 * hid, LANES),
            jax.ShapeDtypeStruct((SUBLANES, LANES), jnp.int32),
        ],
        4 * 10**9,
        state_in,
        src_row,
        rel_row,
        table_t,
        query_head.reshape(1, q_local),
        query_rel.reshape(1, q_local),
        pos_tail.reshape(1, q_local),
        layer_weight,
        mlp_entity,
        mlp_query,
        score_row,
    )
    needed = kept_layout(q_local, ent, neg)[-1].stop
    new_state, source_t, kept, gate, coef, totals = call(
        functools.partial(forward_kernel, (chunk, q_local * queries)),
        "forward",
        [
            (ent, width_all),
            (width_all, edges),
            (width, max(needed, edges)),
            jax.ShapeDtypeStruct((width_all, ent), BF16),
            (pad_to(columns // LANES, SUBLANES), LANES),
            (nodes, pad_to(q_local + 1, SUBLANES), LANES),
        ],
        4 * 10**9,
        count,
        state_in,
        received,
        src_row,
        dst_row,
        neg_ids,
        local,
        relation,
        prep,
        marks,
        layer_weight,
        mlp_entity,
        alias={6: 1, 7: 2} if needed <= edges else {6: 1},
    )
    all_totals = swap(totals, "nodes")
    rel_lanes = pad_to(relations, LANES)
    lanes = rel_lanes + pad_to(width + 3 * hid, LANES)
    across = lanes // LANES
    grads = call(
        functools.partial(backward_kernel, (chunk, relations)),
        "backward",
        [((q_local + 1) * width, lanes)],
        4 * 10**9,
        count,
        source_t,
        dst_row,
        rel_row,
        neg_ids,
        prep,
        marks,
        layer_weight,
        mlp_entity,
        mlp_query,
        kept,
        gate,
        coef,
    )
    tiles = width // SUBLANES * across
    wide = nodes * queries
    group = wide if wide <= pad_to(tiles, nodes) else nodes
    held = pad_to(tiles, group)
    sent = call(
        functools.partial(combine_kernel, (q_local, width)),
        "combine",
        [(held, SUBLANES, LANES)],
        10**6,
        all_totals,
        grads,
    )
    axes = ("nodes", "queries") if group == wide else "nodes"
    own = held // group
    parts = swap(sent, axes).reshape(group, own * SUBLANES, LANES)
    if group == wide:
        mine = call(spread_kernel, "spread", [(group, own * SUBLANES, LANES)], 10**6, parts)
    else:
        mine = lax.psum(jnp.sum(parts, axis=0), "queries")
        mine = jnp.broadcast_to(mine, (group,) + mine.shape)
    final = swap(mine, axes).reshape(held, SUBLANES, LANES)
    grad_rel, grad_layer, grad_entity, grad_query, grad_score, loss = call(
        functools.partial(unpack_kernel, (relations, across)),
        "unpack",
        [(width, relations), (width, width), (width, hid), (width, hid), (1, hid), (1, q_local)],
        10**6,
        final,
        all_totals,
    )
    return (
        new_state,
        loss.reshape(q_local),
        grad_rel.T,
        grad_layer,
        grad_entity,
        grad_query,
        grad_score.reshape(hid),
    )


def solution(mesh):
    in_specs = (
        P("nodes", "queries"),
        P("nodes"),
        P("nodes"),
        P("nodes"),
        P("nodes"),
        P("nodes", None, None),
        P("queries"),
        P("queries"),
        P("queries"),
        P("queries", "nodes"),
        P(),
        P(),
        P(),
        P(),
        P(),
    )
    out_specs = (P("nodes", "queries"), P("queries"), P(), P(), P(), P(), P())
    return jax.shard_map(body, mesh=mesh, in_specs=in_specs, out_specs=out_specs, check_vma=False)
```

```python
import functools

import jax
import jax.numpy as jnp
from jax import lax
from jax.experimental import pallas as pl
from jax.experimental.pallas import tpu as pltpu
from jax.sharding import PartitionSpec as P

adversarial = 0.5
HIGH = lax.Precision.HIGHEST
F32 = jnp.float32
BF16 = jnp.bfloat16
LANES = 128
SUBLANES = 8
FORWARD = 3
BACKWARD = 2
SEND_LIMIT = 64 << 20


def pad_to(count, unit):
    return -(-count // unit) * unit


def split(values, pieces, axis=0):
    found = []
    for _ in range(pieces):
        piece = values.astype(BF16)
        values = values - piece.astype(F32)
        found.append(piece)
    return jnp.concatenate(found, axis=axis)


def join(values, pieces, axis=0):
    size = values.shape[axis] // pieces
    parts = [
        lax.slice_in_dim(values, piece * size, (piece + 1) * size, axis=axis)
        for piece in range(pieces)
    ]
    return functools.reduce(jnp.add, parts)


def one_hot(index_row, rows):
    parts = []
    for base in range(0, rows, 256):
        size = min(256, rows - base)
        local = index_row - base
        key = jnp.where((local >= 0) & (local < size), local, -1).astype(F32).astype(BF16)
        spots = lax.broadcasted_iota(jnp.int32, (size, index_row.shape[1]), 0)
        same = spots.astype(F32).astype(BF16) == key
        parts.append(jnp.where(same, jnp.ones((), BF16), jnp.zeros((), BF16)))
    return parts[0] if len(parts) == 1 else jnp.concatenate(parts, axis=0)


def dot_nn(left, right, precision=None):
    return lax.dot_general(
        left, right, (((1,), (0,)), ((), ())), precision=precision, preferred_element_type=F32
    )


def dot_nt(left, right, precision=None):
    return lax.dot_general(
        left, right, (((1,), (1,)), ((), ())), precision=precision, preferred_element_type=F32
    )


def pieces_of(values, count):
    found = []
    for _ in range(count):
        piece = values.astype(BF16)
        values = values - piece.astype(F32)
        found.append(piece)
    return found


LEFT = {6: (0, 0, 1, 0, 2, 1), 3: (0, 0, 1)}
RIGHT = {6: (0, 1, 0, 2, 0, 1), 3: (0, 1, 0)}


def stack_left(values, terms, axis=1):
    pieces = pieces_of(values, max(LEFT[terms]) + 1)
    return jnp.concatenate([pieces[spot] for spot in LEFT[terms]], axis=axis)


def stack_right(values, terms, axis=0):
    pieces = pieces_of(values, max(RIGHT[terms]) + 1)
    return jnp.concatenate([pieces[spot] for spot in RIGHT[terms]], axis=axis)


def pick_lanes(table, index_row, otherwise):
    rows, size = table.shape
    parts = []
    for left in range(0, index_row.shape[1], LANES):
        index = index_row[:, left : left + LANES]
        low = jnp.broadcast_to(index & (LANES - 1), (rows, LANES))
        tile = index >> (LANES.bit_length() - 1)
        found = otherwise[:, left : left + LANES]
        for spot in range(size // LANES):
            block = table[:, spot * LANES : (spot + 1) * LANES]
            taken = jnp.take_along_axis(block, low, axis=1, mode="promise_in_bounds")
            found = jnp.where(tile == spot, taken, found)
        parts.append(found)
    return jnp.concatenate(parts, axis=1)


def local_row(entity, ent_local):
    node = lax.axis_index("nodes")
    return jnp.where(entity // ent_local == node, entity % ent_local, -1)


def in_lanes(small_row):
    lane = lax.broadcasted_iota(jnp.int32, (1, LANES), 1)
    found = jnp.full((1, LANES), -1, jnp.int32)
    for spot in range(small_row.shape[1]):
        found = jnp.where(lane == spot, small_row[:, spot : spot + 1], found)
    return found


def as_column(row):
    size = row.shape[1]
    across = lax.broadcasted_iota(jnp.int32, (size, size), 1)
    down = lax.broadcasted_iota(jnp.int32, (size, size), 0)
    return jnp.sum(jnp.where(across == down, row, 0.0), axis=1, keepdims=True)


def as_row(column):
    size = column.shape[0]
    across = lax.broadcasted_iota(jnp.int32, (size, size), 1)
    down = lax.broadcasted_iota(jnp.int32, (size, size), 0)
    return jnp.sum(jnp.where(across == down, column, 0.0), axis=0, keepdims=True)


def fill_rows(rows, count):
    missing = count - len(rows)
    return jnp.concatenate(rows + [jnp.zeros((missing,) + rows[0].shape[1:], rows[0].dtype)], axis=0)


def kept_layout(q_local, ent, neg, parts=2):
    columns = q_local * neg + LANES
    ends = [0, q_local * ent] + [q_local * ent + (part + 1) * columns for part in range(1 + parts)]
    return [slice(low, high) for low, high in zip(ends, ends[1:])]


def tick_kernel(out_ref):
    out_ref[...] = jnp.zeros(out_ref.shape, F32)


def send_kernel(tick_ref, send_ref, state_ref, out_ref):
    count, bound = send_ref.shape
    ent = state_ref.shape[0]
    pieces = split(state_ref[...], FORWARD, axis=1)
    wanted = send_ref[...].T
    entity = lax.broadcasted_iota(jnp.int32, (bound, ent), 1)
    hot = [jnp.where(entity == wanted[:, n : n + 1], 1.0, 0.0).astype(BF16) for n in range(count)]
    rows = join(dot_nn(jnp.concatenate(hot, axis=0), pieces), FORWARD, axis=1)
    for n in range(count):
        out_ref[n] = rows[n * bound : (n + 1) * bound]


def early_kernel(
    sizes,
    state_ref,
    src_ref,
    rel_ref,
    table_ref,
    head_ref,
    qrel_ref,
    tail_ref,
    layer_ref,
    ment_ref,
    mquery_ref,
    score_ref,
    local_ref,
    relation_ref,
    prep_ref,
    marks_ref,
):
    (chunk,) = sizes
    ent = state_ref.shape[0]
    width, relations = table_ref.shape
    hid = ment_ref.shape[1]
    edges = src_ref.shape[1]
    rel_rows = pad_to(relations, 16)
    state_bits = split(state_ref[...].T, FORWARD)
    rel_bits = split(table_ref[...], FORWARD)
    rel_bits = jnp.concatenate(
        [rel_bits, jnp.zeros((FORWARD * width, rel_rows - relations), BF16)], axis=1
    )
    for start in range(0, edges, chunk):
        span = slice(start, start + chunk)
        local_ref[:, span] = join(dot_nn(state_bits, one_hot(src_ref[:, span], ent)), FORWARD)
        relation_ref[:, span] = join(
            dot_nn(rel_bits, one_hot(rel_ref[:, span], rel_rows)), FORWARD
        )
    heads = in_lanes(local_row(head_ref[...], ent))
    tails = in_lanes(local_row(tail_ref[...], ent))
    qrels = in_lanes(qrel_ref[...])
    marks_ref[...] = fill_rows([heads, tails, qrels], SUBLANES)
    qvec = join(dot_nn(rel_bits, one_hot(qrels, rel_rows)), FORWARD)
    prep_ref[:width, :] = qvec
    prep_ref[width : width + hid, :] = dot_nn(mquery_ref[...].T, qvec, HIGH)
    prep_ref[width + hid :, :] = jnp.broadcast_to(as_column(score_ref[...]), (hid, LANES))


def forward_kernel(
    sizes,
    count_ref,
    state_ref,
    recv_ref,
    src_ref,
    dst_ref,
    neg_ref,
    local_ref,
    relation_ref,
    prep_ref,
    marks_ref,
    layer_ref,
    ment_ref,
    new_ref,
    srct_ref,
    kept_ref,
    gate_ref,
    coef_ref,
    totals_ref,
):
    chunk, queries_total = sizes
    ent, blocks = state_ref.shape
    edges = src_ref.shape[1]
    width, hid = ment_ref.shape
    q_local, neg = neg_ref.shape
    per_query = neg // LANES
    layout = kept_layout(q_local, ent, neg)
    recv_t = recv_ref[...].T
    near = min(256, recv_t.shape[1])
    recv_bits = split(recv_t[:, near:], FORWARD)
    live = count_ref[...]
    total = jnp.zeros((FORWARD * blocks, ent), F32)
    def fetch(start):
        span = slice(start, start + chunk)
        slot = src_ref[:, span] - ent
        first = pick_lanes(recv_t[:, :near], slot, local_ref[:, span])
        return first, dot_nn(recv_bits, one_hot(slot - near, recv_bits.shape[1]))

    coming = fetch(0)
    for start in range(0, edges, chunk):
        span = slice(start, start + chunk)
        remote = coming
        if start + chunk < edges:
            coming = fetch(start + chunk)
        source = remote[0] + join(remote[1], FORWARD)
        srct_ref[:, span] = source
        message = source * jnp.concatenate([relation_ref[:, span]] * q_local, axis=0)
        spot = lax.broadcasted_iota(jnp.int32, (1, chunk), 1) + start
        ends = jnp.where(spot < live, dst_ref[:, span], -1)
        total = total + dot_nt(split(message, FORWARD), one_hot(ends, ent))
    summed = join(total, FORWARD)

    entity_row = lax.broadcasted_iota(jnp.int32, (1, ent), 1)
    lane_row = lax.broadcasted_iota(jnp.int32, (1, LANES), 1)
    heads = marks_ref[0:1, :]
    tails = marks_ref[1:2, :]
    parts = []
    for q in range(q_local):
        at_head = (entity_row == heads[:, q : q + 1]).astype(F32)
        parts.append(summed[q * width : (q + 1) * width] + prep_ref[:width, q : q + 1] * at_head)
    wide = jnp.concatenate(parts, axis=1)
    kept_ref[:, layout[0]] = wide
    pre = dot_nn(stack_left(layer_ref[...].T, 6), stack_right(wide, 6))
    state_t = state_ref[...].T
    new_parts, picks, positive = [], [], None
    for q in range(q_local):
        rows = slice(q * width, (q + 1) * width)
        mine = pre[:, q * ent : (q + 1) * ent]
        gate_ref[rows, :] = (mine > 0.0).astype(F32).astype(BF16)
        new = state_t[rows] + jnp.maximum(mine, 0.0)
        new_parts.append(new)
        own_tail = jnp.where(lane_row == q, tails, -1)
        picks.append(pick_lanes(new, neg_ref[q : q + 1, :], jnp.zeros((width, neg), F32)))
        last = pick_lanes(new, own_tail, jnp.zeros((width, LANES), F32))
        positive = last if positive is None else positive + last
    new_ref[...] = jnp.concatenate(new_parts, axis=0).T
    picked = jnp.concatenate(picks + [positive], axis=1)
    kept_ref[:, layout[1]] = picked
    plain = dot_nn(stack_left(ment_ref[...].T, 6), stack_right(picked, 6))
    rows = []
    for block in range(plain.shape[1] // LANES):
        span = slice(block * LANES, (block + 1) * LANES)
        q = block // per_query
        part = prep_ref[width : width + hid, :]
        if q < q_local:
            part = part[:, q : q + 1]
        hidden = plain[:, span] + part
        for part in range(hid // width):
            left = layout[2 + part].start + block * LANES
            kept_ref[:, left : left + LANES] = hidden[part * width : (part + 1) * width]
        weighted = jnp.maximum(hidden, 0.0) * prep_ref[width + hid :, :]
        rows.append(jnp.sum(weighted, axis=0, keepdims=True))
    height = coef_ref.shape[0]
    scores = fill_rows(rows, height)
    weights = jnp.exp(adversarial * scores)
    decay = jnp.exp(-jnp.abs(scores))
    near = jnp.log1p(decay)
    softplus = jnp.maximum(scores, 0.0) + near
    flipped = jnp.maximum(-scores, 0.0) + near
    share = 1.0 / (1.0 + decay)
    sigmoid = jnp.where(scores >= 0.0, share, decay * share)
    missing = jnp.where(scores >= 0.0, decay * share, share)
    row_total = jnp.sum(weights, axis=1, keepdims=True)
    row_weighted = jnp.sum(weights * softplus, axis=1, keepdims=True)
    present = (tails >= 0) & (lane_row < q_local)
    tail_row = len(rows) - 1
    positives = jnp.where(present, flipped[tail_row : tail_row + 1], 0.0)
    owns, weighteds, row_owns = [], [], []
    for q in range(q_local):
        mine = slice(q * per_query, (q + 1) * per_query)
        own = jnp.sum(row_total[mine], axis=0, keepdims=True)
        owns.append(own)
        row_owns.extend([own] * per_query)
        weighteds.append(jnp.sum(row_weighted[mine], axis=0, keepdims=True))
    row_own = fill_rows(row_owns, height)
    coef = weights * sigmoid / jnp.where(row_own > 0.0, row_own, 1.0)
    spot = lax.broadcasted_iota(jnp.int32, (height, LANES), 0)
    coef = jnp.where(spot < tail_row, coef, 0.0)
    coef = jnp.where((spot == tail_row) & present, -missing, coef)
    coef_ref[...] = coef * (1.0 / queries_total)
    tile = jnp.zeros((1, LANES), F32)
    for q in range(q_local):
        tile = jnp.where(lane_row == q, owns[q], tile)
        tile = jnp.where(lane_row == q_local + q, weighteds[q], tile)
        tile = jnp.where(lane_row == 2 * q_local + q, positives[:, q : q + 1], tile)
    for n in range(totals_ref.shape[0]):
        totals_ref[n] = tile


def backward_kernel(
    sizes,
    count_ref,
    srct_ref,
    dst_ref,
    rel_ref,
    neg_ref,
    prep_ref,
    marks_ref,
    layer_ref,
    ment_ref,
    mquery_ref,
    kept_ref,
    gate_ref,
    coef_ref,
    out_ref,
):
    chunk, relations = sizes
    width, hid = ment_ref.shape
    blocks, ent = gate_ref.shape
    q_local, neg = neg_ref.shape
    edges = dst_ref.shape[1]
    layout = kept_layout(q_local, ent, neg)
    picked = kept_ref[:, layout[1]]
    hidden = jnp.concatenate([kept_ref[:, spot] for spot in layout[2:]], axis=0)
    per_query = neg // LANES
    rel_lanes = pad_to(relations, LANES)
    rel_rows = pad_to(relations, 16)
    heads = marks_ref[0:1, :]
    tails = marks_ref[1:2, :]
    qrels = marks_ref[2:3, :]
    entity_row = lax.broadcasted_iota(jnp.int32, (1, ent), 1)
    rel_row = lax.broadcasted_iota(jnp.int32, (1, rel_lanes), 1)
    grad_parts, coef_parts = [], []
    for block in range(hidden.shape[1] // LANES):
        span = slice(block * LANES, (block + 1) * LANES)
        coef = coef_ref[block : block + 1, :]
        coef_parts.append(coef)
        grad_parts.append(
            jnp.where(hidden[:, span] > 0.0, coef * prep_ref[width + hid :, :], 0.0)
        )
    grad_hidden = jnp.concatenate(grad_parts, axis=1)
    both = jnp.concatenate([ment_ref[...], mquery_ref[...]], axis=0)
    grad_both = dot_nn(stack_left(both, 3), stack_right(grad_hidden, 3))
    last = q_local * neg
    pres, tail_pres = [], []
    for q in range(q_local):
        rows = slice(q * width, (q + 1) * width)
        span = slice(q * neg, (q + 1) * neg)
        gate = gate_ref[rows, :].astype(F32)
        hot = one_hot(neg_ref[q : q + 1, :], ent)
        cube = join(dot_nt(split(grad_both[:width, span], BACKWARD), hot), BACKWARD)
        pres.append(gate * cube)
        at_tail = (entity_row == tails[:, q : q + 1]).astype(F32)
        tail_pres.append(gate * (grad_both[:width, last + q : last + q + 1] * at_tail))
    stacked = stack_right(jnp.concatenate(pres + tail_pres, axis=1), 3)
    sums = dot_nn(stack_left(layer_ref[...], 3), stacked)
    grad_sums = [sums[:, q * ent : (q + 1) * ent] for q in range(2 * q_local)]
    sum_bits = split(jnp.concatenate(grad_sums[:q_local], axis=0), BACKWARD)
    tail_columns = [
        jnp.sum(grad_sums[q_local + q], axis=1, keepdims=True) for q in range(q_local)
    ]

    live = count_ref[...]

    def fetch(start):
        spot = lax.broadcasted_iota(jnp.int32, (1, chunk), 1) + start
        ends = jnp.where(spot < live, dst_ref[:, start : start + chunk], -2)
        return ends, dot_nn(sum_bits, one_hot(ends, ent))

    total = jnp.zeros((BACKWARD * (blocks + width), rel_rows), F32)
    coming = fetch(0)
    for start in range(0, edges, chunk):
        span = slice(start, start + chunk)
        ends, upstream = coming
        if start + chunk < edges:
            coming = fetch(start + chunk)
        source = srct_ref[:, span]
        tail_terms = jnp.zeros((width, chunk), F32)
        for q in range(q_local):
            rows = slice(q * width, (q + 1) * width)
            hit = (ends == tails[:, q : q + 1]).astype(F32)
            tail_terms = tail_terms + (tail_columns[q] * hit) * source[rows]
        terms = jnp.concatenate([join(upstream, BACKWARD) * source, tail_terms], axis=0)
        total = total + dot_nt(split(terms, BACKWARD), one_hot(rel_ref[:, span], rel_rows))
    gathered = join(total, BACKWARD)
    if rel_lanes > rel_rows:
        gathered = jnp.concatenate(
            [gathered, jnp.zeros((blocks + width, rel_lanes - rel_rows), F32)], axis=1
        )

    seeds = []
    tail_seed = jnp.zeros((width, rel_lanes), F32)
    tail_layer = jnp.zeros((width, width), F32)
    spare = jnp.zeros((width, out_ref.shape[1] - rel_lanes - width - 3 * hid), F32)
    for block in range(q_local + 1):
        if block < q_local:
            q = block
            rows = slice(q * width, (q + 1) * width)
            span = slice(q * neg, (q + 1) * neg)
            at_head = (entity_row == heads[:, q : q + 1]).astype(F32)
            at_rel = (rel_row == qrels[:, q : q + 1]).astype(F32)
            grad_qvec = jnp.sum(grad_both[width:, span], axis=1, keepdims=True) + jnp.sum(
                grad_sums[q] * at_head, axis=1, keepdims=True
            )
            seeds.append(grad_qvec * at_rel)
            tail_qvec = grad_both[width:, last + q : last + q + 1] + jnp.sum(
                grad_sums[q_local + q] * at_head, axis=1, keepdims=True
            )
            tail_seed = tail_seed + tail_qvec * at_rel
            left = stack_left(kept_ref[:, q * ent : (q + 1) * ent], 3)
            right = jnp.concatenate(
                [stack_right(pres[q], 3, axis=1), stack_right(tail_pres[q], 3, axis=1)], axis=0
            )
            layers = dot_nt(left, right)
            layer_part = layers[:, :width]
            tail_layer = tail_layer + layers[:, width:]
            vectors = prep_ref[:width, q : q + 1] + jnp.zeros((width, neg), F32)
            coef_rows = coef_parts[q * per_query : (q + 1) * per_query]
        else:
            span = slice(last, last + LANES)
            layer_part = tail_layer
            vectors = prep_ref[:width, :]
            coef_rows = coef_parts[-1:]
        size = span.stop - span.start
        coef = jnp.broadcast_to(jnp.concatenate(coef_rows, axis=1), (width, size))
        right = jnp.concatenate([grad_hidden[:, span], jnp.maximum(hidden[:, span], 0.0)], axis=0)
        left = jnp.concatenate([picked[:, span], vectors, coef], axis=0)
        products = dot_nt(stack_left(left, 3), stack_right(right, 3, axis=1))
        entity_part = products[:width, :hid]
        query_part = products[width : 2 * width, :hid]
        score_part = products[2 * width :, hid:]
        rest = [layer_part, entity_part, query_part, score_part, spare]
        out_ref[block * width : (block + 1) * width, rel_lanes:] = jnp.concatenate(rest, axis=1)
    seeds.append(tail_seed)
    out_ref[:, :rel_lanes] = gathered + jnp.concatenate(seeds, axis=0)


def combine_kernel(sizes, totals_ref, grads_ref, sent_ref):
    q_local, width = sizes
    total = jnp.sum(totals_ref[...], axis=0)
    scale = totals_ref[lax.axis_index("nodes")] / total
    mixed = grads_ref[q_local * width :, :]
    for q in range(q_local):
        mixed = mixed + grads_ref[q * width : (q + 1) * width, :] * scale[:, q : q + 1]
    across = mixed.shape[1] // LANES
    tiles = width // SUBLANES * across
    for tile in range(tiles):
        top, left = tile // across * SUBLANES, tile % across * LANES
        sent_ref[tile] = mixed[top : top + SUBLANES, left : left + LANES]
    for tile in range(tiles, sent_ref.shape[0]):
        sent_ref[tile] = jnp.zeros((SUBLANES, LANES), F32)


def spread_kernel(parts_ref, out_ref):
    total = jnp.sum(parts_ref[...], axis=0)
    for n in range(out_ref.shape[0]):
        out_ref[n] = total


def unpack_kernel(
    sizes, tiles_ref, totals_ref, rel_ref, layer_ref, ment_ref, mquery_ref, score_ref, loss_ref
):
    relations, across = sizes
    width, hid = ment_ref.shape
    down = width // SUBLANES
    flat = jnp.concatenate(
        [
            jnp.concatenate([tiles_ref[row * across + tile] for tile in range(across)], axis=1)
            for row in range(down)
        ],
        axis=0,
    )
    rel_lanes = pad_to(relations, LANES)
    rel_ref[...] = flat[:, :relations]
    start = rel_lanes
    layer_ref[...] = flat[:, start : start + width]
    start += width
    ment_ref[...] = flat[:, start : start + hid]
    start += hid
    mquery_ref[...] = flat[:, start : start + hid]
    start += hid
    score_ref[...] = flat[0:1, start : start + hid]
    everyone = jnp.sum(totals_ref[...], axis=0)
    count = loss_ref.shape[1]
    ratio = everyone[:, count : 2 * count] / everyone[:, :count]
    loss_ref[...] = everyone[:, 2 * count : 3 * count] + ratio


def call(kernel, name, outs, flops, *operands, scratch=(), limit=40 << 20, far=(), alias=None):
    spaces = [pltpu.HBM if spot in far else pltpu.VMEM for spot in range(len(operands))]
    found = pl.pallas_call(
        kernel,
        out_shape=tuple(
            dims if isinstance(dims, jax.ShapeDtypeStruct) else jax.ShapeDtypeStruct(dims, F32)
            for dims in outs
        ),
        in_specs=[pl.BlockSpec(memory_space=space) for space in spaces],
        out_specs=tuple(pl.BlockSpec(memory_space=pltpu.VMEM) for _ in outs),
        scratch_shapes=scratch,
        input_output_aliases=alias or {},
        compiler_params=pltpu.CompilerParams(vmem_limit_bytes=limit),
        cost_estimate=pl.CostEstimate(flops=flops, bytes_accessed=1 << 20, transcendentals=0),
        name=name,
    )(*operands)
    return found[0] if len(outs) == 1 else found


def swap(values, axes):
    return lax.all_to_all(values, axes, split_axis=0, concat_axis=0, tiled=True)


def body(
    state_in,
    edge_src,
    edge_dst,
    edge_rel,
    edge_count,
    send_list,
    query_head,
    query_rel,
    pos_tail,
    neg_ids,
    rel_table,
    layer_weight,
    mlp_entity,
    mlp_query,
    score_weight,
):
    nodes = lax.axis_size("nodes")
    queries = lax.axis_size("queries")
    ent, width_all = state_in.shape
    relations, width = rel_table.shape
    hid = mlp_entity.shape[1]
    q_local = width_all // width
    edges = edge_src.shape[0]
    bound = send_list.shape[2]
    neg = neg_ids.shape[1]
    columns = q_local * neg + LANES
    chunk = min(512, edges)
    src_row = edge_src.reshape(1, edges)
    dst_row = edge_dst.reshape(1, edges)
    rel_row = edge_rel.reshape(1, edges)
    count = edge_count.reshape(1, 1)
    score_row = score_weight.reshape(1, hid)
    table_t = rel_table.T
    tick = call(tick_kernel, "tick", [(SUBLANES, LANES)], 10**10)
    outgoing = call(
        send_kernel, "send", [(nodes, bound, width_all)], 10**9, tick, send_list[0], state_in
    )
    received = swap(outgoing, "nodes").reshape(nodes * bound, width_all)
    local, relation, prep, marks = call(
        functools.partial(early_kernel, (chunk,)),
        "early",
        [
            (width_all, edges),
            (width, edges),
            (width + 2 * hid, LANES),
            jax.ShapeDtypeStruct((SUBLANES, LANES), jnp.int32),
        ],
        4 * 10**9,
        state_in,
        src_row,
        rel_row,
        table_t,
        query_head.reshape(1, q_local),
        query_rel.reshape(1, q_local),
        pos_tail.reshape(1, q_local),
        layer_weight,
        mlp_entity,
        mlp_query,
        score_row,
    )
    needed = kept_layout(q_local, ent, neg)[-1].stop
    new_state, source_t, kept, gate, coef, totals = call(
        functools.partial(forward_kernel, (chunk, q_local * queries)),
        "forward",
        [
            (ent, width_all),
            (width_all, edges),
            (width, max(needed, edges)),
            jax.ShapeDtypeStruct((width_all, ent), BF16),
            (pad_to(columns // LANES, SUBLANES), LANES),
            (nodes, 1, LANES),
        ],
        4 * 10**9,
        count,
        state_in,
        received,
        src_row,
        dst_row,
        neg_ids,
        local,
        relation,
        prep,
        marks,
        layer_weight,
        mlp_entity,
        alias={6: 1, 7: 2} if needed <= edges else {6: 1},
    )
    all_totals = swap(totals, "nodes")
    rel_lanes = pad_to(relations, LANES)
    lanes = rel_lanes + pad_to(width + 3 * hid, LANES)
    across = lanes // LANES
    grads = call(
        functools.partial(backward_kernel, (chunk, relations)),
        "backward",
        [((q_local + 1) * width, lanes)],
        4 * 10**9,
        count,
        source_t,
        dst_row,
        rel_row,
        neg_ids,
        prep,
        marks,
        layer_weight,
        mlp_entity,
        mlp_query,
        kept,
        gate,
        coef,
    )
    tiles = width // SUBLANES * across
    wide = nodes * queries
    group = wide if wide <= pad_to(tiles, nodes) else nodes
    held = pad_to(tiles, group)
    sent = call(
        functools.partial(combine_kernel, (q_local, width)),
        "combine",
        [(held, SUBLANES, LANES)],
        10**6,
        all_totals,
        grads,
    )
    axes = ("nodes", "queries") if group == wide else "nodes"
    own = held // group
    parts = swap(sent, axes).reshape(group, own * SUBLANES, LANES)
    if group == wide:
        mine = call(spread_kernel, "spread", [(group, own * SUBLANES, LANES)], 10**6, parts)
    else:
        mine = lax.psum(jnp.sum(parts, axis=0), "queries")
        mine = jnp.broadcast_to(mine, (group,) + mine.shape)
    final = swap(mine, axes).reshape(held, SUBLANES, LANES)
    grad_rel, grad_layer, grad_entity, grad_query, grad_score, loss = call(
        functools.partial(unpack_kernel, (relations, across)),
        "unpack",
        [(width, relations), (width, width), (width, hid), (width, hid), (1, hid), (1, q_local)],
        10**6,
        final,
        all_totals,
    )
    return (
        new_state,
        loss.reshape(q_local),
        grad_rel.T,
        grad_layer,
        grad_entity,
        grad_query,
        grad_score.reshape(hid),
    )


def solution(mesh):
    in_specs = (
        P("nodes", "queries"),
        P("nodes"),
        P("nodes"),
        P("nodes"),
        P("nodes"),
        P("nodes", None, None),
        P("queries"),
        P("queries"),
        P("queries"),
        P("queries", "nodes"),
        P(),
        P(),
        P(),
        P(),
        P(),
    )
    out_specs = (P("nodes", "queries"), P("queries"), P(), P(), P(), P(), P())
    return jax.shard_map(body, mesh=mesh, in_specs=in_specs, out_specs=out_specs, check_vma=False)
```

```python
import functools

import jax
import jax.numpy as jnp
from jax import lax
from jax.experimental import pallas as pl
from jax.experimental.pallas import tpu as pltpu
from jax.sharding import PartitionSpec as P

adversarial = 0.5
HIGH = lax.Precision.HIGHEST
F32 = jnp.float32
BF16 = jnp.bfloat16
LANES = 128
SUBLANES = 8
FORWARD = 3
BACKWARD = 2


def pad_to(count, unit):
    return -(-count // unit) * unit


def split(values, pieces, axis=0):
    found = []
    for _ in range(pieces):
        piece = values.astype(BF16)
        values = values - piece.astype(F32)
        found.append(piece)
    return jnp.concatenate(found, axis=axis)


def join(values, pieces, axis=0):
    size = values.shape[axis] // pieces
    parts = [
        lax.slice_in_dim(values, piece * size, (piece + 1) * size, axis=axis)
        for piece in range(pieces)
    ]
    return functools.reduce(jnp.add, parts)


def one_hot(index_row, rows):
    parts = []
    for base in range(0, rows, 256):
        size = min(256, rows - base)
        local = index_row - base
        key = jnp.where((local >= 0) & (local < size), local, -1).astype(F32).astype(BF16)
        spots = lax.broadcasted_iota(jnp.int32, (size, index_row.shape[1]), 0)
        same = spots.astype(F32).astype(BF16) == key
        parts.append(jnp.where(same, jnp.ones((), BF16), jnp.zeros((), BF16)))
    return parts[0] if len(parts) == 1 else jnp.concatenate(parts, axis=0)


def dot_nn(left, right, precision=None):
    return lax.dot_general(
        left, right, (((1,), (0,)), ((), ())), precision=precision, preferred_element_type=F32
    )


def dot_nt(left, right, precision=None):
    return lax.dot_general(
        left, right, (((1,), (1,)), ((), ())), precision=precision, preferred_element_type=F32
    )


def pieces_of(values, count):
    found = []
    for _ in range(count):
        piece = values.astype(BF16)
        values = values - piece.astype(F32)
        found.append(piece)
    return found


LEFT = {6: (0, 0, 1, 0, 2, 1), 3: (0, 0, 1)}
RIGHT = {6: (0, 1, 0, 2, 0, 1), 3: (0, 1, 0)}


def stack_left(values, terms, axis=1):
    pieces = pieces_of(values, max(LEFT[terms]) + 1)
    return jnp.concatenate([pieces[spot] for spot in LEFT[terms]], axis=axis)


def stack_right(values, terms, axis=0):
    pieces = pieces_of(values, max(RIGHT[terms]) + 1)
    return jnp.concatenate([pieces[spot] for spot in RIGHT[terms]], axis=axis)


def pick_lanes(table, index_row, otherwise):
    rows, size = table.shape
    parts = []
    for left in range(0, index_row.shape[1], LANES):
        index = index_row[:, left : left + LANES]
        low = jnp.broadcast_to(index & (LANES - 1), (rows, LANES))
        tile = index >> (LANES.bit_length() - 1)
        found = otherwise[:, left : left + LANES]
        for spot in range(size // LANES):
            block = table[:, spot * LANES : (spot + 1) * LANES]
            taken = jnp.take_along_axis(block, low, axis=1, mode="promise_in_bounds")
            found = jnp.where(tile == spot, taken, found)
        parts.append(found)
    return jnp.concatenate(parts, axis=1)


def local_row(entity, ent_local):
    node = lax.axis_index("nodes")
    return jnp.where(entity // ent_local == node, entity % ent_local, -1)


def in_lanes(small_row):
    lane = lax.broadcasted_iota(jnp.int32, (1, LANES), 1)
    found = jnp.full((1, LANES), -1, jnp.int32)
    for spot in range(small_row.shape[1]):
        found = jnp.where(lane == spot, small_row[:, spot : spot + 1], found)
    return found


def as_column(row):
    size = row.shape[1]
    across = lax.broadcasted_iota(jnp.int32, (size, size), 1)
    down = lax.broadcasted_iota(jnp.int32, (size, size), 0)
    return jnp.sum(jnp.where(across == down, row, 0.0), axis=1, keepdims=True)


def as_row(column):
    size = column.shape[0]
    across = lax.broadcasted_iota(jnp.int32, (size, size), 1)
    down = lax.broadcasted_iota(jnp.int32, (size, size), 0)
    return jnp.sum(jnp.where(across == down, column, 0.0), axis=0, keepdims=True)


def fill_rows(rows, count):
    missing = count - len(rows)
    return jnp.concatenate(rows + [jnp.zeros((missing,) + rows[0].shape[1:], rows[0].dtype)], axis=0)


def kept_layout(q_local, ent, neg, parts=2):
    columns = q_local * neg + LANES
    ends = [0]
    for size in [q_local * ent] + [columns] * (1 + parts) + [q_local * ent]:
        ends.append(ends[-1] + size)
    return [slice(low, high) for low, high in zip(ends, ends[1:])]


def tick_kernel(out_ref):
    out_ref[...] = jnp.zeros(out_ref.shape, F32)


def send_kernel(tick_ref, send_ref, state_ref, out_ref):
    count, bound = send_ref.shape
    ent = state_ref.shape[0]
    pieces = split(state_ref[...], FORWARD, axis=1)
    wanted = send_ref[...].T
    entity = lax.broadcasted_iota(jnp.int32, (bound, ent), 1)
    hot = [jnp.where(entity == wanted[:, n : n + 1], 1.0, 0.0).astype(BF16) for n in range(count)]
    rows = join(dot_nn(jnp.concatenate(hot, axis=0), pieces), FORWARD, axis=1)
    for n in range(count):
        out_ref[n] = rows[n * bound : (n + 1) * bound]


def early_kernel(
    sizes,
    state_ref,
    src_ref,
    rel_ref,
    table_ref,
    head_ref,
    qrel_ref,
    tail_ref,
    layer_ref,
    ment_ref,
    mquery_ref,
    score_ref,
    local_ref,
    relation_ref,
    prep_ref,
    marks_ref,
):
    (chunk,) = sizes
    ent = state_ref.shape[0]
    width, relations = table_ref.shape
    hid = ment_ref.shape[1]
    edges = src_ref.shape[1]
    rel_rows = pad_to(relations, 16)
    state_bits = split(state_ref[...].T, FORWARD)
    rel_bits = split(table_ref[...], FORWARD)
    rel_bits = jnp.concatenate(
        [rel_bits, jnp.zeros((FORWARD * width, rel_rows - relations), BF16)], axis=1
    )
    for start in range(0, edges, chunk):
        span = slice(start, start + chunk)
        local_ref[:, span] = join(dot_nn(state_bits, one_hot(src_ref[:, span], ent)), FORWARD)
        relation_ref[:, span] = join(
            dot_nn(rel_bits, one_hot(rel_ref[:, span], rel_rows)), FORWARD
        )
    heads = in_lanes(local_row(head_ref[...], ent))
    tails = in_lanes(local_row(tail_ref[...], ent))
    qrels = in_lanes(qrel_ref[...])
    marks_ref[...] = fill_rows([heads, tails, qrels], SUBLANES)
    qvec = join(dot_nn(rel_bits, one_hot(qrels, rel_rows)), FORWARD)
    prep_ref[:width, :] = qvec
    prep_ref[width : width + hid, :] = dot_nn(mquery_ref[...].T, qvec, HIGH)
    prep_ref[width + hid :, :] = jnp.broadcast_to(as_column(score_ref[...]), (hid, LANES))


def forward_kernel(
    sizes,
    count_ref,
    state_ref,
    recv_ref,
    src_ref,
    dst_ref,
    neg_ref,
    local_ref,
    relation_ref,
    prep_ref,
    marks_ref,
    layer_ref,
    ment_ref,
    srct_ref,
    kept_ref,
    gate_ref,
    coef_ref,
    totals_ref,
):
    (chunk,) = sizes
    ent, blocks = state_ref.shape
    edges = src_ref.shape[1]
    width, hid = ment_ref.shape
    q_local, neg = neg_ref.shape
    per_query = neg // LANES
    layout = kept_layout(q_local, ent, neg)
    recv_t = recv_ref[...].T
    near = min(256, recv_t.shape[1])
    recv_bits = split(recv_t[:, near:], FORWARD)
    live = count_ref[...]
    total = jnp.zeros((FORWARD * blocks, ent), F32)
    def fetch(start):
        span = slice(start, start + chunk)
        slot = src_ref[:, span] - ent
        first = pick_lanes(recv_t[:, :near], slot, local_ref[:, span])
        return first, dot_nn(recv_bits, one_hot(slot - near, recv_bits.shape[1]))

    coming = fetch(0)
    for start in range(0, edges, chunk):
        span = slice(start, start + chunk)
        remote = coming
        if start + chunk < edges:
            coming = fetch(start + chunk)
        source = remote[0] + join(remote[1], FORWARD)
        srct_ref[:, span] = source
        message = source * jnp.concatenate([relation_ref[:, span]] * q_local, axis=0)
        spot = lax.broadcasted_iota(jnp.int32, (1, chunk), 1) + start
        ends = jnp.where(spot < live, dst_ref[:, span], -1)
        total = total + dot_nt(split(message, FORWARD), one_hot(ends, ent))
    summed = join(total, FORWARD)

    entity_row = lax.broadcasted_iota(jnp.int32, (1, ent), 1)
    lane_row = lax.broadcasted_iota(jnp.int32, (1, LANES), 1)
    heads = marks_ref[0:1, :]
    tails = marks_ref[1:2, :]
    parts = []
    for q in range(q_local):
        at_head = (entity_row == heads[:, q : q + 1]).astype(F32)
        parts.append(summed[q * width : (q + 1) * width] + prep_ref[:width, q : q + 1] * at_head)
    wide = jnp.concatenate(parts, axis=1)
    kept_ref[:, layout[0]] = wide
    pre = dot_nn(stack_left(layer_ref[...].T, 6), stack_right(wide, 6))
    state_t = state_ref[...].T
    new_parts, picks, positive = [], [], None
    for q in range(q_local):
        rows = slice(q * width, (q + 1) * width)
        mine = pre[:, q * ent : (q + 1) * ent]
        gate_ref[rows, :] = (mine > 0.0).astype(F32).astype(BF16)
        new = state_t[rows] + jnp.maximum(mine, 0.0)
        new_parts.append(new)
        own_tail = jnp.where(lane_row == q, tails, -1)
        picks.append(pick_lanes(new, neg_ref[q : q + 1, :], jnp.zeros((width, neg), F32)))
        last = pick_lanes(new, own_tail, jnp.zeros((width, LANES), F32))
        positive = last if positive is None else positive + last
    kept_ref[:, layout[-1]] = jnp.concatenate(new_parts, axis=1)
    picked = jnp.concatenate(picks + [positive], axis=1)
    kept_ref[:, layout[1]] = picked
    plain = dot_nn(stack_left(ment_ref[...].T, 6), stack_right(picked, 6))
    rows = []
    for block in range(plain.shape[1] // LANES):
        span = slice(block * LANES, (block + 1) * LANES)
        q = block // per_query
        part = prep_ref[width : width + hid, :]
        if q < q_local:
            part = part[:, q : q + 1]
        hidden = plain[:, span] + part
        for part in range(hid // width):
            left = layout[2 + part].start + block * LANES
            kept_ref[:, left : left + LANES] = hidden[part * width : (part + 1) * width]
        weighted = jnp.maximum(hidden, 0.0) * prep_ref[width + hid :, :]
        rows.append(jnp.sum(weighted, axis=0, keepdims=True))
    height = coef_ref.shape[0] // 2
    scores = fill_rows(rows, height)
    weights = jnp.exp(adversarial * scores)
    near_zero = jnp.log1p(jnp.exp(-jnp.abs(scores)))
    softplus = jnp.maximum(scores, 0.0) + near_zero
    flipped = jnp.maximum(-scores, 0.0) + near_zero
    row_total = jnp.sum(weights, axis=1, keepdims=True)
    row_weighted = jnp.sum(weights * softplus, axis=1, keepdims=True)
    tail_row = len(rows) - 1
    positives = jnp.where(tails >= 0, flipped[tail_row : tail_row + 1], 0.0)
    owns, weighteds, row_owns = [], [], []
    for q in range(q_local):
        mine = slice(q * per_query, (q + 1) * per_query)
        own = jnp.sum(row_total[mine], axis=0, keepdims=True)
        owns.append(own)
        row_owns.extend([own] * per_query)
        weighteds.append(jnp.sum(row_weighted[mine], axis=0, keepdims=True))
    coef_ref[:height, :] = scores
    coef_ref[height:, :] = jnp.broadcast_to(fill_rows(row_owns, height), (height, LANES))
    tile = jnp.zeros((1, LANES), F32)
    for q in range(q_local):
        tile = jnp.where(lane_row == q, owns[q], tile)
        tile = jnp.where(lane_row == q_local + q, weighteds[q], tile)
        tile = jnp.where(lane_row == 2 * q_local + q, positives[:, q : q + 1], tile)
    for n in range(totals_ref.shape[0]):
        totals_ref[n] = tile


def backward_kernel(
    sizes,
    count_ref,
    srct_ref,
    dst_ref,
    rel_ref,
    neg_ref,
    prep_ref,
    marks_ref,
    layer_ref,
    ment_ref,
    mquery_ref,
    kept_ref,
    gate_ref,
    coef_ref,
    out_ref,
    new_hbm,
    new_ref,
    sems,
):
    chunk, relations, queries_total = sizes
    width, hid = ment_ref.shape
    blocks, ent = gate_ref.shape
    q_local, neg = neg_ref.shape
    edges = dst_ref.shape[1]
    layout = kept_layout(q_local, ent, neg)
    first = layout[-1].start
    new_parts = [kept_ref[:, first + q * ent : first + (q + 1) * ent] for q in range(q_local)]
    new_ref[...] = jnp.concatenate(new_parts, axis=0).T
    new_copy = pltpu.make_async_copy(new_ref, new_hbm, sems.at[0])
    new_copy.start()
    picked = kept_ref[:, layout[1]]
    hidden = jnp.concatenate([kept_ref[:, spot] for spot in layout[2:-1]], axis=0)
    per_query = neg // LANES
    rel_lanes = pad_to(relations, LANES)
    rel_rows = pad_to(relations, 16)
    heads = marks_ref[0:1, :]
    tails = marks_ref[1:2, :]
    qrels = marks_ref[2:3, :]
    entity_row = lax.broadcasted_iota(jnp.int32, (1, ent), 1)
    rel_row = lax.broadcasted_iota(jnp.int32, (1, rel_lanes), 1)
    height = coef_ref.shape[0] // 2
    scores, row_own = coef_ref[:height, :], coef_ref[height:, :]
    decay = jnp.exp(-jnp.abs(scores))
    share = 1.0 / (1.0 + decay)
    sigmoid = jnp.where(scores >= 0.0, share, decay * share)
    missing = jnp.where(scores >= 0.0, decay * share, share)
    weights = jnp.exp(adversarial * scores)
    coefs = weights * sigmoid / jnp.where(row_own > 0.0, row_own, 1.0)
    spot = lax.broadcasted_iota(jnp.int32, (height, LANES), 0)
    tail_row = hidden.shape[1] // LANES - 1
    coefs = jnp.where(spot < tail_row, coefs, 0.0)
    coefs = jnp.where((spot == tail_row) & (tails >= 0), -missing, coefs) * (1.0 / queries_total)
    grad_parts, coef_parts = [], []
    for block in range(hidden.shape[1] // LANES):
        span = slice(block * LANES, (block + 1) * LANES)
        coef = coefs[block : block + 1, :]
        coef_parts.append(coef)
        grad_parts.append(
            jnp.where(hidden[:, span] > 0.0, coef * prep_ref[width + hid :, :], 0.0)
        )
    grad_hidden = jnp.concatenate(grad_parts, axis=1)
    both = jnp.concatenate([ment_ref[...], mquery_ref[...]], axis=0)
    grad_both = dot_nn(stack_left(both, 3), stack_right(grad_hidden, 3))
    last = q_local * neg
    pres, tail_pres = [], []
    for q in range(q_local):
        rows = slice(q * width, (q + 1) * width)
        span = slice(q * neg, (q + 1) * neg)
        gate = gate_ref[rows, :].astype(F32)
        hot = one_hot(neg_ref[q : q + 1, :], ent)
        cube = join(dot_nt(split(grad_both[:width, span], BACKWARD), hot), BACKWARD)
        pres.append(gate * cube)
        at_tail = (entity_row == tails[:, q : q + 1]).astype(F32)
        tail_pres.append(gate * (grad_both[:width, last + q : last + q + 1] * at_tail))
    stacked = stack_right(jnp.concatenate(pres + tail_pres, axis=1), 3)
    sums = dot_nn(stack_left(layer_ref[...], 3), stacked)
    grad_sums = [sums[:, q * ent : (q + 1) * ent] for q in range(2 * q_local)]
    sum_bits = split(jnp.concatenate(grad_sums[:q_local], axis=0), BACKWARD)
    tail_columns = [
        jnp.sum(grad_sums[q_local + q], axis=1, keepdims=True) for q in range(q_local)
    ]

    live = count_ref[...]

    def fetch(start):
        spot = lax.broadcasted_iota(jnp.int32, (1, chunk), 1) + start
        ends = jnp.where(spot < live, dst_ref[:, start : start + chunk], -2)
        return ends, dot_nn(sum_bits, one_hot(ends, ent))

    total = jnp.zeros((BACKWARD * (blocks + width), rel_rows), F32)
    coming = fetch(0)
    for start in range(0, edges, chunk):
        span = slice(start, start + chunk)
        ends, upstream = coming
        if start + chunk < edges:
            coming = fetch(start + chunk)
        source = srct_ref[:, span]
        tail_terms = jnp.zeros((width, chunk), F32)
        for q in range(q_local):
            rows = slice(q * width, (q + 1) * width)
            hit = (ends == tails[:, q : q + 1]).astype(F32)
            tail_terms = tail_terms + (tail_columns[q] * hit) * source[rows]
        terms = jnp.concatenate([join(upstream, BACKWARD) * source, tail_terms], axis=0)
        total = total + dot_nt(split(terms, BACKWARD), one_hot(rel_ref[:, span], rel_rows))
    gathered = join(total, BACKWARD)
    if rel_lanes > rel_rows:
        gathered = jnp.concatenate(
            [gathered, jnp.zeros((blocks + width, rel_lanes - rel_rows), F32)], axis=1
        )

    seeds = []
    tail_seed = jnp.zeros((width, rel_lanes), F32)
    tail_layer = jnp.zeros((width, width), F32)
    spare = jnp.zeros((width, out_ref.shape[1] - rel_lanes - width - 3 * hid), F32)
    for block in range(q_local + 1):
        if block < q_local:
            q = block
            rows = slice(q * width, (q + 1) * width)
            span = slice(q * neg, (q + 1) * neg)
            at_head = (entity_row == heads[:, q : q + 1]).astype(F32)
            at_rel = (rel_row == qrels[:, q : q + 1]).astype(F32)
            grad_qvec = jnp.sum(grad_both[width:, span], axis=1, keepdims=True) + jnp.sum(
                grad_sums[q] * at_head, axis=1, keepdims=True
            )
            seeds.append(grad_qvec * at_rel)
            tail_qvec = grad_both[width:, last + q : last + q + 1] + jnp.sum(
                grad_sums[q_local + q] * at_head, axis=1, keepdims=True
            )
            tail_seed = tail_seed + tail_qvec * at_rel
            left = stack_left(kept_ref[:, q * ent : (q + 1) * ent], 3)
            right = jnp.concatenate(
                [stack_right(pres[q], 3, axis=1), stack_right(tail_pres[q], 3, axis=1)], axis=0
            )
            layers = dot_nt(left, right)
            layer_part = layers[:, :width]
            tail_layer = tail_layer + layers[:, width:]
            vectors = prep_ref[:width, q : q + 1] + jnp.zeros((width, neg), F32)
            coef_rows = coef_parts[q * per_query : (q + 1) * per_query]
        else:
            span = slice(last, last + LANES)
            layer_part = tail_layer
            vectors = prep_ref[:width, :]
            coef_rows = coef_parts[-1:]
        size = span.stop - span.start
        coef = jnp.broadcast_to(jnp.concatenate(coef_rows, axis=1), (width, size))
        right = jnp.concatenate([grad_hidden[:, span], jnp.maximum(hidden[:, span], 0.0)], axis=0)
        left = jnp.concatenate([picked[:, span], vectors, coef], axis=0)
        products = dot_nt(stack_left(left, 3), stack_right(right, 3, axis=1))
        entity_part = products[:width, :hid]
        query_part = products[width : 2 * width, :hid]
        score_part = products[2 * width :, hid:]
        rest = [layer_part, entity_part, query_part, score_part, spare]
        out_ref[block * width : (block + 1) * width, rel_lanes:] = jnp.concatenate(rest, axis=1)
    seeds.append(tail_seed)
    out_ref[:, :rel_lanes] = gathered + jnp.concatenate(seeds, axis=0)
    new_copy.wait()


def combine_kernel(sizes, totals_ref, grads_ref, sent_ref):
    q_local, width = sizes
    total = jnp.sum(totals_ref[...], axis=0)
    scale = totals_ref[lax.axis_index("nodes")] / total
    mixed = grads_ref[q_local * width :, :]
    for q in range(q_local):
        mixed = mixed + grads_ref[q * width : (q + 1) * width, :] * scale[:, q : q + 1]
    across = mixed.shape[1] // LANES
    tiles = width // SUBLANES * across
    for tile in range(tiles):
        top, left = tile // across * SUBLANES, tile % across * LANES
        sent_ref[tile] = mixed[top : top + SUBLANES, left : left + LANES]
    for tile in range(tiles, sent_ref.shape[0]):
        sent_ref[tile] = jnp.zeros((SUBLANES, LANES), F32)


def spread_kernel(parts_ref, out_ref):
    total = jnp.sum(parts_ref[...], axis=0)
    for n in range(out_ref.shape[0]):
        out_ref[n] = total


def unpack_kernel(
    sizes, tiles_ref, totals_ref, rel_ref, layer_ref, ment_ref, mquery_ref, score_ref, loss_ref
):
    relations, across = sizes
    width, hid = ment_ref.shape
    down = width // SUBLANES
    flat = jnp.concatenate(
        [
            jnp.concatenate([tiles_ref[row * across + tile] for tile in range(across)], axis=1)
            for row in range(down)
        ],
        axis=0,
    )
    rel_lanes = pad_to(relations, LANES)
    rel_ref[...] = flat[:, :relations]
    start = rel_lanes
    layer_ref[...] = flat[:, start : start + width]
    start += width
    ment_ref[...] = flat[:, start : start + hid]
    start += hid
    mquery_ref[...] = flat[:, start : start + hid]
    start += hid
    score_ref[...] = flat[0:1, start : start + hid]
    everyone = jnp.sum(totals_ref[...], axis=0)
    count = loss_ref.shape[1]
    ratio = everyone[:, count : 2 * count] / everyone[:, :count]
    loss_ref[...] = everyone[:, 2 * count : 3 * count] + ratio


def call(kernel, name, outs, flops, *operands, scratch=(), far_out=(), alias=None):
    spaces = [pl.ANY if spot in far_out else pltpu.VMEM for spot in range(len(outs))]
    found = pl.pallas_call(
        kernel,
        out_shape=tuple(
            dims if isinstance(dims, jax.ShapeDtypeStruct) else jax.ShapeDtypeStruct(dims, F32)
            for dims in outs
        ),
        in_specs=[pl.BlockSpec(memory_space=pltpu.VMEM) for _ in operands],
        out_specs=tuple(pl.BlockSpec(memory_space=space) for space in spaces),
        scratch_shapes=scratch,
        input_output_aliases=alias or {},
        compiler_params=pltpu.CompilerParams(vmem_limit_bytes=40 << 20),
        cost_estimate=pl.CostEstimate(flops=flops, bytes_accessed=1 << 20, transcendentals=0),
        name=name,
    )(*operands)
    return found[0] if len(outs) == 1 else found


def swap(values, axes):
    return lax.all_to_all(values, axes, split_axis=0, concat_axis=0, tiled=True)


def body(
    state_in,
    edge_src,
    edge_dst,
    edge_rel,
    edge_count,
    send_list,
    query_head,
    query_rel,
    pos_tail,
    neg_ids,
    rel_table,
    layer_weight,
    mlp_entity,
    mlp_query,
    score_weight,
):
    nodes = lax.axis_size("nodes")
    queries = lax.axis_size("queries")
    ent, width_all = state_in.shape
    relations, width = rel_table.shape
    hid = mlp_entity.shape[1]
    q_local = width_all // width
    edges = edge_src.shape[0]
    bound = send_list.shape[2]
    neg = neg_ids.shape[1]
    columns = q_local * neg + LANES
    chunk = min(512, edges)
    src_row = edge_src.reshape(1, edges)
    dst_row = edge_dst.reshape(1, edges)
    rel_row = edge_rel.reshape(1, edges)
    count = edge_count.reshape(1, 1)
    score_row = score_weight.reshape(1, hid)
    table_t = rel_table.T
    tick = call(tick_kernel, "tick", [(SUBLANES, LANES)], 10**10)
    outgoing = call(
        send_kernel, "send", [(nodes, bound, width_all)], 10**9, tick, send_list[0], state_in
    )
    received = swap(outgoing, "nodes").reshape(nodes * bound, width_all)
    local, relation, prep, marks = call(
        functools.partial(early_kernel, (chunk,)),
        "early",
        [
            (width_all, edges),
            (width, edges),
            (width + 2 * hid, LANES),
            jax.ShapeDtypeStruct((SUBLANES, LANES), jnp.int32),
        ],
        4 * 10**9,
        state_in,
        src_row,
        rel_row,
        table_t,
        query_head.reshape(1, q_local),
        query_rel.reshape(1, q_local),
        pos_tail.reshape(1, q_local),
        layer_weight,
        mlp_entity,
        mlp_query,
        score_row,
    )
    needed = kept_layout(q_local, ent, neg)[-1].stop
    source_t, kept, gate, coef, totals = call(
        functools.partial(forward_kernel, (chunk,)),
        "forward",
        [
            (width_all, edges),
            (width, max(needed, edges)),
            jax.ShapeDtypeStruct((width_all, ent), BF16),
            (2 * pad_to(columns // LANES, SUBLANES), LANES),
            (nodes, 1, LANES),
        ],
        4 * 10**9,
        count,
        state_in,
        received,
        src_row,
        dst_row,
        neg_ids,
        local,
        relation,
        prep,
        marks,
        layer_weight,
        mlp_entity,
        alias={6: 0, 7: 1} if needed <= edges else {6: 0},
    )
    all_totals = swap(totals, "nodes")
    rel_lanes = pad_to(relations, LANES)
    lanes = rel_lanes + pad_to(width + 3 * hid, LANES)
    across = lanes // LANES
    grads, new_state = call(
        functools.partial(backward_kernel, (chunk, relations, q_local * queries)),
        "backward",
        [((q_local + 1) * width, lanes), (ent, width_all)],
        4 * 10**9,
        count,
        source_t,
        dst_row,
        rel_row,
        neg_ids,
        prep,
        marks,
        layer_weight,
        mlp_entity,
        mlp_query,
        kept,
        gate,
        coef,
        scratch=[pltpu.VMEM((ent, width_all), F32), pltpu.SemaphoreType.DMA((1,))],
        far_out=(1,),
    )
    tiles = width // SUBLANES * across
    wide = nodes * queries
    group = wide if wide <= pad_to(tiles, nodes) else nodes
    held = pad_to(tiles, group)
    sent = call(
        functools.partial(combine_kernel, (q_local, width)),
        "combine",
        [(held, SUBLANES, LANES)],
        10**6,
        all_totals,
        grads,
    )
    axes = ("nodes", "queries") if group == wide else "nodes"
    own = held // group
    parts = swap(sent, axes).reshape(group, own * SUBLANES, LANES)
    if group == wide:
        mine = call(spread_kernel, "spread", [(group, own * SUBLANES, LANES)], 10**6, parts)
    else:
        mine = lax.psum(jnp.sum(parts, axis=0), "queries")
        mine = jnp.broadcast_to(mine, (group,) + mine.shape)
    final = swap(mine, axes).reshape(held, SUBLANES, LANES)
    grad_rel, grad_layer, grad_entity, grad_query, grad_score, loss = call(
        functools.partial(unpack_kernel, (relations, across)),
        "unpack",
        [(width, relations), (width, width), (width, hid), (width, hid), (1, hid), (1, q_local)],
        10**6,
        final,
        all_totals,
    )
    return (
        new_state,
        loss.reshape(q_local),
        grad_rel.T,
        grad_layer,
        grad_entity,
        grad_query,
        grad_score.reshape(hid),
    )


def solution(mesh):
    in_specs = (
        P("nodes", "queries"),
        P("nodes"),
        P("nodes"),
        P("nodes"),
        P("nodes"),
        P("nodes", None, None),
        P("queries"),
        P("queries"),
        P("queries"),
        P("queries", "nodes"),
        P(),
        P(),
        P(),
        P(),
        P(),
    )
    out_specs = (P("nodes", "queries"), P("queries"), P(), P(), P(), P(), P())
    return jax.shard_map(body, mesh=mesh, in_specs=in_specs, out_specs=out_specs, check_vma=False)
```

```python
import functools

import jax
import jax.numpy as jnp
from jax import lax
from jax.experimental import pallas as pl
from jax.experimental.pallas import tpu as pltpu
from jax.sharding import PartitionSpec as P

adversarial = 0.5
HIGH = lax.Precision.HIGHEST
F32 = jnp.float32
BF16 = jnp.bfloat16
LANES = 128
SUBLANES = 8
FORWARD = 3
BACKWARD = 2


def pad_to(count, unit):
    return -(-count // unit) * unit


def split(values, pieces, axis=0):
    found = []
    for _ in range(pieces):
        piece = values.astype(BF16)
        values = values - piece.astype(F32)
        found.append(piece)
    return jnp.concatenate(found, axis=axis)


def join(values, pieces, axis=0):
    size = values.shape[axis] // pieces
    parts = [
        lax.slice_in_dim(values, piece * size, (piece + 1) * size, axis=axis)
        for piece in range(pieces)
    ]
    return functools.reduce(jnp.add, parts)


def one_hot(index_row, rows):
    parts = []
    for base in range(0, rows, 256):
        size = min(256, rows - base)
        local = index_row - base
        key = jnp.where((local >= 0) & (local < size), local, -1).astype(F32).astype(BF16)
        spots = lax.broadcasted_iota(jnp.int32, (size, index_row.shape[1]), 0)
        same = spots.astype(F32).astype(BF16) == key
        parts.append(jnp.where(same, jnp.ones((), BF16), jnp.zeros((), BF16)))
    return parts[0] if len(parts) == 1 else jnp.concatenate(parts, axis=0)


def dot_nn(left, right, precision=None):
    return lax.dot_general(
        left, right, (((1,), (0,)), ((), ())), precision=precision, preferred_element_type=F32
    )


def dot_nt(left, right, precision=None):
    return lax.dot_general(
        left, right, (((1,), (1,)), ((), ())), precision=precision, preferred_element_type=F32
    )


def pieces_of(values, count):
    found = []
    for _ in range(count):
        piece = values.astype(BF16)
        values = values - piece.astype(F32)
        found.append(piece)
    return found


LEFT = {6: (0, 0, 1, 0, 2, 1), 3: (0, 0, 1)}
RIGHT = {6: (0, 1, 0, 2, 0, 1), 3: (0, 1, 0)}


def stack_left(values, terms, axis=1):
    pieces = pieces_of(values, max(LEFT[terms]) + 1)
    return jnp.concatenate([pieces[spot] for spot in LEFT[terms]], axis=axis)


def stack_right(values, terms, axis=0):
    pieces = pieces_of(values, max(RIGHT[terms]) + 1)
    return jnp.concatenate([pieces[spot] for spot in RIGHT[terms]], axis=axis)


def pick_lanes(table, index_row, otherwise):
    rows, size = table.shape
    parts = []
    for left in range(0, index_row.shape[1], LANES):
        index = index_row[:, left : left + LANES]
        low = jnp.broadcast_to(index & (LANES - 1), (rows, LANES))
        tile = index >> (LANES.bit_length() - 1)
        found = otherwise[:, left : left + LANES]
        for spot in range(size // LANES):
            block = table[:, spot * LANES : (spot + 1) * LANES]
            taken = jnp.take_along_axis(block, low, axis=1, mode="promise_in_bounds")
            found = jnp.where(tile == spot, taken, found)
        parts.append(found)
    return jnp.concatenate(parts, axis=1)


def local_row(entity, ent_local):
    node = lax.axis_index("nodes")
    return jnp.where(entity // ent_local == node, entity % ent_local, -1)


def in_lanes(small_row):
    lane = lax.broadcasted_iota(jnp.int32, (1, LANES), 1)
    found = jnp.full((1, LANES), -1, jnp.int32)
    for spot in range(small_row.shape[1]):
        found = jnp.where(lane == spot, small_row[:, spot : spot + 1], found)
    return found


def as_column(row):
    size = row.shape[1]
    across = lax.broadcasted_iota(jnp.int32, (size, size), 1)
    down = lax.broadcasted_iota(jnp.int32, (size, size), 0)
    return jnp.sum(jnp.where(across == down, row, 0.0), axis=1, keepdims=True)


def as_row(column):
    size = column.shape[0]
    across = lax.broadcasted_iota(jnp.int32, (size, size), 1)
    down = lax.broadcasted_iota(jnp.int32, (size, size), 0)
    return jnp.sum(jnp.where(across == down, column, 0.0), axis=0, keepdims=True)


def fill_rows(rows, count):
    missing = count - len(rows)
    return jnp.concatenate(rows + [jnp.zeros((missing,) + rows[0].shape[1:], rows[0].dtype)], axis=0)


def kept_layout(q_local, ent, neg, parts=2):
    columns = q_local * neg + LANES
    ends = [0]
    for size in [q_local * ent] + [columns] * (1 + parts) + [q_local * ent]:
        ends.append(ends[-1] + size)
    return [slice(low, high) for low, high in zip(ends, ends[1:])]


def tick_kernel(out_ref):
    out_ref[...] = jnp.zeros(out_ref.shape, F32)


def wanted_kernel(tick_ref, send_ref, hot_ref):
    count, bound = send_ref.shape
    ent = hot_ref.shape[1]
    wanted = send_ref[...].T
    entity = lax.broadcasted_iota(jnp.int32, (bound, ent), 1)
    for n in range(count):
        same = entity == wanted[:, n : n + 1]
        hot_ref[n * bound : (n + 1) * bound, :] = jnp.where(same, 1.0, 0.0).astype(BF16)


def send_kernel(hot_ref, state_ref, out_ref):
    count, bound = out_ref.shape[:2]
    pieces = split(state_ref[...], FORWARD, axis=1)
    rows = join(dot_nn(hot_ref[...], pieces), FORWARD, axis=1)
    for n in range(count):
        out_ref[n] = rows[n * bound : (n + 1) * bound]


def early_kernel(
    sizes,
    state_ref,
    src_ref,
    rel_ref,
    table_ref,
    head_ref,
    qrel_ref,
    tail_ref,
    layer_ref,
    ment_ref,
    mquery_ref,
    score_ref,
    local_ref,
    relation_ref,
    prep_ref,
    marks_ref,
):
    (chunk,) = sizes
    ent = state_ref.shape[0]
    width, relations = table_ref.shape
    hid = ment_ref.shape[1]
    edges = src_ref.shape[1]
    rel_rows = pad_to(relations, 16)
    state_bits = split(state_ref[...].T, FORWARD)
    rel_bits = split(table_ref[...], FORWARD)
    rel_bits = jnp.concatenate(
        [rel_bits, jnp.zeros((FORWARD * width, rel_rows - relations), BF16)], axis=1
    )
    for start in range(0, edges, chunk):
        span = slice(start, start + chunk)
        local_ref[:, span] = join(dot_nn(state_bits, one_hot(src_ref[:, span], ent)), FORWARD)
        relation_ref[:, span] = join(
            dot_nn(rel_bits, one_hot(rel_ref[:, span], rel_rows)), FORWARD
        )
    heads = in_lanes(local_row(head_ref[...], ent))
    tails = in_lanes(local_row(tail_ref[...], ent))
    qrels = in_lanes(qrel_ref[...])
    marks_ref[...] = fill_rows([heads, tails, qrels], SUBLANES)
    qvec = join(dot_nn(rel_bits, one_hot(qrels, rel_rows)), FORWARD)
    prep_ref[:width, :] = qvec
    prep_ref[width : width + hid, :] = dot_nn(mquery_ref[...].T, qvec, HIGH)
    prep_ref[width + hid :, :] = jnp.broadcast_to(as_column(score_ref[...]), (hid, LANES))


def forward_kernel(
    sizes,
    count_ref,
    state_ref,
    recv_ref,
    src_ref,
    dst_ref,
    neg_ref,
    local_ref,
    relation_ref,
    prep_ref,
    marks_ref,
    layer_ref,
    ment_ref,
    srct_ref,
    kept_ref,
    gate_ref,
    coef_ref,
    totals_ref,
):
    (chunk,) = sizes
    ent, blocks = state_ref.shape
    edges = src_ref.shape[1]
    width, hid = ment_ref.shape
    q_local, neg = neg_ref.shape
    per_query = neg // LANES
    layout = kept_layout(q_local, ent, neg)
    recv_t = recv_ref[...].T
    near = min(256, recv_t.shape[1])
    recv_bits = split(recv_t[:, near:], FORWARD)
    live = count_ref[...]
    total = jnp.zeros((FORWARD * blocks, ent), F32)
    def fetch(start):
        span = slice(start, start + chunk)
        slot = src_ref[:, span] - ent
        first = pick_lanes(recv_t[:, :near], slot, local_ref[:, span])
        return first, dot_nn(recv_bits, one_hot(slot - near, recv_bits.shape[1]))

    coming = fetch(0)
    for start in range(0, edges, chunk):
        span = slice(start, start + chunk)
        remote = coming
        if start + chunk < edges:
            coming = fetch(start + chunk)
        source = remote[0] + join(remote[1], FORWARD)
        srct_ref[:, span] = source
        message = source * jnp.concatenate([relation_ref[:, span]] * q_local, axis=0)
        spot = lax.broadcasted_iota(jnp.int32, (1, chunk), 1) + start
        ends = jnp.where(spot < live, dst_ref[:, span], -1)
        total = total + dot_nt(split(message, FORWARD), one_hot(ends, ent))
    summed = join(total, FORWARD)

    entity_row = lax.broadcasted_iota(jnp.int32, (1, ent), 1)
    lane_row = lax.broadcasted_iota(jnp.int32, (1, LANES), 1)
    heads = marks_ref[0:1, :]
    tails = marks_ref[1:2, :]
    parts = []
    for q in range(q_local):
        at_head = (entity_row == heads[:, q : q + 1]).astype(F32)
        parts.append(summed[q * width : (q + 1) * width] + prep_ref[:width, q : q + 1] * at_head)
    wide = jnp.concatenate(parts, axis=1)
    kept_ref[:, layout[0]] = wide
    pre = dot_nn(stack_left(layer_ref[...].T, 6), stack_right(wide, 6))
    state_t = state_ref[...].T
    new_parts, picks, positive = [], [], None
    for q in range(q_local):
        rows = slice(q * width, (q + 1) * width)
        mine = pre[:, q * ent : (q + 1) * ent]
        gate_ref[rows, :] = (mine > 0.0).astype(F32).astype(BF16)
        new = state_t[rows] + jnp.maximum(mine, 0.0)
        new_parts.append(new)
        own_tail = jnp.where(lane_row == q, tails, -1)
        picks.append(pick_lanes(new, neg_ref[q : q + 1, :], jnp.zeros((width, neg), F32)))
        last = pick_lanes(new, own_tail, jnp.zeros((width, LANES), F32))
        positive = last if positive is None else positive + last
    kept_ref[:, layout[-1]] = jnp.concatenate(new_parts, axis=1)
    picked = jnp.concatenate(picks + [positive], axis=1)
    kept_ref[:, layout[1]] = picked
    plain = dot_nn(stack_left(ment_ref[...].T, 6), stack_right(picked, 6))
    rows = []
    for block in range(plain.shape[1] // LANES):
        span = slice(block * LANES, (block + 1) * LANES)
        q = block // per_query
        part = prep_ref[width : width + hid, :]
        if q < q_local:
            part = part[:, q : q + 1]
        hidden = plain[:, span] + part
        for part in range(hid // width):
            left = layout[2 + part].start + block * LANES
            kept_ref[:, left : left + LANES] = hidden[part * width : (part + 1) * width]
        weighted = jnp.maximum(hidden, 0.0) * prep_ref[width + hid :, :]
        rows.append(jnp.sum(weighted, axis=0, keepdims=True))
    height = coef_ref.shape[0] // 2
    scores = fill_rows(rows, height)
    weights = jnp.exp(adversarial * scores)
    near_zero = jnp.log1p(jnp.exp(-jnp.abs(scores)))
    softplus = jnp.maximum(scores, 0.0) + near_zero
    flipped = jnp.maximum(-scores, 0.0) + near_zero
    row_total = jnp.sum(weights, axis=1, keepdims=True)
    row_weighted = jnp.sum(weights * softplus, axis=1, keepdims=True)
    tail_row = len(rows) - 1
    positives = jnp.where(tails >= 0, flipped[tail_row : tail_row + 1], 0.0)
    owns, weighteds, row_owns = [], [], []
    for q in range(q_local):
        mine = slice(q * per_query, (q + 1) * per_query)
        own = jnp.sum(row_total[mine], axis=0, keepdims=True)
        owns.append(own)
        row_owns.extend([own] * per_query)
        weighteds.append(jnp.sum(row_weighted[mine], axis=0, keepdims=True))
    coef_ref[:height, :] = scores
    coef_ref[height:, :] = jnp.broadcast_to(fill_rows(row_owns, height), (height, LANES))
    tile = jnp.zeros((1, LANES), F32)
    for q in range(q_local):
        tile = jnp.where(lane_row == q, owns[q], tile)
        tile = jnp.where(lane_row == q_local + q, weighteds[q], tile)
        tile = jnp.where(lane_row == 2 * q_local + q, positives[:, q : q + 1], tile)
    for n in range(totals_ref.shape[0]):
        totals_ref[n] = tile


def backward_kernel(
    sizes,
    count_ref,
    srct_ref,
    dst_ref,
    rel_ref,
    neg_ref,
    prep_ref,
    marks_ref,
    layer_ref,
    ment_ref,
    mquery_ref,
    kept_ref,
    gate_ref,
    coef_ref,
    out_ref,
    new_hbm,
    new_ref,
    sems,
):
    chunk, relations, queries_total = sizes
    width, hid = ment_ref.shape
    blocks, ent = gate_ref.shape
    q_local, neg = neg_ref.shape
    edges = dst_ref.shape[1]
    layout = kept_layout(q_local, ent, neg)
    first = layout[-1].start
    new_parts = [kept_ref[:, first + q * ent : first + (q + 1) * ent] for q in range(q_local)]
    new_ref[...] = jnp.concatenate(new_parts, axis=0).T
    new_copy = pltpu.make_async_copy(new_ref, new_hbm, sems.at[0])
    new_copy.start()
    picked = kept_ref[:, layout[1]]
    hidden = jnp.concatenate([kept_ref[:, spot] for spot in layout[2:-1]], axis=0)
    per_query = neg // LANES
    rel_lanes = pad_to(relations, LANES)
    rel_rows = pad_to(relations, 16)
    heads = marks_ref[0:1, :]
    tails = marks_ref[1:2, :]
    qrels = marks_ref[2:3, :]
    entity_row = lax.broadcasted_iota(jnp.int32, (1, ent), 1)
    rel_row = lax.broadcasted_iota(jnp.int32, (1, rel_lanes), 1)
    height = coef_ref.shape[0] // 2
    scores, row_own = coef_ref[:height, :], coef_ref[height:, :]
    decay = jnp.exp(-jnp.abs(scores))
    share = 1.0 / (1.0 + decay)
    sigmoid = jnp.where(scores >= 0.0, share, decay * share)
    missing = jnp.where(scores >= 0.0, decay * share, share)
    weights = jnp.exp(adversarial * scores)
    coefs = weights * sigmoid / jnp.where(row_own > 0.0, row_own, 1.0)
    spot = lax.broadcasted_iota(jnp.int32, (height, LANES), 0)
    tail_row = hidden.shape[1] // LANES - 1
    coefs = jnp.where(spot < tail_row, coefs, 0.0)
    coefs = jnp.where((spot == tail_row) & (tails >= 0), -missing, coefs) * (1.0 / queries_total)
    grad_parts, coef_parts = [], []
    for block in range(hidden.shape[1] // LANES):
        span = slice(block * LANES, (block + 1) * LANES)
        coef = coefs[block : block + 1, :]
        coef_parts.append(coef)
        grad_parts.append(
            jnp.where(hidden[:, span] > 0.0, coef * prep_ref[width + hid :, :], 0.0)
        )
    grad_hidden = jnp.concatenate(grad_parts, axis=1)
    both = jnp.concatenate([ment_ref[...], mquery_ref[...]], axis=0)
    grad_both = dot_nn(stack_left(both, 3), stack_right(grad_hidden, 3))
    last = q_local * neg
    pres, tail_pres = [], []
    for q in range(q_local):
        rows = slice(q * width, (q + 1) * width)
        span = slice(q * neg, (q + 1) * neg)
        gate = gate_ref[rows, :].astype(F32)
        hot = one_hot(neg_ref[q : q + 1, :], ent)
        cube = join(dot_nt(split(grad_both[:width, span], BACKWARD), hot), BACKWARD)
        pres.append(gate * cube)
        at_tail = (entity_row == tails[:, q : q + 1]).astype(F32)
        tail_pres.append(gate * (grad_both[:width, last + q : last + q + 1] * at_tail))
    stacked = stack_right(jnp.concatenate(pres + tail_pres, axis=1), 3)
    sums = dot_nn(stack_left(layer_ref[...], 3), stacked)
    grad_sums = [sums[:, q * ent : (q + 1) * ent] for q in range(2 * q_local)]
    sum_bits = split(jnp.concatenate(grad_sums[:q_local], axis=0), BACKWARD)
    tail_columns = [
        jnp.sum(grad_sums[q_local + q], axis=1, keepdims=True) for q in range(q_local)
    ]

    live = count_ref[...]

    def fetch(start):
        spot = lax.broadcasted_iota(jnp.int32, (1, chunk), 1) + start
        ends = jnp.where(spot < live, dst_ref[:, start : start + chunk], -2)
        return ends, dot_nn(sum_bits, one_hot(ends, ent))

    total = jnp.zeros((BACKWARD * (blocks + width), rel_rows), F32)
    coming = fetch(0)
    for start in range(0, edges, chunk):
        span = slice(start, start + chunk)
        ends, upstream = coming
        if start + chunk < edges:
            coming = fetch(start + chunk)
        source = srct_ref[:, span]
        tail_terms = jnp.zeros((width, chunk), F32)
        for q in range(q_local):
            rows = slice(q * width, (q + 1) * width)
            hit = (ends == tails[:, q : q + 1]).astype(F32)
            tail_terms = tail_terms + (tail_columns[q] * hit) * source[rows]
        terms = jnp.concatenate([join(upstream, BACKWARD) * source, tail_terms], axis=0)
        total = total + dot_nt(split(terms, BACKWARD), one_hot(rel_ref[:, span], rel_rows))
    gathered = join(total, BACKWARD)
    if rel_lanes > rel_rows:
        gathered = jnp.concatenate(
            [gathered, jnp.zeros((blocks + width, rel_lanes - rel_rows), F32)], axis=1
        )

    seeds = []
    tail_seed = jnp.zeros((width, rel_lanes), F32)
    tail_layer = jnp.zeros((width, width), F32)
    spare = jnp.zeros((width, out_ref.shape[1] - rel_lanes - width - 3 * hid), F32)
    for block in range(q_local + 1):
        if block < q_local:
            q = block
            rows = slice(q * width, (q + 1) * width)
            span = slice(q * neg, (q + 1) * neg)
            at_head = (entity_row == heads[:, q : q + 1]).astype(F32)
            at_rel = (rel_row == qrels[:, q : q + 1]).astype(F32)
            grad_qvec = jnp.sum(grad_both[width:, span], axis=1, keepdims=True) + jnp.sum(
                grad_sums[q] * at_head, axis=1, keepdims=True
            )
            seeds.append(grad_qvec * at_rel)
            tail_qvec = grad_both[width:, last + q : last + q + 1] + jnp.sum(
                grad_sums[q_local + q] * at_head, axis=1, keepdims=True
            )
            tail_seed = tail_seed + tail_qvec * at_rel
            left = stack_left(kept_ref[:, q * ent : (q + 1) * ent], 3)
            right = jnp.concatenate(
                [stack_right(pres[q], 3, axis=1), stack_right(tail_pres[q], 3, axis=1)], axis=0
            )
            layers = dot_nt(left, right)
            layer_part = layers[:, :width]
            tail_layer = tail_layer + layers[:, width:]
            vectors = prep_ref[:width, q : q + 1] + jnp.zeros((width, neg), F32)
            coef_rows = coef_parts[q * per_query : (q + 1) * per_query]
        else:
            span = slice(last, last + LANES)
            layer_part = tail_layer
            vectors = prep_ref[:width, :]
            coef_rows = coef_parts[-1:]
        size = span.stop - span.start
        coef = jnp.broadcast_to(jnp.concatenate(coef_rows, axis=1), (width, size))
        right = jnp.concatenate([grad_hidden[:, span], jnp.maximum(hidden[:, span], 0.0)], axis=0)
        left = jnp.concatenate([picked[:, span], vectors, coef], axis=0)
        products = dot_nt(stack_left(left, 3), stack_right(right, 3, axis=1))
        entity_part = products[:width, :hid]
        query_part = products[width : 2 * width, :hid]
        score_part = products[2 * width :, hid:]
        rest = [layer_part, entity_part, query_part, score_part, spare]
        out_ref[block * width : (block + 1) * width, rel_lanes:] = jnp.concatenate(rest, axis=1)
    seeds.append(tail_seed)
    out_ref[:, :rel_lanes] = gathered + jnp.concatenate(seeds, axis=0)
    new_copy.wait()


def combine_kernel(sizes, totals_ref, grads_ref, sent_ref):
    q_local, width = sizes
    total = jnp.sum(totals_ref[...], axis=0)
    scale = totals_ref[lax.axis_index("nodes")] / total
    mixed = grads_ref[q_local * width :, :]
    for q in range(q_local):
        mixed = mixed + grads_ref[q * width : (q + 1) * width, :] * scale[:, q : q + 1]
    across = mixed.shape[1] // LANES
    tiles = width // SUBLANES * across
    for tile in range(tiles):
        top, left = tile // across * SUBLANES, tile % across * LANES
        sent_ref[tile] = mixed[top : top + SUBLANES, left : left + LANES]
    for tile in range(tiles, sent_ref.shape[0]):
        sent_ref[tile] = jnp.zeros((SUBLANES, LANES), F32)


def spread_kernel(parts_ref, out_ref):
    total = jnp.sum(parts_ref[...], axis=0)
    for n in range(out_ref.shape[0]):
        out_ref[n] = total


def unpack_kernel(
    sizes, tiles_ref, totals_ref, rel_ref, layer_ref, ment_ref, mquery_ref, score_ref, loss_ref
):
    relations, across = sizes
    width, hid = ment_ref.shape
    down = width // SUBLANES
    flat = jnp.concatenate(
        [
            jnp.concatenate([tiles_ref[row * across + tile] for tile in range(across)], axis=1)
            for row in range(down)
        ],
        axis=0,
    )
    rel_lanes = pad_to(relations, LANES)
    rel_ref[...] = flat[:, :relations]
    start = rel_lanes
    layer_ref[...] = flat[:, start : start + width]
    start += width
    ment_ref[...] = flat[:, start : start + hid]
    start += hid
    mquery_ref[...] = flat[:, start : start + hid]
    start += hid
    score_ref[...] = flat[0:1, start : start + hid]
    everyone = jnp.sum(totals_ref[...], axis=0)
    count = loss_ref.shape[1]
    ratio = everyone[:, count : 2 * count] / everyone[:, :count]
    loss_ref[...] = everyone[:, 2 * count : 3 * count] + ratio


def call(kernel, name, outs, flops, *operands, scratch=(), far_out=(), alias=None):
    spaces = [pl.ANY if spot in far_out else pltpu.VMEM for spot in range(len(outs))]
    found = pl.pallas_call(
        kernel,
        out_shape=tuple(
            dims if isinstance(dims, jax.ShapeDtypeStruct) else jax.ShapeDtypeStruct(dims, F32)
            for dims in outs
        ),
        in_specs=[pl.BlockSpec(memory_space=pltpu.VMEM) for _ in operands],
        out_specs=tuple(pl.BlockSpec(memory_space=space) for space in spaces),
        scratch_shapes=scratch,
        input_output_aliases=alias or {},
        compiler_params=pltpu.CompilerParams(vmem_limit_bytes=40 << 20),
        cost_estimate=pl.CostEstimate(flops=flops, bytes_accessed=min(flops, 1 << 20), transcendentals=0),
        name=name,
    )(*operands)
    return found[0] if len(outs) == 1 else found


def swap(values, axes):
    return lax.all_to_all(values, axes, split_axis=0, concat_axis=0, tiled=True)


def body(
    state_in,
    edge_src,
    edge_dst,
    edge_rel,
    edge_count,
    send_list,
    query_head,
    query_rel,
    pos_tail,
    neg_ids,
    rel_table,
    layer_weight,
    mlp_entity,
    mlp_query,
    score_weight,
):
    nodes = lax.axis_size("nodes")
    queries = lax.axis_size("queries")
    ent, width_all = state_in.shape
    relations, width = rel_table.shape
    hid = mlp_entity.shape[1]
    q_local = width_all // width
    edges = edge_src.shape[0]
    bound = send_list.shape[2]
    neg = neg_ids.shape[1]
    columns = q_local * neg + LANES
    chunk = min(512, edges)
    src_row = edge_src.reshape(1, edges)
    dst_row = edge_dst.reshape(1, edges)
    rel_row = edge_rel.reshape(1, edges)
    count = edge_count.reshape(1, 1)
    score_row = score_weight.reshape(1, hid)
    table_t = rel_table.T
    tick = call(tick_kernel, "tick", [(SUBLANES, LANES)], 10**10)
    hot = call(
        wanted_kernel,
        "wanted",
        [jax.ShapeDtypeStruct((nodes * bound, ent), BF16)],
        1,
        tick,
        send_list[0],
    )
    outgoing = call(send_kernel, "send", [(nodes, bound, width_all)], 10**9, hot, state_in)
    received = swap(outgoing, "nodes").reshape(nodes * bound, width_all)
    local, relation, prep, marks = call(
        functools.partial(early_kernel, (chunk,)),
        "early",
        [
            (width_all, edges),
            (width, edges),
            (width + 2 * hid, LANES),
            jax.ShapeDtypeStruct((SUBLANES, LANES), jnp.int32),
        ],
        4 * 10**9,
        state_in,
        src_row,
        rel_row,
        table_t,
        query_head.reshape(1, q_local),
        query_rel.reshape(1, q_local),
        pos_tail.reshape(1, q_local),
        layer_weight,
        mlp_entity,
        mlp_query,
        score_row,
    )
    needed = kept_layout(q_local, ent, neg)[-1].stop
    source_t, kept, gate, coef, totals = call(
        functools.partial(forward_kernel, (chunk,)),
        "forward",
        [
            (width_all, edges),
            (width, max(needed, edges)),
            jax.ShapeDtypeStruct((width_all, ent), BF16),
            (2 * pad_to(columns // LANES, SUBLANES), LANES),
            (nodes, 1, LANES),
        ],
        4 * 10**9,
        count,
        state_in,
        received,
        src_row,
        dst_row,
        neg_ids,
        local,
        relation,
        prep,
        marks,
        layer_weight,
        mlp_entity,
        alias={6: 0, 7: 1} if needed <= edges else {6: 0},
    )
    all_totals = swap(totals, "nodes")
    rel_lanes = pad_to(relations, LANES)
    lanes = rel_lanes + pad_to(width + 3 * hid, LANES)
    across = lanes // LANES
    grads, new_state = call(
        functools.partial(backward_kernel, (chunk, relations, q_local * queries)),
        "backward",
        [((q_local + 1) * width, lanes), (ent, width_all)],
        4 * 10**9,
        count,
        source_t,
        dst_row,
        rel_row,
        neg_ids,
        prep,
        marks,
        layer_weight,
        mlp_entity,
        mlp_query,
        kept,
        gate,
        coef,
        scratch=[pltpu.VMEM((ent, width_all), F32), pltpu.SemaphoreType.DMA((1,))],
        far_out=(1,),
    )
    tiles = width // SUBLANES * across
    wide = nodes * queries
    group = wide if wide <= pad_to(tiles, nodes) else nodes
    held = pad_to(tiles, group)
    sent = call(
        functools.partial(combine_kernel, (q_local, width)),
        "combine",
        [(held, SUBLANES, LANES)],
        10**6,
        all_totals,
        grads,
    )
    axes = ("nodes", "queries") if group == wide else "nodes"
    own = held // group
    parts = swap(sent, axes).reshape(group, own * SUBLANES, LANES)
    if group == wide:
        mine = call(spread_kernel, "spread", [(group, own * SUBLANES, LANES)], 10**6, parts)
    else:
        mine = lax.psum(jnp.sum(parts, axis=0), "queries")
        mine = jnp.broadcast_to(mine, (group,) + mine.shape)
    final = swap(mine, axes).reshape(held, SUBLANES, LANES)
    grad_rel, grad_layer, grad_entity, grad_query, grad_score, loss = call(
        functools.partial(unpack_kernel, (relations, across)),
        "unpack",
        [(width, relations), (width, width), (width, hid), (width, hid), (1, hid), (1, q_local)],
        10**6,
        final,
        all_totals,
    )
    return (
        new_state,
        loss.reshape(q_local),
        grad_rel.T,
        grad_layer,
        grad_entity,
        grad_query,
        grad_score.reshape(hid),
    )


def solution(mesh):
    in_specs = (
        P("nodes", "queries"),
        P("nodes"),
        P("nodes"),
        P("nodes"),
        P("nodes"),
        P("nodes", None, None),
        P("queries"),
        P("queries"),
        P("queries"),
        P("queries", "nodes"),
        P(),
        P(),
        P(),
        P(),
        P(),
    )
    out_specs = (P("nodes", "queries"), P("queries"), P(), P(), P(), P(), P())
    return jax.shard_map(body, mesh=mesh, in_specs=in_specs, out_specs=out_specs, check_vma=False)
```

```python
import functools

import jax
import jax.numpy as jnp
from jax import lax
from jax.experimental import pallas as pl
from jax.experimental.pallas import tpu as pltpu
from jax.sharding import PartitionSpec as P

adversarial = 0.5
HIGH = lax.Precision.HIGHEST
F32 = jnp.float32
BF16 = jnp.bfloat16
LANES = 128
SUBLANES = 8
FORWARD = 3
BACKWARD = 2


def pad_to(count, unit):
    return -(-count // unit) * unit


def split(values, pieces, axis=0):
    found = []
    for _ in range(pieces):
        piece = values.astype(BF16)
        values = values - piece.astype(F32)
        found.append(piece)
    return jnp.concatenate(found, axis=axis)


def join(values, pieces, axis=0):
    size = values.shape[axis] // pieces
    parts = [
        lax.slice_in_dim(values, piece * size, (piece + 1) * size, axis=axis)
        for piece in range(pieces)
    ]
    return functools.reduce(jnp.add, parts)


def one_hot(index_row, rows):
    parts = []
    for base in range(0, rows, 256):
        size = min(256, rows - base)
        local = index_row - base
        key = jnp.where((local >= 0) & (local < size), local, -1).astype(F32).astype(BF16)
        spots = lax.broadcasted_iota(jnp.int32, (size, index_row.shape[1]), 0)
        same = spots.astype(F32).astype(BF16) == key
        parts.append(jnp.where(same, jnp.ones((), BF16), jnp.zeros((), BF16)))
    return parts[0] if len(parts) == 1 else jnp.concatenate(parts, axis=0)


def dot_nn(left, right, precision=None):
    return lax.dot_general(
        left, right, (((1,), (0,)), ((), ())), precision=precision, preferred_element_type=F32
    )


def dot_nt(left, right, precision=None):
    return lax.dot_general(
        left, right, (((1,), (1,)), ((), ())), precision=precision, preferred_element_type=F32
    )


def pieces_of(values, count):
    found = []
    for _ in range(count):
        piece = values.astype(BF16)
        values = values - piece.astype(F32)
        found.append(piece)
    return found


LEFT = {6: (0, 0, 1, 0, 2, 1), 3: (0, 0, 1)}
RIGHT = {6: (0, 1, 0, 2, 0, 1), 3: (0, 1, 0)}


def stack_left(values, terms, axis=1):
    pieces = pieces_of(values, max(LEFT[terms]) + 1)
    return jnp.concatenate([pieces[spot] for spot in LEFT[terms]], axis=axis)


def stack_right(values, terms, axis=0):
    pieces = pieces_of(values, max(RIGHT[terms]) + 1)
    return jnp.concatenate([pieces[spot] for spot in RIGHT[terms]], axis=axis)


def pick_lanes(table, index_row, otherwise):
    rows, size = table.shape
    parts = []
    for left in range(0, index_row.shape[1], LANES):
        index = index_row[:, left : left + LANES]
        low = jnp.broadcast_to(index & (LANES - 1), (rows, LANES))
        tile = index >> (LANES.bit_length() - 1)
        found = otherwise[:, left : left + LANES]
        for spot in range(size // LANES):
            block = table[:, spot * LANES : (spot + 1) * LANES]
            taken = jnp.take_along_axis(block, low, axis=1, mode="promise_in_bounds")
            found = jnp.where(tile == spot, taken, found)
        parts.append(found)
    return jnp.concatenate(parts, axis=1)


def local_row(entity, ent_local):
    node = lax.axis_index("nodes")
    return jnp.where(entity // ent_local == node, entity % ent_local, -1)


def in_lanes(small_row):
    lane = lax.broadcasted_iota(jnp.int32, (1, LANES), 1)
    found = jnp.full((1, LANES), -1, jnp.int32)
    for spot in range(small_row.shape[1]):
        found = jnp.where(lane == spot, small_row[:, spot : spot + 1], found)
    return found


def as_column(row):
    size = row.shape[1]
    across = lax.broadcasted_iota(jnp.int32, (size, size), 1)
    down = lax.broadcasted_iota(jnp.int32, (size, size), 0)
    return jnp.sum(jnp.where(across == down, row, 0.0), axis=1, keepdims=True)


def as_row(column):
    size = column.shape[0]
    across = lax.broadcasted_iota(jnp.int32, (size, size), 1)
    down = lax.broadcasted_iota(jnp.int32, (size, size), 0)
    return jnp.sum(jnp.where(across == down, column, 0.0), axis=0, keepdims=True)


def fill_rows(rows, count):
    missing = count - len(rows)
    return jnp.concatenate(rows + [jnp.zeros((missing,) + rows[0].shape[1:], rows[0].dtype)], axis=0)


def kept_layout(q_local, ent, neg, parts=2):
    columns = q_local * neg + LANES
    ends = [0]
    for size in [q_local * ent] + [columns] * (1 + parts) + [q_local * ent]:
        ends.append(ends[-1] + size)
    return [slice(low, high) for low, high in zip(ends, ends[1:])]


def tick_kernel(out_ref):
    out_ref[...] = jnp.zeros(out_ref.shape, F32)


def wanted_kernel(tick_ref, send_ref, hot_ref):
    count, bound = send_ref.shape
    ent = hot_ref.shape[1]
    wanted = send_ref[...].T
    entity = lax.broadcasted_iota(jnp.int32, (bound, ent), 1)
    for n in range(count):
        same = entity == wanted[:, n : n + 1]
        hot_ref[n * bound : (n + 1) * bound, :] = jnp.where(same, 1.0, 0.0).astype(BF16)


def send_kernel(hot_ref, state_ref, out_ref):
    count, bound = out_ref.shape[:2]
    pieces = split(state_ref[...], FORWARD, axis=1)
    rows = join(dot_nn(hot_ref[...], pieces), FORWARD, axis=1)
    for n in range(count):
        out_ref[n] = rows[n * bound : (n + 1) * bound]


def early_kernel(
    sizes,
    state_ref,
    src_ref,
    rel_ref,
    table_ref,
    head_ref,
    qrel_ref,
    tail_ref,
    layer_ref,
    ment_ref,
    mquery_ref,
    score_ref,
    local_ref,
    relation_ref,
    prep_ref,
    marks_ref,
):
    (chunk,) = sizes
    ent = state_ref.shape[0]
    width, relations = table_ref.shape
    hid = ment_ref.shape[1]
    edges = src_ref.shape[1]
    rel_rows = pad_to(relations, 16)
    state_bits = split(state_ref[...].T, FORWARD)
    rel_bits = split(table_ref[...], FORWARD)
    rel_bits = jnp.concatenate(
        [rel_bits, jnp.zeros((FORWARD * width, rel_rows - relations), BF16)], axis=1
    )
    for start in range(0, edges, chunk):
        span = slice(start, start + chunk)
        local_ref[:, span] = join(dot_nn(state_bits, one_hot(src_ref[:, span], ent)), FORWARD)
        relation_ref[:, span] = join(
            dot_nn(rel_bits, one_hot(rel_ref[:, span], rel_rows)), FORWARD
        )
    heads = in_lanes(local_row(head_ref[...], ent))
    tails = in_lanes(local_row(tail_ref[...], ent))
    qrels = in_lanes(qrel_ref[...])
    marks_ref[...] = fill_rows([heads, tails, qrels], SUBLANES)
    qvec = join(dot_nn(rel_bits, one_hot(qrels, rel_rows)), FORWARD)
    prep_ref[:width, :] = qvec
    prep_ref[width : width + hid, :] = dot_nn(mquery_ref[...].T, qvec, HIGH)
    prep_ref[width + hid :, :] = jnp.broadcast_to(as_column(score_ref[...]), (hid, LANES))


def forward_kernel(
    sizes,
    count_ref,
    state_ref,
    recv_ref,
    src_ref,
    dst_ref,
    neg_ref,
    local_ref,
    relation_ref,
    prep_ref,
    marks_ref,
    layer_ref,
    ment_ref,
    srct_ref,
    kept_ref,
    gate_ref,
    coef_ref,
    totals_ref,
):
    (chunk,) = sizes
    ent, blocks = state_ref.shape
    edges = src_ref.shape[1]
    width, hid = ment_ref.shape
    q_local, neg = neg_ref.shape
    per_query = neg // LANES
    layout = kept_layout(q_local, ent, neg)
    recv_t = recv_ref[...].T
    near = min(256, recv_t.shape[1])
    recv_bits = split(recv_t[:, near:], FORWARD)
    live = count_ref[...]
    total = jnp.zeros((FORWARD * blocks, ent), F32)
    def fetch(start):
        span = slice(start, start + chunk)
        slot = src_ref[:, span] - ent
        first = pick_lanes(recv_t[:, :near], slot, local_ref[:, span])
        return first, dot_nn(recv_bits, one_hot(slot - near, recv_bits.shape[1]))

    coming = fetch(0)
    for start in range(0, edges, chunk):
        span = slice(start, start + chunk)
        remote = coming
        if start + chunk < edges:
            coming = fetch(start + chunk)
        source = remote[0] + join(remote[1], FORWARD)
        srct_ref[:, span] = source
        message = source * jnp.concatenate([relation_ref[:, span]] * q_local, axis=0)
        spot = lax.broadcasted_iota(jnp.int32, (1, chunk), 1) + start
        ends = jnp.where(spot < live, dst_ref[:, span], -1)
        total = total + dot_nt(split(message, FORWARD), one_hot(ends, ent))
    summed = join(total, FORWARD)

    entity_row = lax.broadcasted_iota(jnp.int32, (1, ent), 1)
    lane_row = lax.broadcasted_iota(jnp.int32, (1, LANES), 1)
    heads = marks_ref[0:1, :]
    tails = marks_ref[1:2, :]
    parts = []
    for q in range(q_local):
        at_head = (entity_row == heads[:, q : q + 1]).astype(F32)
        parts.append(summed[q * width : (q + 1) * width] + prep_ref[:width, q : q + 1] * at_head)
    wide = jnp.concatenate(parts, axis=1)
    kept_ref[:, layout[0]] = wide
    pre = dot_nn(stack_left(layer_ref[...].T, 6), stack_right(wide, 6))
    state_t = state_ref[...].T
    new_parts, picks, positive = [], [], None
    for q in range(q_local):
        rows = slice(q * width, (q + 1) * width)
        mine = pre[:, q * ent : (q + 1) * ent]
        gate_ref[rows, :] = (mine > 0.0).astype(F32).astype(BF16)
        new = state_t[rows] + jnp.maximum(mine, 0.0)
        new_parts.append(new)
        own_tail = jnp.where(lane_row == q, tails, -1)
        picks.append(pick_lanes(new, neg_ref[q : q + 1, :], jnp.zeros((width, neg), F32)))
        last = pick_lanes(new, own_tail, jnp.zeros((width, LANES), F32))
        positive = last if positive is None else positive + last
    kept_ref[:, layout[-1]] = jnp.concatenate(new_parts, axis=1)
    picked = jnp.concatenate(picks + [positive], axis=1)
    kept_ref[:, layout[1]] = picked
    plain = dot_nn(stack_left(ment_ref[...].T, 6), stack_right(picked, 6))
    rows = []
    for block in range(plain.shape[1] // LANES):
        span = slice(block * LANES, (block + 1) * LANES)
        q = block // per_query
        part = prep_ref[width : width + hid, :]
        if q < q_local:
            part = part[:, q : q + 1]
        hidden = plain[:, span] + part
        for part in range(hid // width):
            left = layout[2 + part].start + block * LANES
            kept_ref[:, left : left + LANES] = hidden[part * width : (part + 1) * width]
        weighted = jnp.maximum(hidden, 0.0) * prep_ref[width + hid :, :]
        rows.append(jnp.sum(weighted, axis=0, keepdims=True))
    height = coef_ref.shape[0] // 2
    scores = fill_rows(rows, height)
    weights = jnp.exp(adversarial * scores)
    near_zero = jnp.log1p(jnp.exp(-jnp.abs(scores)))
    softplus = jnp.maximum(scores, 0.0) + near_zero
    flipped = jnp.maximum(-scores, 0.0) + near_zero
    row_total = jnp.sum(weights, axis=1, keepdims=True)
    row_weighted = jnp.sum(weights * softplus, axis=1, keepdims=True)
    tail_row = len(rows) - 1
    positives = jnp.where(tails >= 0, flipped[tail_row : tail_row + 1], 0.0)
    owns, weighteds, row_owns = [], [], []
    for q in range(q_local):
        mine = slice(q * per_query, (q + 1) * per_query)
        own = jnp.sum(row_total[mine], axis=0, keepdims=True)
        owns.append(own)
        row_owns.extend([own] * per_query)
        weighteds.append(jnp.sum(row_weighted[mine], axis=0, keepdims=True))
    coef_ref[:height, :] = scores
    coef_ref[height:, :] = jnp.broadcast_to(fill_rows(row_owns, height), (height, LANES))
    tile = jnp.zeros((1, LANES), F32)
    for q in range(q_local):
        tile = jnp.where(lane_row == q, owns[q], tile)
        tile = jnp.where(lane_row == q_local + q, weighteds[q], tile)
        tile = jnp.where(lane_row == 2 * q_local + q, positives[:, q : q + 1], tile)
    for n in range(totals_ref.shape[0]):
        totals_ref[n] = tile


def backward_kernel(
    sizes,
    count_ref,
    srct_ref,
    dst_ref,
    rel_ref,
    neg_ref,
    prep_ref,
    marks_ref,
    layer_ref,
    ment_ref,
    mquery_ref,
    kept_ref,
    gate_ref,
    coef_ref,
    out_ref,
    new_hbm,
    new_ref,
    sems,
):
    chunk, relations, queries_total = sizes
    width, hid = ment_ref.shape
    blocks, ent = gate_ref.shape
    q_local, neg = neg_ref.shape
    edges = dst_ref.shape[1]
    layout = kept_layout(q_local, ent, neg)
    first = layout[-1].start
    new_parts = [kept_ref[:, first + q * ent : first + (q + 1) * ent] for q in range(q_local)]
    new_ref[...] = jnp.concatenate(new_parts, axis=0).T
    new_copy = pltpu.make_async_copy(new_ref, new_hbm, sems.at[0])
    new_copy.start()
    picked = kept_ref[:, layout[1]]
    hidden = jnp.concatenate([kept_ref[:, spot] for spot in layout[2:-1]], axis=0)
    per_query = neg // LANES
    rel_lanes = pad_to(relations, LANES)
    rel_rows = pad_to(relations, 16)
    heads = marks_ref[0:1, :]
    tails = marks_ref[1:2, :]
    qrels = marks_ref[2:3, :]
    entity_row = lax.broadcasted_iota(jnp.int32, (1, ent), 1)
    rel_row = lax.broadcasted_iota(jnp.int32, (1, rel_lanes), 1)
    height = coef_ref.shape[0] // 2
    scores, row_own = coef_ref[:height, :], coef_ref[height:, :]
    decay = jnp.exp(-jnp.abs(scores))
    share = 1.0 / (1.0 + decay)
    sigmoid = jnp.where(scores >= 0.0, share, decay * share)
    missing = jnp.where(scores >= 0.0, decay * share, share)
    weights = jnp.exp(adversarial * scores)
    coefs = weights * sigmoid / jnp.where(row_own > 0.0, row_own, 1.0)
    spot = lax.broadcasted_iota(jnp.int32, (height, LANES), 0)
    tail_row = hidden.shape[1] // LANES - 1
    coefs = jnp.where(spot < tail_row, coefs, 0.0)
    coefs = jnp.where((spot == tail_row) & (tails >= 0), -missing, coefs) * (1.0 / queries_total)
    grad_parts, coef_parts = [], []
    for block in range(hidden.shape[1] // LANES):
        span = slice(block * LANES, (block + 1) * LANES)
        coef = coefs[block : block + 1, :]
        coef_parts.append(coef)
        grad_parts.append(
            jnp.where(hidden[:, span] > 0.0, coef * prep_ref[width + hid :, :], 0.0)
        )
    grad_hidden = jnp.concatenate(grad_parts, axis=1)
    both = jnp.concatenate([ment_ref[...], mquery_ref[...]], axis=0)
    grad_both = dot_nn(stack_left(both, 3), stack_right(grad_hidden, 3))
    last = q_local * neg
    pres, tail_pres = [], []
    for q in range(q_local):
        rows = slice(q * width, (q + 1) * width)
        span = slice(q * neg, (q + 1) * neg)
        gate = gate_ref[rows, :].astype(F32)
        hot = one_hot(neg_ref[q : q + 1, :], ent)
        cube = join(dot_nt(split(grad_both[:width, span], BACKWARD), hot), BACKWARD)
        pres.append(gate * cube)
        at_tail = (entity_row == tails[:, q : q + 1]).astype(F32)
        tail_pres.append(gate * (grad_both[:width, last + q : last + q + 1] * at_tail))
    stacked = stack_right(jnp.concatenate(pres + tail_pres, axis=1), 3)
    sums = dot_nn(stack_left(layer_ref[...], 3), stacked)
    grad_sums = [sums[:, q * ent : (q + 1) * ent] for q in range(2 * q_local)]
    sum_bits = split(jnp.concatenate(grad_sums[:q_local], axis=0), BACKWARD)
    tail_columns = [
        jnp.sum(grad_sums[q_local + q], axis=1, keepdims=True) for q in range(q_local)
    ]

    live = count_ref[...]

    def fetch(start):
        spot = lax.broadcasted_iota(jnp.int32, (1, chunk), 1) + start
        ends = jnp.where(spot < live, dst_ref[:, start : start + chunk], -2)
        return ends, dot_nn(sum_bits, one_hot(ends, ent))

    total = jnp.zeros((BACKWARD * (blocks + width), rel_rows), F32)
    coming = fetch(0)
    for start in range(0, edges, chunk):
        span = slice(start, start + chunk)
        ends, upstream = coming
        if start + chunk < edges:
            coming = fetch(start + chunk)
        source = srct_ref[:, span]
        tail_terms = jnp.zeros((width, chunk), F32)
        for q in range(q_local):
            rows = slice(q * width, (q + 1) * width)
            hit = (ends == tails[:, q : q + 1]).astype(F32)
            tail_terms = tail_terms + (tail_columns[q] * hit) * source[rows]
        terms = jnp.concatenate([join(upstream, BACKWARD) * source, tail_terms], axis=0)
        total = total + dot_nt(split(terms, BACKWARD), one_hot(rel_ref[:, span], rel_rows))
    gathered = join(total, BACKWARD)
    if rel_lanes > rel_rows:
        gathered = jnp.concatenate(
            [gathered, jnp.zeros((blocks + width, rel_lanes - rel_rows), F32)], axis=1
        )

    seeds = []
    tail_seed = jnp.zeros((width, rel_lanes), F32)
    tail_layer = jnp.zeros((width, width), F32)
    spare = jnp.zeros((width, out_ref.shape[1] - rel_lanes - width - 3 * hid), F32)
    for block in range(q_local + 1):
        if block < q_local:
            q = block
            rows = slice(q * width, (q + 1) * width)
            span = slice(q * neg, (q + 1) * neg)
            at_head = (entity_row == heads[:, q : q + 1]).astype(F32)
            at_rel = (rel_row == qrels[:, q : q + 1]).astype(F32)
            grad_qvec = jnp.sum(grad_both[width:, span], axis=1, keepdims=True) + jnp.sum(
                grad_sums[q] * at_head, axis=1, keepdims=True
            )
            seeds.append(grad_qvec * at_rel)
            tail_qvec = grad_both[width:, last + q : last + q + 1] + jnp.sum(
                grad_sums[q_local + q] * at_head, axis=1, keepdims=True
            )
            tail_seed = tail_seed + tail_qvec * at_rel
            left = stack_left(kept_ref[:, q * ent : (q + 1) * ent], 3)
            right = jnp.concatenate(
                [stack_right(pres[q], 3, axis=1), stack_right(tail_pres[q], 3, axis=1)], axis=0
            )
            layers = dot_nt(left, right)
            layer_part = layers[:, :width]
            tail_layer = tail_layer + layers[:, width:]
            vectors = prep_ref[:width, q : q + 1] + jnp.zeros((width, neg), F32)
            coef_rows = coef_parts[q * per_query : (q + 1) * per_query]
        else:
            span = slice(last, last + LANES)
            layer_part = tail_layer
            vectors = prep_ref[:width, :]
            coef_rows = coef_parts[-1:]
        size = span.stop - span.start
        coef = jnp.broadcast_to(jnp.concatenate(coef_rows, axis=1), (width, size))
        right = jnp.concatenate([grad_hidden[:, span], jnp.maximum(hidden[:, span], 0.0)], axis=0)
        left = jnp.concatenate([picked[:, span], vectors, coef], axis=0)
        products = dot_nt(stack_left(left, 3), stack_right(right, 3, axis=1))
        entity_part = products[:width, :hid]
        query_part = products[width : 2 * width, :hid]
        score_part = products[2 * width :, hid:]
        rest = [layer_part, entity_part, query_part, score_part, spare]
        out_ref[block * width : (block + 1) * width, rel_lanes:] = jnp.concatenate(rest, axis=1)
    seeds.append(tail_seed)
    out_ref[:, :rel_lanes] = gathered + jnp.concatenate(seeds, axis=0)
    new_copy.wait()


def combine_kernel(sizes, totals_ref, grads_ref, sent_ref):
    q_local, width = sizes
    total = jnp.sum(totals_ref[...], axis=0)
    scale = totals_ref[lax.axis_index("nodes")] / total
    mixed = grads_ref[q_local * width :, :]
    for q in range(q_local):
        mixed = mixed + grads_ref[q * width : (q + 1) * width, :] * scale[:, q : q + 1]
    across = mixed.shape[1] // LANES
    tiles = width // SUBLANES * across
    for tile in range(tiles):
        top, left = tile // across * SUBLANES, tile % across * LANES
        sent_ref[tile] = mixed[top : top + SUBLANES, left : left + LANES]
    for tile in range(tiles, sent_ref.shape[0]):
        sent_ref[tile] = jnp.zeros((SUBLANES, LANES), F32)


def spread_kernel(parts_ref, out_ref):
    total = jnp.sum(parts_ref[...], axis=0)
    for n in range(out_ref.shape[0]):
        out_ref[n] = total


def unpack_kernel(
    sizes, tiles_ref, totals_ref, rel_ref, layer_ref, ment_ref, mquery_ref, score_ref, loss_ref
):
    relations, across = sizes
    width, hid = ment_ref.shape
    down = width // SUBLANES
    flat = jnp.concatenate(
        [
            jnp.concatenate([tiles_ref[row * across + tile] for tile in range(across)], axis=1)
            for row in range(down)
        ],
        axis=0,
    )
    rel_lanes = pad_to(relations, LANES)
    rel_ref[...] = flat[:, :relations]
    start = rel_lanes
    layer_ref[...] = flat[:, start : start + width]
    start += width
    ment_ref[...] = flat[:, start : start + hid]
    start += hid
    mquery_ref[...] = flat[:, start : start + hid]
    start += hid
    score_ref[...] = flat[0:1, start : start + hid]
    everyone = jnp.sum(totals_ref[...], axis=0)
    count = loss_ref.shape[1]
    ratio = everyone[:, count : 2 * count] / everyone[:, :count]
    loss_ref[...] = everyone[:, 2 * count : 3 * count] + ratio


def call(kernel, name, outs, flops, *operands, scratch=(), far_out=(), alias=None):
    spaces = [pl.ANY if spot in far_out else pltpu.VMEM for spot in range(len(outs))]
    found = pl.pallas_call(
        kernel,
        out_shape=tuple(
            dims if isinstance(dims, jax.ShapeDtypeStruct) else jax.ShapeDtypeStruct(dims, F32)
            for dims in outs
        ),
        in_specs=[pl.BlockSpec(memory_space=pltpu.VMEM) for _ in operands],
        out_specs=tuple(pl.BlockSpec(memory_space=space) for space in spaces),
        scratch_shapes=scratch,
        input_output_aliases=alias or {},
        compiler_params=pltpu.CompilerParams(vmem_limit_bytes=40 << 20),
        cost_estimate=pl.CostEstimate(flops=flops, bytes_accessed=min(flops, 1 << 20), transcendentals=0),
        name=name,
    )(*operands)
    return found[0] if len(outs) == 1 else found


def swap(values, axes):
    return lax.all_to_all(values, axes, split_axis=0, concat_axis=0, tiled=True)


def body(
    state_in,
    edge_src,
    edge_dst,
    edge_rel,
    edge_count,
    send_list,
    query_head,
    query_rel,
    pos_tail,
    neg_ids,
    rel_table,
    layer_weight,
    mlp_entity,
    mlp_query,
    score_weight,
):
    nodes = lax.axis_size("nodes")
    queries = lax.axis_size("queries")
    ent, width_all = state_in.shape
    relations, width = rel_table.shape
    hid = mlp_entity.shape[1]
    q_local = width_all // width
    edges = edge_src.shape[0]
    bound = send_list.shape[2]
    neg = neg_ids.shape[1]
    columns = q_local * neg + LANES
    chunk = min(512, edges)
    src_row = edge_src.reshape(1, edges)
    dst_row = edge_dst.reshape(1, edges)
    rel_row = edge_rel.reshape(1, edges)
    count = edge_count.reshape(1, 1)
    score_row = score_weight.reshape(1, hid)
    table_t = rel_table.T
    tick = call(tick_kernel, "tick", [(SUBLANES, LANES)], 10**10)
    hot = call(
        wanted_kernel,
        "wanted",
        [jax.ShapeDtypeStruct((nodes * bound, ent), BF16)],
        1,
        tick,
        send_list[0],
    )
    outgoing = call(send_kernel, "send", [(nodes, bound, width_all)], 10**9, hot, state_in)
    received = swap(outgoing, "nodes").reshape(nodes * bound, width_all)
    local, relation, prep, marks = call(
        functools.partial(early_kernel, (chunk,)),
        "early",
        [
            (width_all, edges),
            (width, edges),
            (width + 2 * hid, LANES),
            jax.ShapeDtypeStruct((SUBLANES, LANES), jnp.int32),
        ],
        4 * 10**9,
        state_in,
        src_row,
        rel_row,
        table_t,
        query_head.reshape(1, q_local),
        query_rel.reshape(1, q_local),
        pos_tail.reshape(1, q_local),
        layer_weight,
        mlp_entity,
        mlp_query,
        score_row,
    )
    needed = kept_layout(q_local, ent, neg)[-1].stop
    source_t, kept, gate, coef, totals = call(
        functools.partial(forward_kernel, (chunk,)),
        "forward",
        [
            (width_all, edges),
            (width, max(needed, edges)),
            jax.ShapeDtypeStruct((width_all, ent), BF16),
            (2 * pad_to(columns // LANES, SUBLANES), LANES),
            (nodes, 1, LANES),
        ],
        4 * 10**9,
        count,
        state_in,
        received,
        src_row,
        dst_row,
        neg_ids,
        local,
        relation,
        prep,
        marks,
        layer_weight,
        mlp_entity,
        alias={6: 0, 7: 1} if needed <= edges else {6: 0},
    )
    all_totals = swap(totals, "nodes")
    rel_lanes = pad_to(relations, LANES)
    lanes = rel_lanes + pad_to(width + 3 * hid, LANES)
    across = lanes // LANES
    grads, new_state = call(
        functools.partial(backward_kernel, (chunk, relations, q_local * queries)),
        "backward",
        [((q_local + 1) * width, lanes), (ent, width_all)],
        4 * 10**9,
        count,
        source_t,
        dst_row,
        rel_row,
        neg_ids,
        prep,
        marks,
        layer_weight,
        mlp_entity,
        mlp_query,
        kept,
        gate,
        coef,
        scratch=[pltpu.VMEM((ent, width_all), F32), pltpu.SemaphoreType.DMA((1,))],
        far_out=(1,),
    )
    tiles = width // SUBLANES * across
    wide = nodes * queries
    group = wide if wide <= pad_to(tiles, nodes) else nodes
    held = pad_to(tiles, group)
    sent = call(
        functools.partial(combine_kernel, (q_local, width)),
        "combine",
        [(held, SUBLANES, LANES)],
        10**6,
        all_totals,
        grads,
    )
    axes = ("queries", "nodes") if group == wide else "nodes"
    own = held // group
    parts = swap(sent, axes).reshape(group, own * SUBLANES, LANES)
    if group == wide:
        mine = call(spread_kernel, "spread", [(group, own * SUBLANES, LANES)], 10**6, parts)
    else:
        mine = lax.psum(jnp.sum(parts, axis=0), "queries")
        mine = jnp.broadcast_to(mine, (group,) + mine.shape)
    final = swap(mine, axes).reshape(held, SUBLANES, LANES)
    grad_rel, grad_layer, grad_entity, grad_query, grad_score, loss = call(
        functools.partial(unpack_kernel, (relations, across)),
        "unpack",
        [(width, relations), (width, width), (width, hid), (width, hid), (1, hid), (1, q_local)],
        10**6,
        final,
        all_totals,
    )
    return (
        new_state,
        loss.reshape(q_local),
        grad_rel.T,
        grad_layer,
        grad_entity,
        grad_query,
        grad_score.reshape(hid),
    )


def solution(mesh):
    in_specs = (
        P("nodes", "queries"),
        P("nodes"),
        P("nodes"),
        P("nodes"),
        P("nodes"),
        P("nodes", None, None),
        P("queries"),
        P("queries"),
        P("queries"),
        P("queries", "nodes"),
        P(),
        P(),
        P(),
        P(),
        P(),
    )
    out_specs = (P("nodes", "queries"), P("queries"), P(), P(), P(), P(), P())
    return jax.shard_map(body, mesh=mesh, in_specs=in_specs, out_specs=out_specs, check_vma=False)
```
